128 devices in a mesh: dp: 8 (over y_hi, z), lib: 16 (over y_lo, x, core).
Axes of the slice: x: 4, y: 4 (y_hi: 2, y_lo: 2; y = y_hi * 2 + y_lo), z: 4, core: 2. Of those that a mesh axis runs over, the one named last changes fastest.
Arguments:
- spectra: bfloat16 [49152, 512], P(('dp', 'lib')), may hold values from -6 to 6
- w_proj: bfloat16 [512, 512], replicated, may hold values from -0.25 to 0.25
- fixed_library_matrix: bfloat16 [16384, 512], P('lib')
- mol_rows: bfloat16 [262144, 512], P(('dp', 'lib'))
- cand_ids: int32 [49152, 4], P(('dp', 'lib')), may hold values from 0 to 262143, as said below
- iso_count: int32 [49152], P(('dp', 'lib')), may hold values from 1 to 3
Outputs:
- grad_w: float32 [512, 512], replicated
- grad_mol: float32 [262144, 512], P(('dp', 'lib'))
- loss: float32 [], replicated
The draws below stay inside these ranges and needn't reach their ends.
Inputs may be any that keep to these rules, and one draw needn't show every extreme that they name: cand_ids of a spectrum on device dp, lib (in dp+lib order) name rows of the dp group's molecules: id // 2048 // 16 equals dp. Over one device's 1536 slots (all columns, live or not), at most 192 name rows whose (id // 2048) % 16 is one lib index, and exactly 192 for some lib index on every device.
All inputs are finite; a program needn't handle non-finite values.
Results may differ from the reference program's by a relative error of at most 0.0074.
Values may be sent and summed in bfloat16 or wider, within the bound.
A program may use at most 64 MiB of HBM per device.

```python
import jax
import jax.numpy as jnp
from jax import lax

D = 512
Q_DEV = 384
MOL_DEV = 2048
ISO = 3
QUERIES = 49152
BANK = 16384
MOLS = 262144
SLOTS = 1536
CAP = 192
N_LIB = 16


def draw_fixed_library_matrix(key, part):
    key_base, key_scale = jax.random.split(key, 2)
    normal_part = jax.random.normal(key_base, (BANK, D), jnp.float32)
    row_scale = jnp.exp(jax.random.uniform(key_scale, (BANK, 1), jnp.float32, jnp.log(0.2), jnp.log(0.3)))
    return (normal_part * row_scale).astype(jnp.bfloat16)


def draw_mol_rows(key, part):
    own_key = jax.random.fold_in(key, 101)
    key_base, key_scale = jax.random.split(own_key, 2)
    base = jax.random.normal(key_base, (MOLS, D), jnp.float32)
    row_scale = jnp.exp(jax.random.uniform(key_scale, (MOLS, 1), jnp.float32, jnp.log(0.1), jnp.log(3.0)))
    return (base * row_scale).astype(jnp.bfloat16)


def draw_cand_ids(key, part):
    blocks = QUERIES // Q_DEV
    key_owner, key_slot, key_local = jax.random.split(key, 3)
    rest = SLOTS - CAP
    base = rest // (N_LIB - 1)
    spare = rest % (N_LIB - 1)
    rank = jnp.arange(N_LIB, dtype=jnp.int32)
    counts = jnp.where(rank == 0, CAP, base + (rank - 1 < spare).astype(jnp.int32))
    bounds = jnp.cumsum(counts)
    slots = jnp.arange(SLOTS, dtype=jnp.int32)
    rank_of_slot = jnp.sum((bounds[None, :] <= slots[:, None]).astype(jnp.int32), axis=1)
    owner_scores = jax.random.randint(key_owner, (blocks, N_LIB), 0, 1 << 20) * N_LIB + rank[None, :]
    owner_order = jnp.argsort(owner_scores, axis=1).astype(jnp.int32)
    slot_scores = jax.random.randint(key_slot, (blocks, SLOTS), 0, 1 << 16) * SLOTS + slots[None, :]
    shuffle = jnp.argsort(slot_scores, axis=1).astype(jnp.int32)
    shuffled_rank = rank_of_slot[shuffle]
    owner = jnp.take_along_axis(owner_order, shuffled_rank, axis=1)
    local = jax.random.randint(key_local, (blocks, SLOTS), 0, MOL_DEV)
    block_ids = jnp.arange(blocks, dtype=jnp.int32)[:, None]
    group = block_ids // N_LIB
    ids = (group * N_LIB + owner) * MOL_DEV + local
    return ids.reshape(QUERIES, 1 + ISO).astype(jnp.int32)


def with_ends(entries, key, smallest, largest):
    longest = entries.shape.index(max(entries.shape))
    spots = []
    for shift in (0, 1):
        where = [jax.random.randint(jax.random.fold_in(key, axis), (), 0, length) for axis, length in enumerate(entries.shape)]
        where[longest] = (where[longest] + shift) % entries.shape[longest]
        spots.append(tuple(where))
    return entries.at[spots[0]].set(smallest).at[spots[1]].set(largest)


def steps_of(rng, extent, shards, low, high):
    level, own = 1.0, jax.random.fold_in(rng, 6)
    for dim, shards_of in shards:
        draws = jnp.exp(jax.random.uniform(jax.random.fold_in(own, dim), (shards_of,), jnp.float32, low / len(shards), high / len(shards)))
        level = level * jnp.repeat(draws, extent[dim] // shards_of).reshape([-1 if axis == dim else 1 for axis in range(len(extent))])
    return level


def normal_values(key, extent, deviation, reach, pieces=(), held_as=jnp.bfloat16):
    result = jax.random.normal(key, extent, jnp.float32) * deviation
    if len(pieces) > 0:
        result = steps_of(key, extent, pieces, -0.22, 0.18) * result
    return jnp.clip(result, min=-reach, max=reach).astype(held_as)


def setup_inputs(seed: int = 0) -> dict:
    arg_keys = jax.random.split(jax.random.key(seed), 7)
    spectra = normal_values(arg_keys[0], (QUERIES, D), 1.0, 6.0, ((0, 128),))
    w_proj = normal_values(arg_keys[1], (D, D), D ** -0.5, 0.25)
    fixed_library_matrix = draw_fixed_library_matrix(jax.random.fold_in(arg_keys[6], 71), 0)
    mol_rows = draw_mol_rows(jax.random.fold_in(arg_keys[6], 71), 0)
    cand_ids = draw_cand_ids(jax.random.fold_in(arg_keys[6], 71), 0)
    iso_count = with_ends(jax.random.randint(arg_keys[5], (QUERIES,), 1, ISO + 1), jax.random.fold_in(arg_keys[5], 1), 1, ISO).astype(jnp.int32)
    return dict(spectra=spectra, w_proj=w_proj, fixed_library_matrix=fixed_library_matrix, mol_rows=mol_rows, cand_ids=cand_ids, iso_count=iso_count)


sharpness_divisor = 0.07

def reference(spectra, w_proj, fixed_library_matrix, mol_rows, cand_ids, iso_count):
    u_proj = jnp.dot(spectra, w_proj, preferred_element_type=jnp.float32)
    norm_all = jnp.sqrt(lax.optimization_barrier(jnp.sum(u_proj * u_proj, axis=1, keepdims=True)) + 1e-06)
    unit_all = u_proj / norm_all
    query_all = unit_all.astype(jnp.bfloat16)
    column = jnp.arange(1 + ISO, dtype=jnp.int32)[None, :]
    live_all = column <= iso_count[:, None]
    first = (column == 0).astype(jnp.float32)

    def one_block(index):
        start = (index * Q_DEV).astype(jnp.int32)
        spectrum_encoding = lax.dynamic_slice_in_dim(query_all, start, Q_DEV, 0)
        normalized_spectrum_matrix = lax.dynamic_slice_in_dim(unit_all, start, Q_DEV, 0)
        norm = lax.dynamic_slice_in_dim(norm_all, start, Q_DEV, 0)
        live = lax.dynamic_slice_in_dim(live_all, start, Q_DEV, 0)
        ids = lax.dynamic_slice_in_dim(cand_ids, start, Q_DEV, 0)
        contender_embedding_matrix = mol_rows[ids].astype(jnp.float32)
        contender_similarity_values = jnp.einsum('ti,tmi->tm', spectrum_encoding.astype(jnp.float32), contender_embedding_matrix) / sharpness_divisor
        library_similarity_values = jnp.dot(spectrum_encoding, fixed_library_matrix.T, preferred_element_type=jnp.float32) / sharpness_divisor
        top = jnp.maximum(lax.optimization_barrier(jnp.max(jnp.where(live, contender_similarity_values, -1e+30), axis=1)), lax.optimization_barrier(jnp.max(library_similarity_values, axis=1)))
        weight_cand = jnp.where(live, jnp.exp(contender_similarity_values - top[:, None]), 0.0)
        weight_bank = jnp.exp(library_similarity_values - top[:, None])
        objective_aggregate = lax.optimization_barrier(jnp.sum(weight_cand, axis=1)) + lax.optimization_barrier(jnp.sum(weight_bank, axis=1))
        derivative_tally = jnp.dot(weight_bank.astype(jnp.bfloat16), fixed_library_matrix, preferred_element_type=jnp.float32)
        derivative_tally = derivative_tally + jnp.einsum('qk,qkd->qd', weight_cand, contender_embedding_matrix)
        lse = top + jnp.log(objective_aggregate)
        losses = lse - contender_similarity_values[:, 0]
        spectrum_derivative = (derivative_tally / objective_aggregate[:, None] - contender_embedding_matrix[:, 0, :]) / sharpness_divisor
        grad_u = (spectrum_derivative - normalized_spectrum_matrix * lax.optimization_barrier(jnp.sum(normalized_spectrum_matrix * spectrum_derivative, axis=1, keepdims=True))) / norm
        inverse_sharpness = jnp.where(live, weight_cand / objective_aggregate[:, None] - first, 0.0)
        contender_derivative = (inverse_sharpness[:, :, None] * normalized_spectrum_matrix[:, None, :] / sharpness_divisor).astype(jnp.bfloat16)
        return (losses, grad_u.astype(jnp.bfloat16), contender_derivative)
    blocks = jnp.arange(QUERIES // Q_DEV, dtype=jnp.int32)
    losses, grad_u, contender_derivative = lax.map(one_block, blocks)
    grad_u = grad_u.reshape(QUERIES, D)
    grad_w = jnp.dot(spectra.T, grad_u, preferred_element_type=jnp.float32)
    grad_mol = jnp.zeros((MOLS, D), jnp.float32).at[cand_ids.reshape(-1)].add(contender_derivative.reshape(-1, D).astype(jnp.float32))
    loss = jnp.sum(losses) / QUERIES
    return (grad_w, grad_mol, loss)
```

```python
import functools

import jax
import jax.numpy as jnp
from jax import lax
from jax.experimental import pallas as pl
from jax.experimental.pallas import tpu as pltpu
from jax.sharding import PartitionSpec as P

F32 = jnp.float32
BF16 = jnp.bfloat16
I32 = jnp.int32
MESH = pl.DeviceIdType.MESH

D = 512
Q = 384
COLS = 4
NLIB = 16
NCHIP = 8
CAP = 192
BANK = 1024
MOL = 2048
CODE_ROWS = 16
SUB = 256
ROW_BITS = 11
SLOT_MASK = 2047
OWNER_SHIFT = 22
INV_T = 1.0 / 0.07


def iota(shape, dim):
    return lax.broadcasted_iota(I32, shape, dim)


def to_row(v):
    n = v.shape[0]
    parts = []
    for lo in range(0, n, 128):
        m = min(128, n - lo)
        eye = iota((m, m), 0) == iota((m, m), 1)
        parts.append(jnp.sum(jnp.where(eye, v[lo : lo + m], 0.0), axis=0, keepdims=True))
    return parts[0] if len(parts) == 1 else jnp.concatenate(parts, axis=1)


def to_col(parts):
    eye = iota((128, 128), 0) == iota((128, 128), 1)
    return jnp.concatenate(
        [jnp.sum(jnp.where(eye, r, 0.0), axis=1, keepdims=True) for r in parts], axis=0
    )


def onehot(mask):
    return jnp.where(mask, 1.0, 0.0).astype(BF16)


def dot(a, b):
    return jnp.dot(a, b, preferred_element_type=F32)


def dot_nt(a, b):
    return lax.dot_general(a, b, (((1,), (1,)), ((), ())), preferred_element_type=F32)


def dot_tn(a, b):
    return lax.dot_general(a, b, (((0,), (0,)), ((), ())), preferred_element_type=F32)


def kernel(
    ndp,
    spec_hbm,
    w_hbm,
    bank_hbm,
    mol_hbm,
    code_ref,
    gw_out,
    gm_out,
    loss_out,
    gat,
    wv,
    bankv,
    molv,
    codes,
    posr,
    valr,
    pkt,
    mrow,
    qs,
    unit,
    acc,
    qcol,
    scol,
    stats,
    lse,
    gwacc,
    gwb,
    rsb,
    dpb,
    dlb,
    ggb,
    loc_sem,
    ids_send,
    ids_recv,
    ag_send,
    ag_recv,
    sb_send,
    sb_recv,
    st_send,
    st_recv,
    rs_send,
    rs_recv,
    dp_send,
    dp_recv,
    dl_send,
    dl_recv,
    gg_send,
    gg_recv,
    out_sem,
):
    dp = lax.axis_index("dp")
    me = lax.axis_index("lib")
    core = lax.rem(me, 2)
    chip = me // 2
    y = chip // 4
    x = lax.rem(chip, 4)

    def chip_at(dy, dx):
        return lax.rem(y + dy, 2) * 4 + lax.rem(x + dx, 4)

    def peer(j):
        return lax.rem(me + j, NLIB)

    def dpeer(j):
        return lax.rem(dp + j, ndp)

    own_rows = pl.ds(pl.multiple_of(core * Q, Q), Q)
    loads = [
        pltpu.make_async_copy(spec_hbm, gat.at[chip, own_rows, :], loc_sem.at[0]),
        pltpu.make_async_copy(w_hbm, wv, loc_sem.at[1]),
        pltpu.make_async_copy(bank_hbm, bankv, loc_sem.at[2]),
        pltpu.make_async_copy(mol_hbm, molv, loc_sem.at[3]),
    ]
    for load in loads:
        load.start()

    barrier = pltpu.get_barrier_semaphore()

    def greet(j, carry):
        pl.semaphore_signal(barrier, inc=1, device_id={"lib": peer(j)}, device_id_type=MESH)
        return carry

    lax.fori_loop(1, NLIB, greet, 0)

    def greet_dp(j, carry):
        pl.semaphore_signal(barrier, inc=1, device_id={"dp": dpeer(j)}, device_id_type=MESH)
        return carry

    lax.fori_loop(1, ndp, greet_dp, 0)
    codes[me] = code_ref[...]
    pl.semaphore_wait(barrier, NLIB - 1 + ndp - 1)

    def ids_copy(j):
        return pltpu.make_async_remote_copy(
            src_ref=codes.at[me],
            dst_ref=codes.at[me],
            send_sem=ids_send.at[j],
            recv_sem=ids_recv.at[me],
            device_id={"lib": peer(j)},
            device_id_type=MESH,
        )

    def ids_from(j):
        s = peer(j)
        return pltpu.make_async_remote_copy(
            src_ref=codes.at[s],
            dst_ref=codes.at[s],
            send_sem=ids_send.at[j],
            recv_sem=ids_recv.at[s],
            device_id={"lib": s},
            device_id_type=MESH,
        )

    lax.fori_loop(1, NLIB, lambda j, c: (ids_copy(j).start(), c)[1], 0)

    def piece(ch, cr, lo, n):
        return gat.at[ch, pl.ds(pl.multiple_of(cr * Q + lo, 64), n), :]

    HALF = Q // 2
    right = {"lib": chip_at(0, 1) * 2 + core}
    left = {"lib": chip_at(0, 3) * 2 + core}
    across = {"lib": chip_at(1, 0) * 2 + core}
    sibling = {"lib": chip * 2 + 1 - core}

    def ag(idx, dy, dx, lo, n, to):
        ref = piece(chip_at(dy, dx), core, lo, n)
        return pltpu.make_async_remote_copy(
            src_ref=ref, dst_ref=ref, send_sem=ag_send.at[idx], recv_sem=ag_recv.at[idx],
            device_id=to, device_id_type=MESH,
        )

    ag_out = [
        ag(0, 0, 0, 0, Q, right),
        ag(1, 0, 0, 0, Q, left),
        ag(2, 0, 0, 0, Q, across),
        ag(3, 0, 3, 0, HALF, right),
        ag(4, 0, 1, HALF, HALF, left),
        ag(5, 1, 0, 0, Q, right),
        ag(6, 1, 0, 0, Q, left),
        ag(7, 0, 2, 0, HALF, across),
        ag(8, 0, 2, HALF, HALF, across),
    ]
    arriving = [
        (0, 3, 0, Q),
        (0, 1, 0, Q),
        (1, 0, 0, Q),
        (0, 2, 0, HALF),
        (0, 2, HALF, HALF),
        (1, 3, 0, Q),
        (1, 1, 0, Q),
        (1, 2, 0, HALF),
        (1, 2, HALF, HALF),
    ]
    ag_in = [ag(k, dy, dx, lo, n, right) for k, (dy, dx, lo, n) in enumerate(arriving)]

    def sb(idx, dy, dx, lo, n, cr):
        ref = piece(chip_at(dy, dx), cr, lo, n)
        return pltpu.make_async_remote_copy(
            src_ref=ref, dst_ref=ref, send_sem=sb_send.at[idx], recv_sem=sb_recv.at[idx],
            device_id=sibling, device_id_type=MESH,
        )

    sb_list = arriving + [(0, 0, 0, Q)]
    sb_out = [sb(k, dy, dx, lo, n, core) for k, (dy, dx, lo, n) in enumerate(sb_list)]
    sb_in = [sb(k, dy, dx, lo, n, 1 - core) for k, (dy, dx, lo, n) in enumerate(sb_list)]

    loads[0].wait()
    for k in (0, 1, 2):
        ag_out[k].start()
    sb_out[9].start()
    for load in loads[1:]:
        load.wait()
    sb_in[9].wait_recv()

    def compaction():
        lax.fori_loop(1, NLIB, lambda j, c: (ids_from(j).wait_recv(), c)[1], 0)
        n = NLIB * CODE_ROWS
        code = codes[...].reshape(n, 128)
        mine = (code >> OWNER_SHIFT) == me
        ones = onehot(mine)
        before = onehot(iota((128, 128), 0) < iota((128, 128), 1))
        inside = dot(ones, before)
        totals = dot(ones, jnp.ones((128, 128), BF16)).astype(BF16)
        ri, ci = iota((n, n), 0), iota((n, n), 1)
        ahead = onehot((ri // CODE_ROWS == ci // CODE_ROWS) & (ci < ri))
        pos = inside + dot(ahead, totals)
        low = (code & (2**OWNER_SHIFT - 1)) + 1
        posr[...] = jnp.where(mine, pos, -1.0).reshape(NLIB, CODE_ROWS, 128)
        valr[...] = jnp.where(mine, low.astype(F32), 0.0).reshape(NLIB, CODE_ROWS, 128)

        def one(i, carry):
            place = iota((CAP, 128), 0).astype(F32)
            both = []
            for c in (0, 1):
                s = 2 * i + c
                p_all, v_all = posr[s], valr[s]
                total = jnp.zeros((CAP, 128), F32)
                for j in range(Q * COLS // 128):
                    total += jnp.where(p_all[j : j + 1] == place, v_all[j : j + 1], 0.0)
                packed = jnp.sum(total, axis=1, keepdims=True)
                both.append(packed)
                pkt[i, 1 + c : 2 + c, 0:CAP] = to_row(packed)
            packed = jnp.concatenate(both, axis=0)
            scol[i, :, 0:1] = packed
            pkt[i, 0:1, :] = to_row(packed)
            row = (packed.astype(I32) - 1) >> ROW_BITS
            pick = onehot(row == iota((2 * CAP, MOL), 1))
            mrow[i] = dot(pick, molv[...]).astype(BF16)
            return carry

        lax.fori_loop(0, NCHIP, one, 0)

    def bank_unit(ch):
        def project(b):
            sp = gat[ch, b * SUB : (b + 1) * SUB, :]
            u = dot(sp, wv[...])
            rn = lax.rsqrt(jnp.sum(u * u, axis=1, keepdims=True) + 1e-6)
            u = u * rn
            unit[ch, b * SUB : (b + 1) * SUB, :] = u
            qcol[ch, b * SUB : (b + 1) * SUB, 0:1] = rn
            return dot_nt(u.astype(BF16), bankv[...])

        def weigh(b, s):
            m = jnp.max(s, axis=1, keepdims=True)
            e = jnp.exp((s - m) * INV_T)
            qcol[ch, b * SUB : (b + 1) * SUB, 1:2] = m * INV_T
            qcol[ch, b * SUB : (b + 1) * SUB, 2:3] = jnp.sum(e, axis=1, keepdims=True)
            acc[ch, b * SUB : (b + 1) * SUB, :] = dot(e.astype(BF16), bankv[...])

        nsub = 2 * Q // SUB
        s_prev = project(0)
        for b in range(1, nsub):
            s_next = project(b)
            weigh(b - 1, s_prev)
            s_prev = s_next
        weigh(nsub - 1, s_prev)

    def step(t, carry):
        @pl.when(t == 1)
        def _():
            compaction()
            for k in (0, 1, 2):
                ag_in[k].wait_recv()
            for k in (3, 4, 5, 6):
                ag_out[k].start()
            for k in (0, 1, 2):
                sb_out[k].start()
            for k in (1, 0, 2):
                sb_in[k].wait_recv()

        @pl.when(t == 3)
        def _():
            for k in (3, 4):
                ag_in[k].wait_recv()
            for k in (7, 8):
                ag_out[k].start()
            for k in (3, 4):
                sb_out[k].start()

        @pl.when(t == 4)
        def _():
            for k in (3, 4):
                sb_in[k].wait_recv()
            for k in (5, 6):
                ag_in[k].wait_recv()
            for k in (5, 6):
                sb_out[k].start()

        @pl.when(t == 5)
        def _():
            for k in (5, 6):
                sb_in[k].wait_recv()

        @pl.when(t == 6)
        def _():
            for k in (7, 8):
                ag_in[k].wait_recv()
            for k in (7, 8):
                sb_out[k].start()

        @pl.when(t == 7)
        def _():
            for k in (7, 8):
                sb_in[k].wait_recv()

        dy = jnp.where((t == 3) | (t >= 5), 1, 0)
        dx = jnp.where(
            (t == 1) | (t == 5), 1, jnp.where((t == 2) | (t == 6), 3, jnp.where((t == 4) | (t == 7), 2, 0))
        )
        bank_unit(chip_at(dy, dx))
        return carry

    lax.fori_loop(0, NCHIP, step, 0)

    def st_copy(i, j):
        return pltpu.make_async_remote_copy(
            src_ref=stats.at[me, i], dst_ref=stats.at[me, i],
            send_sem=st_send.at[j], recv_sem=st_recv.at[me],
            device_id={"lib": peer(j)}, device_id_type=MESH,
        )

    def st_all(j, s):
        return pltpu.make_async_remote_copy(
            src_ref=stats.at[s], dst_ref=stats.at[s],
            send_sem=st_send.at[j], recv_sem=st_recv.at[s],
            device_id={"lib": peer(j)}, device_id_type=MESH,
        )

    def slots(i, c):
        t = scol[i, c * CAP : (c + 1) * CAP, 0:1].astype(I32) - 1
        q = (t & SLOT_MASK) >> 2
        column = t & 3
        return q, column

    def slot_q_row(i, c):
        t = pkt[i, 1 + c : 2 + c, 0:CAP].astype(I32) - 1
        return (t & SLOT_MASK) >> 2

    def cand_unit(i, carry):
        part = jnp.zeros((1, 1), F32)
        for c in (0, 1):
            rows = pl.ds(c * CAP, CAP)
            qrows = pl.ds(c * Q, Q)
            q, column = slots(i, c)
            query = unit[i, qrows, :].astype(BF16)
            q_slot = dot(onehot(q == iota((CAP, Q), 1)), query)
            qs[i, rows, :] = q_slot.astype(BF16)
            cs = jnp.sum(q_slot * mrow[i, rows, :].astype(F32), axis=1, keepdims=True) * INV_T
            scol[i, rows, 1:2] = cs
            part += jnp.sum(jnp.where(column == 0, cs, 0.0), axis=0, keepdims=True)
            cs_row = to_row(cs)
            chosen = jnp.where(slot_q_row(i, c) == iota((Q, CAP), 0), cs_row, -1e30)
            mb = qcol[i, qrows, 1:2]
            lb = qcol[i, qrows, 2:3]
            top = jnp.maximum(mb, jnp.max(chosen, axis=1, keepdims=True))
            total = lb * jnp.exp(mb - top) + jnp.sum(jnp.exp(chosen - top), axis=1, keepdims=True)
            out = to_row(top + jnp.log(total))
            for k in range(3):
                stats[me, i, 3 * c + k : 3 * c + k + 1, :] = out[:, 128 * k : 128 * (k + 1)]
        stats[me, i, 6:8, :] = jnp.broadcast_to(part, (2, 128))
        lax.fori_loop(1, NLIB, lambda j, k: (st_copy(i, j).start(), k)[1], 0)
        return carry

    lax.fori_loop(0, NCHIP, cand_unit, 0)

    lax.fori_loop(1, NLIB, lambda j, k: (st_all(j, peer(j)).wait_recv(), k)[1], 0)
    lax.fori_loop(1, NLIB, lambda j, k: (st_all(j, me).wait_send(), k)[1], 0)

    top = stats[0]
    for s in range(1, NLIB):
        top = jnp.maximum(top, stats[s])
    total = jnp.zeros((NCHIP, 8, 128), F32)
    first_scores = jnp.zeros((NCHIP, 8, 128), F32)
    for s in range(NLIB):
        total += jnp.exp(stats[s] - top)
        first_scores += stats[s]
    value = top + jnp.log(total)
    lse[...] = value
    in_row = iota((NCHIP, 8, 128), 1)
    lane0 = iota((NCHIP, 8, 128), 2) == 0
    terms = jnp.where(in_row < 6, value, jnp.where((in_row == 6) & lane0, -first_scores, 0.0))
    terms = jnp.sum(terms, axis=0)
    group_loss = jnp.sum(jnp.sum(terms, axis=1, keepdims=True), axis=0, keepdims=True)
    dlb[dp] = jnp.broadcast_to(group_loss, (8, 128))

    def dl_copy(j, s, to):
        return pltpu.make_async_remote_copy(
            src_ref=dlb.at[s], dst_ref=dlb.at[s], send_sem=dl_send.at[j], recv_sem=dl_recv.at[s],
            device_id={"dp": to}, device_id_type=MESH,
        )

    lax.fori_loop(1, ndp, lambda j, k: (dl_copy(j, dp, dpeer(j)).start(), k)[1], 0)

    gwacc[...] = jnp.zeros((D, D), F32)

    def grad_unit(i, carry):
        du_parts = []
        for c in (0, 1):
            rows = pl.ds(c * CAP, CAP)
            qrows = pl.ds(c * Q, Q)
            q, column = slots(i, c)
            lse_rows = [lse[i, 3 * c + k : 3 * c + k + 1, :] for k in range(3)]
            lse_slot = jnp.sum(
                jnp.where(q == iota((CAP, Q), 1), jnp.concatenate(lse_rows, axis=1), 0.0),
                axis=1,
                keepdims=True,
            )
            cs = scol[i, rows, 1:2]
            coef = jnp.where(q < Q, jnp.exp(cs - lse_slot) - jnp.where(column == 0, 1.0, 0.0), 0.0)
            qs[i, rows, :] = (qs[i, rows, :].astype(F32) * (coef * INV_T)).astype(BF16)
            spread = jnp.where(slot_q_row(i, c) == iota((Q, CAP), 0), to_row(coef), 0.0)
            scale = jnp.exp(qcol[i, qrows, 1:2] - to_col(lse_rows))
            dq = acc[i, qrows, :] * scale + dot(spread.astype(BF16), mrow[i, rows, :])
            u = unit[i, qrows, :]
            along = jnp.sum(u * dq, axis=1, keepdims=True)
            du = (dq - u * along) * (qcol[i, qrows, 0:1] * INV_T)
            du_parts.append(du.astype(BF16))
        du_all = jnp.concatenate(du_parts, axis=0)
        gwacc[...] += dot_tn(gat[i], du_all)
        return carry

    lax.fori_loop(0, NCHIP, grad_unit, 0)

    gwb[...] = gwacc[...].astype(BF16).reshape(NLIB, D // NLIB, D)

    def rs_copy(j, src, dst, to):
        return pltpu.make_async_remote_copy(
            src_ref=gwb.at[src], dst_ref=rsb.at[dst], send_sem=rs_send.at[j], recv_sem=rs_recv.at[dst],
            device_id={"lib": to}, device_id_type=MESH,
        )

    lax.fori_loop(1, NLIB, lambda j, k: (rs_copy(j, peer(j), me, peer(j)).start(), k)[1], 0)

    nslots = NLIB * CAP

    def out_copy(r):
        return pltpu.make_async_copy(
            acc.at[r, pl.ds(0, 256), :], gm_out.at[pl.ds(pl.multiple_of(r * 256, 256), 256), :], out_sem.at[r]
        )

    def scatter(r, carry):
        slot_row = (
            jnp.concatenate([pkt[i, 0:1, :] for i in range(NCHIP)], axis=1).astype(I32) - 1
        ) >> ROW_BITS
        pick = onehot(slot_row == iota((256, nslots), 0) + r * 256)
        acc[r, 0:256, :] = dot(pick, qs[...].reshape(nslots, D))
        out_copy(r).start()
        return carry

    lax.fori_loop(0, 3, scatter, 0)

    lax.fori_loop(1, NLIB, lambda j, k: (rs_copy(j, me, peer(j), peer(j)).wait_recv(), k)[1], 0)
    rsb[me] = gwb[me]
    part = jnp.zeros((D // NLIB, D), F32)
    for s in range(NLIB):
        part += rsb[s].astype(F32)
    dpb[dp] = part.astype(BF16)

    def dp_copy(j, s, to):
        return pltpu.make_async_remote_copy(
            src_ref=dpb.at[s], dst_ref=dpb.at[s], send_sem=dp_send.at[j], recv_sem=dp_recv.at[s],
            device_id={"dp": to}, device_id_type=MESH,
        )

    lax.fori_loop(1, ndp, lambda j, k: (dp_copy(j, dp, dpeer(j)).start(), k)[1], 0)

    lax.fori_loop(3, 6, scatter, 0)

    lax.fori_loop(1, ndp, lambda j, k: (dp_copy(j, dpeer(j), dpeer(j)).wait_recv(), k)[1], 0)
    part = jnp.zeros((D // NLIB, D), F32)
    for s in range(ndp):
        part += dpb[s].astype(F32)
    ggb[me] = part.astype(BF16)

    def gg_copy(j, s, to):
        return pltpu.make_async_remote_copy(
            src_ref=ggb.at[s], dst_ref=ggb.at[s], send_sem=gg_send.at[j], recv_sem=gg_recv.at[s],
            device_id={"lib": to}, device_id_type=MESH,
        )

    lax.fori_loop(1, NLIB, lambda j, k: (gg_copy(j, me, peer(j)).start(), k)[1], 0)

    lax.fori_loop(6, 8, scatter, 0)

    lax.fori_loop(1, ndp, lambda j, k: (dl_copy(j, dpeer(j), dpeer(j)).wait_recv(), k)[1], 0)
    whole = jnp.zeros((8, 128), F32)
    for s in range(ndp):
        whole += dlb[s]
    loss_out[...] = whole * (1.0 / (Q * NLIB * ndp))

    lax.fori_loop(1, NLIB, lambda j, k: (gg_copy(j, peer(j), peer(j)).wait_recv(), k)[1], 0)
    gw_out[...] = ggb[...].astype(F32).reshape(D, D)

    lax.fori_loop(0, 8, lambda r, k: (out_copy(r).wait(), k)[1], 0)
    lax.fori_loop(1, NLIB, lambda j, k: (ids_copy(j).wait_send(), k)[1], 0)
    for k in range(9):
        ag_out[k].wait_send()
    for k in range(10):
        sb_out[k].wait_send()
    lax.fori_loop(1, NLIB, lambda j, k: (rs_copy(j, peer(j), me, peer(j)).wait_send(), k)[1], 0)
    lax.fori_loop(1, NLIB, lambda j, k: (gg_copy(j, me, peer(j)).wait_send(), k)[1], 0)
    lax.fori_loop(1, ndp, lambda j, k: (dp_copy(j, dp, dpeer(j)).wait_send(), k)[1], 0)
    lax.fori_loop(1, ndp, lambda j, k: (dl_copy(j, dp, dpeer(j)).wait_send(), k)[1], 0)


def per_device(ndp, spectra, w_proj, fixed_library_matrix, mol_rows, cand_ids, iso_count):
    owner = cand_ids // MOL % NLIB
    row = cand_ids % MOL
    slot = lax.broadcasted_iota(I32, (Q, COLS), 0) * COLS + lax.broadcasted_iota(I32, (Q, COLS), 1)
    live = lax.broadcasted_iota(I32, (Q, COLS), 1) <= iso_count[:, None]
    code = jnp.where(live, (owner << OWNER_SHIFT) | (row << ROW_BITS) | slot, -1)
    code = jnp.pad(code.reshape(Q * COLS // 128, 128), ((0, CODE_ROWS - Q * COLS // 128), (0, 0)), constant_values=-1)
    vmem = pl.BlockSpec(memory_space=pltpu.VMEM)
    hbm = pl.BlockSpec(memory_space=pl.ANY)
    dma = pltpu.SemaphoreType.DMA
    gw, gm, loss = pl.pallas_call(
        functools.partial(kernel, ndp),
        out_shape=(
            jax.ShapeDtypeStruct((D, D), F32),
            jax.ShapeDtypeStruct((MOL, D), F32),
            jax.ShapeDtypeStruct((8, 128), F32),
        ),
        in_specs=[hbm, hbm, hbm, hbm, vmem],
        out_specs=(vmem, hbm, vmem),
        scratch_shapes=[
            pltpu.VMEM((NCHIP, 2 * Q, D), BF16),
            pltpu.VMEM((D, D), BF16),
            pltpu.VMEM((BANK, D), BF16),
            pltpu.VMEM((MOL, D), BF16),
            pltpu.VMEM((NLIB, CODE_ROWS, 128), I32),
            pltpu.VMEM((NLIB, CODE_ROWS, 128), F32),
            pltpu.VMEM((NLIB, CODE_ROWS, 128), F32),
            pltpu.VMEM((NCHIP, 8, 2 * CAP), F32),
            pltpu.VMEM((NCHIP, 2 * CAP, D), BF16),
            pltpu.VMEM((NCHIP, 2 * CAP, D), BF16),
            pltpu.VMEM((NCHIP, 2 * Q, D), F32),
            pltpu.VMEM((NCHIP, 2 * Q, D), F32),
            pltpu.VMEM((NCHIP, 2 * Q, 128), F32),
            pltpu.VMEM((NCHIP, 2 * CAP, 128), F32),
            pltpu.VMEM((NLIB, NCHIP, 8, 128), F32),
            pltpu.VMEM((NCHIP, 8, 128), F32),
            pltpu.VMEM((D, D), F32),
            pltpu.VMEM((NLIB, D // NLIB, D), BF16),
            pltpu.VMEM((NLIB, D // NLIB, D), BF16),
            pltpu.VMEM((ndp, D // NLIB, D), BF16),
            pltpu.VMEM((ndp, 8, 128), F32),
            pltpu.VMEM((NLIB, D // NLIB, D), BF16),
            dma((4,)),
            dma((NLIB,)),
            dma((NLIB,)),
            dma((9,)),
            dma((9,)),
            dma((10,)),
            dma((10,)),
            dma((NLIB,)),
            dma((NLIB,)),
            dma((NLIB,)),
            dma((NLIB,)),
            dma((ndp,)),
            dma((ndp,)),
            dma((ndp,)),
            dma((ndp,)),
            dma((NLIB,)),
            dma((NLIB,)),
            dma((8,)),
        ],
        compiler_params=pltpu.CompilerParams(
            collective_id=0, has_side_effects=True, vmem_limit_bytes=62 * 1024 * 1024
        ),
    )(spectra, w_proj, fixed_library_matrix, mol_rows, code)
    return gw, gm, loss[0, 0]


def solution(mesh):
    placed = (
        P(("dp", "lib"), None),
        P(),
        P("lib", None),
        P(("dp", "lib"), None),
        P(("dp", "lib"), None),
        P(("dp", "lib")),
    )
    return jax.shard_map(
        functools.partial(per_device, mesh.shape["dp"]),
        mesh=mesh,
        in_specs=placed,
        out_specs=(P(), P(("dp", "lib"), None), P()),
        check_vma=False,
    )
```

```python
import functools

import jax
import jax.numpy as jnp
from jax import lax
from jax.experimental import pallas as pl
from jax.experimental.pallas import tpu as pltpu
from jax.sharding import PartitionSpec as P

F32 = jnp.float32
BF16 = jnp.bfloat16
I32 = jnp.int32
MESH = pl.DeviceIdType.MESH

D = 512
Q = 384
COLS = 4
NLIB = 16
NCHIP = 8
CAP = 192
BANK = 1024
MOL = 2048
CODE_ROWS = 16
ROW_BITS = 11
SLOT_MASK = 2047
OWNER_SHIFT = 22
INV_T = 1.0 / 0.07
LOG2E = 1.4426950408889634
NSLOTS = NLIB * CAP
PAIR = 2 * CAP


def iota(shape, dim):
    return lax.broadcasted_iota(I32, shape, dim)


def to_row(v):
    eye = iota((128, 128), 0) == iota((128, 128), 1)
    return jnp.concatenate(
        [
            jnp.sum(jnp.where(eye, v[lo : lo + 128], 0.0), axis=0, keepdims=True)
            for lo in range(0, v.shape[0], 128)
        ],
        axis=1,
    )


def to_col(v):
    eye = iota((128, 128), 0) == iota((128, 128), 1)
    return jnp.concatenate(
        [
            jnp.sum(jnp.where(eye, v[:, lo : lo + 128], 0.0), axis=1, keepdims=True)
            for lo in range(0, v.shape[1], 128)
        ],
        axis=0,
    )


def onehot(mask):
    return jnp.where(mask, 1.0, 0.0).astype(BF16)


def dot(a, b):
    return jnp.dot(a, b, preferred_element_type=F32)


def dot_nt(a, b):
    return lax.dot_general(a, b, (((1,), (1,)), ((), ())), preferred_element_type=F32)


def kernel(
    ndp,
    spec_hbm,
    w_hbm,
    bank_hbm,
    mol_hbm,
    code_ref,
    gw_out,
    gm_out,
    loss_out,
    spv,
    gat,
    wv,
    wt,
    bankv,
    bankt,
    molv,
    molt,
    codes,
    posr,
    valr,
    pkt,
    mrow,
    qs,
    unit,
    acc,
    qrow,
    scol,
    stats,
    lse,
    gwacc,
    gwb,
    rsb,
    dpb,
    dlb,
    ggb,
    loc_sem,
    ids_send,
    ids_recv,
    ag_send,
    ag_recv,
    sb_send,
    sb_recv,
    st_send,
    st_recv,
    rs_send,
    rs_recv,
    dp_send,
    dp_recv,
    dl_send,
    dl_recv,
    gg_send,
    gg_recv,
    out_sem,
):
    dp = lax.axis_index("dp")
    me = lax.axis_index("lib")
    core = lax.rem(me, 2)
    chip = me // 2
    y = chip // 4
    x = lax.rem(chip, 4)

    def chip_at(dy, dx):
        return lax.rem(y + dy, 2) * 4 + lax.rem(x + dx, 4)

    def peer(j):
        return lax.rem(me + j, NLIB)

    def dpeer(j):
        return lax.rem(dp + j, ndp)

    loads = [
        pltpu.make_async_copy(spec_hbm, spv, loc_sem.at[0]),
        pltpu.make_async_copy(w_hbm, wv, loc_sem.at[1]),
        pltpu.make_async_copy(bank_hbm, bankv, loc_sem.at[2]),
        pltpu.make_async_copy(mol_hbm, molv, loc_sem.at[3]),
    ]
    for load in loads:
        load.start()

    barrier = pltpu.get_barrier_semaphore()

    def greet(j, carry):
        pl.semaphore_signal(barrier, inc=1, device_id={"lib": peer(j)}, device_id_type=MESH)
        return carry

    lax.fori_loop(1, NLIB, greet, 0)

    def greet_dp(j, carry):
        pl.semaphore_signal(barrier, inc=1, device_id={"dp": dpeer(j)}, device_id_type=MESH)
        return carry

    lax.fori_loop(1, ndp, greet_dp, 0)
    codes[me] = code_ref[...]
    loads[0].wait()
    gat[chip, :, pl.ds(pl.multiple_of(core * Q, 128), Q)] = spv[...].T
    pl.semaphore_wait(barrier, NLIB - 1 + ndp - 1)

    def ids_copy(j):
        return pltpu.make_async_remote_copy(
            src_ref=codes.at[me],
            dst_ref=codes.at[me],
            send_sem=ids_send.at[j],
            recv_sem=ids_recv.at[me],
            device_id={"lib": peer(j)},
            device_id_type=MESH,
        )

    def ids_from(j):
        s = peer(j)
        return pltpu.make_async_remote_copy(
            src_ref=codes.at[s],
            dst_ref=codes.at[s],
            send_sem=ids_send.at[j],
            recv_sem=ids_recv.at[s],
            device_id={"lib": s},
            device_id_type=MESH,
        )

    lax.fori_loop(1, NLIB, lambda j, c: (ids_copy(j).start(), c)[1], 0)

    def piece(ch, cr, lo, n):
        return gat.at[ch, pl.ds(lo, n), pl.ds(pl.multiple_of(cr * Q, 128), Q)]

    HALF = D // 2
    right = {"lib": chip_at(0, 1) * 2 + core}
    left = {"lib": chip_at(0, 3) * 2 + core}
    across = {"lib": chip_at(1, 0) * 2 + core}
    sibling = {"lib": chip * 2 + 1 - core}

    def ag(idx, dy, dx, lo, n, to):
        ref = piece(chip_at(dy, dx), core, lo, n)
        return pltpu.make_async_remote_copy(
            src_ref=ref, dst_ref=ref, send_sem=ag_send.at[idx], recv_sem=ag_recv.at[idx],
            device_id=to, device_id_type=MESH,
        )

    ag_out = [
        ag(0, 0, 0, 0, D, right),
        ag(1, 0, 0, 0, D, left),
        ag(2, 0, 0, 0, D, across),
        ag(3, 0, 3, 0, HALF, right),
        ag(4, 0, 1, HALF, HALF, left),
        ag(5, 1, 0, 0, D, right),
        ag(6, 1, 0, 0, D, left),
        ag(7, 0, 2, 0, HALF, across),
        ag(8, 0, 2, HALF, HALF, across),
    ]
    arriving = [
        (0, 3, 0, D),
        (0, 1, 0, D),
        (1, 0, 0, D),
        (0, 2, 0, HALF),
        (0, 2, HALF, HALF),
        (1, 3, 0, D),
        (1, 1, 0, D),
        (1, 2, 0, HALF),
        (1, 2, HALF, HALF),
    ]
    ag_in = [ag(k, dy, dx, lo, n, right) for k, (dy, dx, lo, n) in enumerate(arriving)]

    def sb(idx, dy, dx, lo, n, cr):
        ref = piece(chip_at(dy, dx), cr, lo, n)
        return pltpu.make_async_remote_copy(
            src_ref=ref, dst_ref=ref, send_sem=sb_send.at[idx], recv_sem=sb_recv.at[idx],
            device_id=sibling, device_id_type=MESH,
        )

    sb_list = arriving + [(0, 0, 0, D)]
    sb_out = [sb(k, dy, dx, lo, n, core) for k, (dy, dx, lo, n) in enumerate(sb_list)]
    sb_in = [sb(k, dy, dx, lo, n, 1 - core) for k, (dy, dx, lo, n) in enumerate(sb_list)]

    for k in (0, 1, 2):
        ag_out[k].start()
    sb_out[9].start()
    for load in loads[1:]:
        load.wait()
    wt[...] = wv[...].T
    bankt[...] = bankv[...].T
    sb_in[9].wait_recv()

    def compaction():
        lax.fori_loop(1, NLIB, lambda j, c: (ids_from(j).wait_recv(), c)[1], 0)
        n = NLIB * CODE_ROWS
        code = codes[...].reshape(n, 128)
        mine = (code >> OWNER_SHIFT) == me
        ones = onehot(mine)
        before = onehot(iota((128, 128), 0) < iota((128, 128), 1))
        inside = dot(ones, before)
        totals = dot(ones, jnp.ones((128, 128), BF16)).astype(BF16)
        ri, ci = iota((n, n), 0), iota((n, n), 1)
        ahead = onehot((ri // CODE_ROWS == ci // CODE_ROWS) & (ci < ri))
        pos = inside + dot(ahead, totals)
        low = (code & (2**OWNER_SHIFT - 1)) + 1
        posr[...] = jnp.where(mine, pos, -1.0).reshape(NLIB, CODE_ROWS, 128)
        valr[...] = jnp.where(mine, low.astype(F32), 0.0).reshape(NLIB, CODE_ROWS, 128)

        def one(i, carry):
            place = iota((CAP, 128), 0).astype(F32)
            both = []
            for c in (0, 1):
                s = 2 * i + c
                p_all, v_all = posr[s], valr[s]
                total = jnp.zeros((CAP, 128), F32)
                for j in range(Q * COLS // 128):
                    total += jnp.where(p_all[j : j + 1] == place, v_all[j : j + 1], 0.0)
                both.append(jnp.sum(total, axis=1, keepdims=True))
            packed = jnp.concatenate(both, axis=0)
            scol[i, :, 0:1] = packed
            pkt[0:1, pl.ds(pl.multiple_of(i * PAIR, 128), PAIR)] = to_row(packed)
            return carry

        lax.fori_loop(0, NCHIP, one, 0)
        molt[...] = molv[...].T

        def fetch(b, carry):
            lanes = pl.ds(pl.multiple_of(b * 256, 128), 256)
            row = (pkt[0:1, lanes].astype(I32) - 1) >> ROW_BITS
            pick = onehot(row == iota((MOL, 256), 0))
            mrow[:, lanes] = dot(molt[...], pick).astype(BF16)
            return carry

        lax.fori_loop(0, NSLOTS // 512, fetch, 0)
        for k in (0, 1, 2):
            ag_in[k].wait_recv()
        for k in (3, 4, 5, 6):
            ag_out[k].start()
        for k in (0, 1, 2):
            sb_out[k].start()
        lax.fori_loop(NSLOTS // 512, NSLOTS // 256, fetch, 0)

    def bank_unit(ch):
        u = dot(wt[...], gat[ch])
        rn = lax.rsqrt(jnp.sum(u * u, axis=0, keepdims=True) + 1e-6)
        u = u * rn
        unit[ch] = u
        qrow[ch, 0:1, :] = rn
        s = dot(bankv[...], u.astype(BF16))
        m = jnp.max(s, axis=0, keepdims=True)
        e = jnp.exp2((s - m) * (INV_T * LOG2E))
        qrow[ch, 1:2, :] = m * INV_T
        qrow[ch, 2:3, :] = jnp.sum(e, axis=0, keepdims=True)
        acc[ch] = dot(bankt[...], e.astype(BF16))

    def st_copy(i, j):
        return pltpu.make_async_remote_copy(
            src_ref=stats.at[me, i], dst_ref=stats.at[me, i],
            send_sem=st_send.at[j], recv_sem=st_recv.at[me],
            device_id={"lib": peer(j)}, device_id_type=MESH,
        )

    def st_all(j, s):
        return pltpu.make_async_remote_copy(
            src_ref=stats.at[s], dst_ref=stats.at[s],
            send_sem=st_send.at[j], recv_sem=st_recv.at[s],
            device_id={"lib": peer(j)}, device_id_type=MESH,
        )

    def pair_lanes(i):
        return pl.ds(pl.multiple_of(i * PAIR, 128), PAIR)

    def slot_rows(i):
        t = pkt[0:1, pair_lanes(i)].astype(I32) - 1
        second = jnp.where(iota((1, PAIR), 1) >= CAP, Q, 0)
        q = jnp.where(t < 0, -1, ((t & SLOT_MASK) >> 2) + second)
        return t >= 0, (t >= 0) & ((t & 3) == 0), onehot(q == iota((2 * Q, PAIR), 0))

    def cand_unit(i):
        lanes = pair_lanes(i)
        _, first, pick = slot_rows(i)
        q_slot = dot(unit[i].astype(BF16), pick)
        qs[:, lanes] = q_slot.astype(BF16)
        cs = jnp.sum(q_slot * mrow[:, lanes].astype(F32), axis=0, keepdims=True) * INV_T
        pkt[1:2, lanes] = cs
        part = jnp.sum(jnp.where(first, cs, 0.0), axis=1, keepdims=True)
        cs_col = to_col(cs)
        for c in (0, 1):
            t = scol[i, c * CAP : (c + 1) * CAP, 0:1].astype(I32) - 1
            q = (t & SLOT_MASK) >> 2
            chosen = jnp.where(q == iota((CAP, Q), 1), cs_col[c * CAP : (c + 1) * CAP], -1e30)
            mb = qrow[i, 1:2, c * Q : (c + 1) * Q]
            lb = qrow[i, 2:3, c * Q : (c + 1) * Q]
            top = jnp.maximum(mb, jnp.max(chosen, axis=0, keepdims=True))
            total = lb * jnp.exp(mb - top) + jnp.sum(jnp.exp(chosen - top), axis=0, keepdims=True)
            out = top + jnp.log(total)
            for k in range(3):
                stats[me, i, 3 * c + k : 3 * c + k + 1, :] = out[:, 128 * k : 128 * (k + 1)]
        stats[me, i, 6:8, :] = jnp.broadcast_to(part, (2, 128))

    def send_stats(i):
        lax.fori_loop(1, NLIB, lambda j, k: (st_copy(i, j).start(), k)[1], 0)

    def order(t):
        dy = jnp.where((t == 3) | (t >= 5), 1, 0)
        dx = jnp.where(
            (t == 1) | (t == 5), 1, jnp.where((t == 2) | (t == 6), 3, jnp.where((t == 4) | (t == 7), 2, 0))
        )
        return chip_at(dy, dx)

    bank_unit(chip)
    compaction()

    def step(t, carry):
        @pl.when(t == 1)
        def _():
            for k in (1, 0, 2):
                sb_in[k].wait_recv()

        @pl.when(t == 3)
        def _():
            for k in (3, 4):
                ag_in[k].wait_recv()
            for k in (7, 8):
                ag_out[k].start()
            for k in (3, 4):
                sb_out[k].start()

        @pl.when(t == 4)
        def _():
            for k in (3, 4):
                sb_in[k].wait_recv()
            for k in (5, 6):
                ag_in[k].wait_recv()
            for k in (5, 6):
                sb_out[k].start()

        @pl.when(t == 5)
        def _():
            for k in (5, 6):
                sb_in[k].wait_recv()

        @pl.when(t == 6)
        def _():
            for k in (7, 8):
                ag_in[k].wait_recv()
            for k in (7, 8):
                sb_out[k].start()

        @pl.when(t == 7)
        def _():
            for k in (7, 8):
                sb_in[k].wait_recv()

        last = order(t - 1)
        cand_unit(last)
        bank_unit(order(t))
        send_stats(last)
        return carry

    lax.fori_loop(1, NCHIP, step, 0)
    cand_unit(chip_at(1, 2))
    send_stats(chip_at(1, 2))

    lax.fori_loop(1, NLIB, lambda j, k: (st_all(j, peer(j)).wait_recv(), k)[1], 0)
    lax.fori_loop(1, NLIB, lambda j, k: (st_all(j, me).wait_send(), k)[1], 0)

    top = stats[0]
    for s in range(1, NLIB):
        top = jnp.maximum(top, stats[s])
    total = jnp.zeros((NCHIP, 8, 128), F32)
    first_scores = jnp.zeros((NCHIP, 8, 128), F32)
    for s in range(NLIB):
        total += jnp.exp(stats[s] - top)
        first_scores += stats[s]
    value = top + jnp.log(total)
    lse[...] = value
    in_row = iota((NCHIP, 8, 128), 1)
    lane0 = iota((NCHIP, 8, 128), 2) == 0
    terms = jnp.where(in_row < 6, value, jnp.where((in_row == 6) & lane0, -first_scores, 0.0))
    terms = jnp.sum(terms, axis=0)
    group_loss = jnp.sum(jnp.sum(terms, axis=1, keepdims=True), axis=0, keepdims=True)
    dlb[dp] = jnp.broadcast_to(group_loss, (8, 128))

    def dl_copy(j, s, to):
        return pltpu.make_async_remote_copy(
            src_ref=dlb.at[s], dst_ref=dlb.at[s], send_sem=dl_send.at[j], recv_sem=dl_recv.at[s],
            device_id={"dp": to}, device_id_type=MESH,
        )

    lax.fori_loop(1, ndp, lambda j, k: (dl_copy(j, dp, dpeer(j)).start(), k)[1], 0)

    gwacc[...] = jnp.zeros((D, D), F32)

    def grad_unit(i, carry):
        lanes = pair_lanes(i)
        lse_row = jnp.concatenate([lse[i, k : k + 1, :] for k in range(6)], axis=1)
        valid, first, pick = slot_rows(i)
        high = lse_row.astype(BF16).astype(F32)
        middle = (lse_row - high).astype(BF16).astype(F32)
        low = lse_row - high - middle
        thirds = jnp.concatenate([high, middle, low, jnp.zeros((5, 2 * Q), F32)], axis=0)
        thirds = dot(thirds.astype(BF16), pick)
        lse_slot = thirds[0:1] + thirds[1:2] + thirds[2:3]
        coef = jnp.where(
            valid, jnp.exp(pkt[1:2, lanes] - lse_slot) - jnp.where(first, 1.0, 0.0), 0.0
        )
        qs[:, lanes] = (qs[:, lanes].astype(F32) * (coef * INV_T)).astype(BF16)
        weighted = (mrow[:, lanes].astype(F32) * coef).astype(BF16)
        scale = jnp.exp(qrow[i, 1:2, :] - lse_row)
        dq = acc[i] * scale + dot_nt(weighted, pick)
        u = unit[i]
        along = jnp.sum(u * dq, axis=0, keepdims=True)
        du = (dq - u * along) * (qrow[i, 0:1, :] * INV_T)
        gwacc[...] += dot_nt(gat[i], du.astype(BF16))
        return carry

    lax.fori_loop(0, NCHIP, grad_unit, 0)

    gwb[...] = gwacc[...].astype(BF16).reshape(NLIB, D // NLIB, D)

    def rs_copy(j, src, dst, to):
        return pltpu.make_async_remote_copy(
            src_ref=gwb.at[src], dst_ref=rsb.at[dst], send_sem=rs_send.at[j], recv_sem=rs_recv.at[dst],
            device_id={"lib": to}, device_id_type=MESH,
        )

    lax.fori_loop(1, NLIB, lambda j, k: (rs_copy(j, peer(j), me, peer(j)).start(), k)[1], 0)

    def out_copy(r):
        return pltpu.make_async_copy(
            acc.at[r, pl.ds(0, 256), pl.ds(0, D)],
            gm_out.at[pl.ds(pl.multiple_of(r * 256, 256), 256), :],
            out_sem.at[r],
        )

    def scatter(r, carry):
        row = (pkt[0:1, :].astype(I32) - 1) >> ROW_BITS
        pick = onehot(row == iota((256, NSLOTS), 0) + r * 256)
        acc[r, 0:256, 0:D] = dot_nt(pick, qs[...])
        out_copy(r).start()
        return carry

    lax.fori_loop(0, 3, scatter, 0)

    lax.fori_loop(1, NLIB, lambda j, k: (rs_copy(j, me, peer(j), peer(j)).wait_recv(), k)[1], 0)
    rsb[me] = gwb[me]
    part = jnp.zeros((D // NLIB, D), F32)
    for s in range(NLIB):
        part += rsb[s].astype(F32)
    dpb[dp] = part.astype(BF16)

    def dp_copy(j, s, to):
        return pltpu.make_async_remote_copy(
            src_ref=dpb.at[s], dst_ref=dpb.at[s], send_sem=dp_send.at[j], recv_sem=dp_recv.at[s],
            device_id={"dp": to}, device_id_type=MESH,
        )

    lax.fori_loop(1, ndp, lambda j, k: (dp_copy(j, dp, dpeer(j)).start(), k)[1], 0)

    lax.fori_loop(3, 6, scatter, 0)

    lax.fori_loop(1, ndp, lambda j, k: (dp_copy(j, dpeer(j), dpeer(j)).wait_recv(), k)[1], 0)
    part = jnp.zeros((D // NLIB, D), F32)
    for s in range(ndp):
        part += dpb[s].astype(F32)
    ggb[me] = part.astype(BF16)

    def gg_copy(j, s, to):
        return pltpu.make_async_remote_copy(
            src_ref=ggb.at[s], dst_ref=ggb.at[s], send_sem=gg_send.at[j], recv_sem=gg_recv.at[s],
            device_id={"lib": to}, device_id_type=MESH,
        )

    lax.fori_loop(1, NLIB, lambda j, k: (gg_copy(j, me, peer(j)).start(), k)[1], 0)

    lax.fori_loop(6, 8, scatter, 0)

    lax.fori_loop(1, ndp, lambda j, k: (dl_copy(j, dpeer(j), dpeer(j)).wait_recv(), k)[1], 0)
    whole = jnp.zeros((8, 128), F32)
    for s in range(ndp):
        whole += dlb[s]
    loss_out[...] = whole[0:1, 0:1] * (1.0 / (Q * NLIB * ndp))

    lax.fori_loop(1, NLIB, lambda j, k: (gg_copy(j, peer(j), peer(j)).wait_recv(), k)[1], 0)
    gw_out[...] = ggb[...].reshape(D, D)

    lax.fori_loop(0, 8, lambda r, k: (out_copy(r).wait(), k)[1], 0)
    lax.fori_loop(1, NLIB, lambda j, k: (ids_copy(j).wait_send(), k)[1], 0)
    for k in range(9):
        ag_out[k].wait_send()
    for k in range(10):
        sb_out[k].wait_send()
    lax.fori_loop(1, NLIB, lambda j, k: (rs_copy(j, peer(j), me, peer(j)).wait_send(), k)[1], 0)
    lax.fori_loop(1, NLIB, lambda j, k: (gg_copy(j, me, peer(j)).wait_send(), k)[1], 0)
    lax.fori_loop(1, ndp, lambda j, k: (dp_copy(j, dp, dpeer(j)).wait_send(), k)[1], 0)
    lax.fori_loop(1, ndp, lambda j, k: (dl_copy(j, dp, dpeer(j)).wait_send(), k)[1], 0)


def per_device(ndp, spectra, w_proj, fixed_library_matrix, mol_rows, cand_ids, iso_count):
    owner = cand_ids // MOL % NLIB
    row = cand_ids % MOL
    slot = lax.broadcasted_iota(I32, (Q, COLS), 0) * COLS + lax.broadcasted_iota(I32, (Q, COLS), 1)
    live = lax.broadcasted_iota(I32, (Q, COLS), 1) <= iso_count[:, None]
    code = jnp.where(live, (owner << OWNER_SHIFT) | (row << ROW_BITS) | slot, -1)
    code = jnp.pad(code.reshape(Q * COLS // 128, 128), ((0, CODE_ROWS - Q * COLS // 128), (0, 0)), constant_values=-1)
    vmem = pl.BlockSpec(memory_space=pltpu.VMEM)
    hbm = pl.BlockSpec(memory_space=pl.ANY)
    dma = pltpu.SemaphoreType.DMA
    gw, gm, loss = pl.pallas_call(
        functools.partial(kernel, ndp),
        out_shape=(
            jax.ShapeDtypeStruct((D, D), BF16),
            jax.ShapeDtypeStruct((MOL, D), F32),
            jax.ShapeDtypeStruct((1, 1), F32),
        ),
        in_specs=[hbm, hbm, hbm, hbm, vmem],
        out_specs=(vmem, hbm, vmem),
        scratch_shapes=[
            pltpu.VMEM((Q, D), BF16),
            pltpu.VMEM((NCHIP, D, 2 * Q), BF16),
            pltpu.VMEM((D, D), BF16),
            pltpu.VMEM((D, D), BF16),
            pltpu.VMEM((BANK, D), BF16),
            pltpu.VMEM((D, BANK), BF16),
            pltpu.VMEM((MOL, D), BF16),
            pltpu.VMEM((D, MOL), BF16),
            pltpu.VMEM((NLIB, CODE_ROWS, 128), I32),
            pltpu.VMEM((NLIB, CODE_ROWS, 128), F32),
            pltpu.VMEM((NLIB, CODE_ROWS, 128), F32),
            pltpu.VMEM((8, NSLOTS), F32),
            pltpu.VMEM((D, NSLOTS), BF16),
            pltpu.VMEM((D, NSLOTS), BF16),
            pltpu.VMEM((NCHIP, D, 2 * Q), F32),
            pltpu.VMEM((NCHIP, D, 2 * Q), F32),
            pltpu.VMEM((NCHIP, 8, 2 * Q), F32),
            pltpu.VMEM((NCHIP, PAIR, 128), F32),
            pltpu.VMEM((NLIB, NCHIP, 8, 128), F32),
            pltpu.VMEM((NCHIP, 8, 128), F32),
            pltpu.VMEM((D, D), F32),
            pltpu.VMEM((NLIB, D // NLIB, D), BF16),
            pltpu.VMEM((NLIB, D // NLIB, D), BF16),
            pltpu.VMEM((ndp, D // NLIB, D), BF16),
            pltpu.VMEM((ndp, 8, 128), F32),
            pltpu.VMEM((NLIB, D // NLIB, D), BF16),
            dma((4,)),
            dma((NLIB,)),
            dma((NLIB,)),
            dma((9,)),
            dma((9,)),
            dma((10,)),
            dma((10,)),
            dma((NLIB,)),
            dma((NLIB,)),
            dma((NLIB,)),
            dma((NLIB,)),
            dma((ndp,)),
            dma((ndp,)),
            dma((ndp,)),
            dma((ndp,)),
            dma((NLIB,)),
            dma((NLIB,)),
            dma((8,)),
        ],
        compiler_params=pltpu.CompilerParams(
            collective_id=0, has_side_effects=True, vmem_limit_bytes=62 * 1024 * 1024
        ),
    )(spectra, w_proj, fixed_library_matrix, mol_rows, code)
    return gw.astype(F32), gm, loss.reshape(())


def solution(mesh):
    placed = (
        P(("dp", "lib"), None),
        P(),
        P("lib", None),
        P(("dp", "lib"), None),
        P(("dp", "lib"), None),
        P(("dp", "lib")),
    )
    return jax.shard_map(
        functools.partial(per_device, mesh.shape["dp"]),
        mesh=mesh,
        in_specs=placed,
        out_specs=(P(), P(("dp", "lib"), None), P()),
        check_vma=False,
    )
```

```python
import functools

import jax
import jax.numpy as jnp
from jax import lax
from jax.experimental import pallas as pl
from jax.experimental.pallas import tpu as pltpu
from jax.sharding import PartitionSpec as P

F32 = jnp.float32
BF16 = jnp.bfloat16
I32 = jnp.int32
MESH = pl.DeviceIdType.MESH

D = 512
Q = 384
COLS = 4
NLIB = 16
NCHIP = 8
CAP = 192
BANK = 1024
MOL = 2048
CODE_ROWS = 16
ROW_BITS = 11
SLOT_MASK = 2047
OWNER_SHIFT = 22
INV_T = 1.0 / 0.07
PIECE = D // 2 // NLIB
LOG2E = 1.4426950408889634
NSLOTS = NLIB * CAP
PAIR = 2 * CAP


def iota(shape, dim):
    return lax.broadcasted_iota(I32, shape, dim)


def to_row(v):
    eye = iota((128, 128), 0) == iota((128, 128), 1)
    return jnp.concatenate(
        [
            jnp.sum(jnp.where(eye, v[lo : lo + 128], 0.0), axis=0, keepdims=True)
            for lo in range(0, v.shape[0], 128)
        ],
        axis=1,
    )


def to_col(v):
    eye = iota((128, 128), 0) == iota((128, 128), 1)
    return jnp.concatenate(
        [
            jnp.sum(jnp.where(eye, v[:, lo : lo + 128], 0.0), axis=1, keepdims=True)
            for lo in range(0, v.shape[1], 128)
        ],
        axis=0,
    )


def onehot(mask):
    return jnp.where(mask, 1.0, 0.0).astype(BF16)


def dot(a, b):
    return jnp.dot(a, b, preferred_element_type=F32)


def dot_nt(a, b):
    return lax.dot_general(a, b, (((1,), (1,)), ((), ())), preferred_element_type=F32)


def kernel(
    ndp,
    spec_hbm,
    w_hbm,
    bank_hbm,
    mol_hbm,
    code_ref,
    gw_out,
    gm_out,
    loss_out,
    spv,
    gat,
    wv,
    wt,
    bankv,
    bankt,
    molv,
    molt,
    codes,
    posr,
    valr,
    pkt,
    mrow,
    qs,
    unit,
    acc,
    qrow,
    scol,
    stats,
    lse,
    dub,
    gwb,
    rsb,
    dpb,
    dlb,
    ggb,
    loc_sem,
    ids_send,
    ids_recv,
    ag_send,
    ag_recv,
    sb_send,
    sb_recv,
    st_send,
    st_recv,
    rs_send,
    rs_recv,
    dp_send,
    dp_recv,
    dl_send,
    dl_recv,
    gg_send,
    gg_recv,
    out_sem,
):
    dp = lax.axis_index("dp")
    me = lax.axis_index("lib")
    core = lax.rem(me, 2)
    chip = me // 2
    y = chip // 4
    x = lax.rem(chip, 4)

    def chip_at(dy, dx):
        return lax.rem(y + dy, 2) * 4 + lax.rem(x + dx, 4)

    def peer(j):
        return lax.rem(me + j, NLIB)

    def dpeer(j):
        return lax.rem(dp + j, ndp)

    loads = [
        pltpu.make_async_copy(spec_hbm, spv, loc_sem.at[0]),
        pltpu.make_async_copy(w_hbm, wv, loc_sem.at[1]),
        pltpu.make_async_copy(bank_hbm, bankv, loc_sem.at[2]),
        pltpu.make_async_copy(mol_hbm, molv, loc_sem.at[3]),
    ]
    for load in loads:
        load.start()

    barrier = pltpu.get_barrier_semaphore()

    def greet(j, carry):
        pl.semaphore_signal(barrier, inc=1, device_id={"lib": peer(j)}, device_id_type=MESH)
        return carry

    lax.fori_loop(1, NLIB, greet, 0)

    def greet_dp(j, carry):
        pl.semaphore_signal(barrier, inc=1, device_id={"dp": dpeer(j)}, device_id_type=MESH)
        return carry

    lax.fori_loop(1, ndp, greet_dp, 0)
    codes[me] = jnp.concatenate(
        [code_ref[...], jnp.full((CODE_ROWS - Q * COLS // 128, 128), -1, I32)], axis=0
    )
    loads[0].wait()
    gat[chip, :, pl.ds(pl.multiple_of(core * Q, 128), Q)] = spv[...].T
    pl.semaphore_wait(barrier, NLIB - 1 + ndp - 1)

    def ids_copy(j):
        return pltpu.make_async_remote_copy(
            src_ref=codes.at[me],
            dst_ref=codes.at[me],
            send_sem=ids_send.at[j],
            recv_sem=ids_recv.at[me],
            device_id={"lib": peer(j)},
            device_id_type=MESH,
        )

    def ids_from(j):
        s = peer(j)
        return pltpu.make_async_remote_copy(
            src_ref=codes.at[s],
            dst_ref=codes.at[s],
            send_sem=ids_send.at[j],
            recv_sem=ids_recv.at[s],
            device_id={"lib": s},
            device_id_type=MESH,
        )

    lax.fori_loop(1, NLIB, lambda j, c: (ids_copy(j).start(), c)[1], 0)

    def piece(ch, cr, lo, n):
        return gat.at[ch, pl.ds(lo, n), pl.ds(pl.multiple_of(cr * Q, 128), Q)]

    HALF = D // 2
    right = {"lib": chip_at(0, 1) * 2 + core}
    left = {"lib": chip_at(0, 3) * 2 + core}
    across = {"lib": chip_at(1, 0) * 2 + core}
    sibling = {"lib": chip * 2 + 1 - core}

    def ag(idx, dy, dx, lo, n, to):
        ref = piece(chip_at(dy, dx), core, lo, n)
        return pltpu.make_async_remote_copy(
            src_ref=ref, dst_ref=ref, send_sem=ag_send.at[idx], recv_sem=ag_recv.at[idx],
            device_id=to, device_id_type=MESH,
        )

    ag_out = [
        ag(0, 0, 0, 0, D, right),
        ag(1, 0, 0, 0, D, left),
        ag(2, 0, 0, 0, D, across),
        ag(3, 0, 3, 0, HALF, right),
        ag(4, 0, 1, HALF, HALF, left),
        ag(5, 1, 0, 0, D, right),
        ag(6, 1, 0, 0, D, left),
        ag(7, 0, 2, 0, HALF, across),
        ag(8, 0, 2, HALF, HALF, across),
    ]
    arriving = [
        (0, 3, 0, D),
        (0, 1, 0, D),
        (1, 0, 0, D),
        (0, 2, 0, HALF),
        (0, 2, HALF, HALF),
        (1, 3, 0, D),
        (1, 1, 0, D),
        (1, 2, 0, HALF),
        (1, 2, HALF, HALF),
    ]
    ag_in = [ag(k, dy, dx, lo, n, right) for k, (dy, dx, lo, n) in enumerate(arriving)]

    def sb(idx, dy, dx, lo, n, cr):
        ref = piece(chip_at(dy, dx), cr, lo, n)
        return pltpu.make_async_remote_copy(
            src_ref=ref, dst_ref=ref, send_sem=sb_send.at[idx], recv_sem=sb_recv.at[idx],
            device_id=sibling, device_id_type=MESH,
        )

    sb_list = arriving + [(0, 0, 0, D)]
    sb_out = [sb(k, dy, dx, lo, n, core) for k, (dy, dx, lo, n) in enumerate(sb_list)]
    sb_in = [sb(k, dy, dx, lo, n, 1 - core) for k, (dy, dx, lo, n) in enumerate(sb_list)]

    for k in (0, 1, 2):
        ag_out[k].start()
    sb_out[9].start()
    for load in loads[1:]:
        load.wait()
    wt[...] = wv[...].T
    bankt[...] = bankv[...].T
    sb_in[9].wait_recv()

    def compaction():
        lax.fori_loop(1, NLIB, lambda j, c: (ids_from(j).wait_recv(), c)[1], 0)
        n = NLIB * CODE_ROWS
        code = codes[...].reshape(n, 128)
        mine = (code >> OWNER_SHIFT) == me
        ones = onehot(mine)
        before = onehot(iota((128, 128), 0) < iota((128, 128), 1))
        inside = dot(ones, before)
        totals = dot(ones, jnp.ones((128, 128), BF16)).astype(BF16)
        ri, ci = iota((n, n), 0), iota((n, n), 1)
        ahead = onehot((ri // CODE_ROWS == ci // CODE_ROWS) & (ci < ri))
        pos = inside + dot(ahead, totals)
        low = (code & (2**OWNER_SHIFT - 1)) + 1
        posr[...] = jnp.where(mine, pos, -1.0).reshape(NLIB, CODE_ROWS, 128)
        valr[...] = jnp.where(mine, low.astype(F32), 0.0).reshape(NLIB, CODE_ROWS, 128)

        def one(i, carry):
            place = iota((CAP, 128), 0).astype(F32)
            both = []
            for c in (0, 1):
                s = 2 * i + c
                p_all, v_all = posr[s], valr[s]
                total = jnp.zeros((CAP, 128), F32)
                for j in range(Q * COLS // 128):
                    total += jnp.where(p_all[j : j + 1] == place, v_all[j : j + 1], 0.0)
                both.append(jnp.sum(total, axis=1, keepdims=True))
            packed = jnp.concatenate(both, axis=0)
            scol[i, :, 0:1] = packed
            pkt[0:1, pl.ds(pl.multiple_of(i * PAIR, 128), PAIR)] = to_row(packed)
            return carry

        lax.fori_loop(0, NCHIP, one, 0)
        molt[...] = molv[...].T

        def fetch(b, carry):
            lanes = pl.ds(pl.multiple_of(b * 768, 128), 768)
            row = (pkt[0:1, lanes].astype(I32) - 1) >> ROW_BITS
            pick = onehot(row == iota((MOL, 768), 0))
            mrow[:, lanes] = dot(molt[...], pick).astype(BF16)
            return carry

        lax.fori_loop(0, 2, fetch, 0)
        for k in (0, 1, 2):
            ag_in[k].wait_recv()
        for k in (3, 4, 5, 6):
            ag_out[k].start()
        for k in (0, 1, 2):
            sb_out[k].start()
        lax.fori_loop(2, NSLOTS // 768, fetch, 0)

    def bank_unit(ch):
        u = dot(wt[...], gat[ch])
        rn = lax.rsqrt(jnp.sum(u * u, axis=0, keepdims=True) + 1e-6)
        u = u * rn
        unit[ch] = u
        qrow[ch, 0:1, :] = rn
        s = dot(bankv[...], u.astype(BF16))
        m = jnp.max(s, axis=0, keepdims=True)
        e = jnp.exp2((s - m) * (INV_T * LOG2E))
        qrow[ch, 1:2, :] = m * INV_T
        qrow[ch, 2:3, :] = jnp.sum(e, axis=0, keepdims=True)
        acc[ch] = dot(bankt[...], e.astype(BF16))

    def st_copy(i, j):
        return pltpu.make_async_remote_copy(
            src_ref=stats.at[me, i], dst_ref=stats.at[me, i],
            send_sem=st_send.at[j], recv_sem=st_recv.at[me],
            device_id={"lib": peer(j)}, device_id_type=MESH,
        )

    def st_all(j, s):
        return pltpu.make_async_remote_copy(
            src_ref=stats.at[s], dst_ref=stats.at[s],
            send_sem=st_send.at[j], recv_sem=st_recv.at[s],
            device_id={"lib": peer(j)}, device_id_type=MESH,
        )

    def pair_lanes(i):
        return pl.ds(pl.multiple_of(i * PAIR, 128), PAIR)

    def slot_rows(i):
        t = pkt[0:1, pair_lanes(i)].astype(I32) - 1
        second = jnp.where(iota((1, PAIR), 1) >= CAP, Q, 0)
        q = jnp.where(t < 0, -1, ((t & SLOT_MASK) >> 2) + second)
        return t >= 0, (t >= 0) & ((t & 3) == 0), onehot(q == iota((2 * Q, PAIR), 0))

    def cand_unit(i):
        lanes = pair_lanes(i)
        _, first, pick = slot_rows(i)
        q_slot = dot(unit[i].astype(BF16), pick)
        qs[:, lanes] = q_slot.astype(BF16)
        cs = jnp.sum(q_slot * mrow[:, lanes].astype(F32), axis=0, keepdims=True) * INV_T
        pkt[1:2, lanes] = cs
        part = jnp.sum(jnp.where(first, cs, 0.0), axis=1, keepdims=True)
        cs_col = to_col(cs)
        for c in (0, 1):
            t = scol[i, c * CAP : (c + 1) * CAP, 0:1].astype(I32) - 1
            q = (t & SLOT_MASK) >> 2
            chosen = jnp.where(q == iota((CAP, Q), 1), cs_col[c * CAP : (c + 1) * CAP], -1e30)
            mb = qrow[i, 1:2, c * Q : (c + 1) * Q]
            lb = qrow[i, 2:3, c * Q : (c + 1) * Q]
            top = jnp.maximum(mb, jnp.max(chosen, axis=0, keepdims=True))
            total = lb * jnp.exp(mb - top) + jnp.sum(jnp.exp(chosen - top), axis=0, keepdims=True)
            out = top + jnp.log(total)
            for k in range(3):
                stats[me, i, 3 * c + k : 3 * c + k + 1, :] = out[:, 128 * k : 128 * (k + 1)]
        stats[me, i, 6:8, :] = jnp.broadcast_to(part, (2, 128))

    def send_stats(i):
        lax.fori_loop(1, NLIB, lambda j, k: (st_copy(i, j).start(), k)[1], 0)

    def order(t):
        dy = jnp.where((t == 3) | (t >= 5), 1, 0)
        dx = jnp.where(
            (t == 1) | (t == 5), 1, jnp.where((t == 2) | (t == 6), 3, jnp.where((t == 4) | (t == 7), 2, 0))
        )
        return chip_at(dy, dx)

    bank_unit(chip)
    compaction()

    def step(t, carry):
        @pl.when(t == 1)
        def _():
            for k in (1, 0, 2):
                sb_in[k].wait_recv()

        @pl.when(t == 3)
        def _():
            for k in (3, 4):
                ag_in[k].wait_recv()
            for k in (7, 8):
                ag_out[k].start()
            for k in (3, 4):
                sb_out[k].start()

        @pl.when(t == 4)
        def _():
            for k in (3, 4):
                sb_in[k].wait_recv()
            for k in (5, 6):
                ag_in[k].wait_recv()
            for k in (5, 6):
                sb_out[k].start()

        @pl.when(t == 5)
        def _():
            for k in (5, 6):
                sb_in[k].wait_recv()

        @pl.when(t == 6)
        def _():
            for k in (7, 8):
                ag_in[k].wait_recv()
            for k in (7, 8):
                sb_out[k].start()

        @pl.when(t == 7)
        def _():
            for k in (7, 8):
                sb_in[k].wait_recv()

        last = order(t - 1)
        cand_unit(last)
        bank_unit(order(t))
        send_stats(last)
        return carry

    lax.fori_loop(1, NCHIP, step, 0)
    cand_unit(chip_at(1, 2))
    send_stats(chip_at(1, 2))

    lax.fori_loop(1, NLIB, lambda j, k: (st_all(j, peer(j)).wait_recv(), k)[1], 0)
    lax.fori_loop(1, NLIB, lambda j, k: (st_all(j, me).wait_send(), k)[1], 0)

    top = stats[0]
    for s in range(1, NLIB):
        top = jnp.maximum(top, stats[s])
    total = jnp.zeros((NCHIP, 8, 128), F32)
    first_scores = jnp.zeros((NCHIP, 8, 128), F32)
    for s in range(NLIB):
        total += jnp.exp(stats[s] - top)
        first_scores += stats[s]
    value = top + jnp.log(total)
    lse[...] = value
    in_row = iota((NCHIP, 8, 128), 1)
    lane0 = iota((NCHIP, 8, 128), 2) == 0
    terms = jnp.where(in_row < 6, value, jnp.where((in_row == 6) & lane0, -first_scores, 0.0))
    terms = jnp.sum(terms, axis=0)
    group_loss = jnp.sum(jnp.sum(terms, axis=1, keepdims=True), axis=0, keepdims=True)
    dlb[dp] = jnp.broadcast_to(group_loss, (8, 128))

    def dl_copy(j, s, to):
        return pltpu.make_async_remote_copy(
            src_ref=dlb.at[s], dst_ref=dlb.at[s], send_sem=dl_send.at[j], recv_sem=dl_recv.at[s],
            device_id={"dp": to}, device_id_type=MESH,
        )

    lax.fori_loop(1, ndp, lambda j, k: (dl_copy(j, dp, dpeer(j)).start(), k)[1], 0)

    def grad_unit(i, carry):
        lanes = pair_lanes(i)
        lse_row = jnp.concatenate([lse[i, k : k + 1, :] for k in range(6)], axis=1)
        valid, first, pick = slot_rows(i)
        high = lse_row.astype(BF16).astype(F32)
        middle = (lse_row - high).astype(BF16).astype(F32)
        low = lse_row - high - middle
        thirds = jnp.concatenate([high, middle, low, jnp.zeros((5, 2 * Q), F32)], axis=0)
        thirds = dot(thirds.astype(BF16), pick)
        lse_slot = thirds[0:1] + thirds[1:2] + thirds[2:3]
        coef = jnp.where(
            valid, jnp.exp(pkt[1:2, lanes] - lse_slot) - jnp.where(first, 1.0, 0.0), 0.0
        )
        qs[:, lanes] = (qs[:, lanes].astype(F32) * (coef * INV_T)).astype(BF16)
        weighted = (mrow[:, lanes].astype(F32) * coef).astype(BF16)
        scale = jnp.exp(qrow[i, 1:2, :] - lse_row)
        dq = acc[i] * scale + dot_nt(weighted, pick)
        u = unit[i]
        along = jnp.sum(u * dq, axis=0, keepdims=True)
        du = (dq - u * along) * (qrow[i, 0:1, :] * INV_T)
        dub[i] = du.astype(BF16)
        return carry

    lax.fori_loop(0, NCHIP, grad_unit, 0)

    def rs_copy(h, j, src, dst, to):
        return pltpu.make_async_remote_copy(
            src_ref=gwb.at[h, src], dst_ref=rsb.at[h, dst],
            send_sem=rs_send.at[h, j], recv_sem=rs_recv.at[h, dst],
            device_id={"lib": to}, device_id_type=MESH,
        )

    def dp_copy(h, j, s, to):
        return pltpu.make_async_remote_copy(
            src_ref=dpb.at[h, s], dst_ref=dpb.at[h, s],
            send_sem=dp_send.at[h, j], recv_sem=dp_recv.at[h, s],
            device_id={"dp": to}, device_id_type=MESH,
        )

    def gg_copy(h, j, s, to):
        return pltpu.make_async_remote_copy(
            src_ref=ggb.at[h, s], dst_ref=ggb.at[h, s],
            send_sem=gg_send.at[h, j], recv_sem=gg_recv.at[h, s],
            device_id={"lib": to}, device_id_type=MESH,
        )

    def rs_begin(h):
        rows = slice(h * (D // 2), (h + 1) * (D // 2))
        half = dot_nt(gat[0, rows, :], dub[0])
        for i in range(1, NCHIP):
            half += dot_nt(gat[i, rows, :], dub[i])
        gwb[h] = half.astype(BF16).reshape(NLIB, PIECE, D)
        lax.fori_loop(1, NLIB, lambda j, k: (rs_copy(h, j, peer(j), me, peer(j)).start(), k)[1], 0)
        rsb[h, me] = gwb[h, me]

    def dp_begin(h):
        lax.fori_loop(1, NLIB, lambda j, k: (rs_copy(h, j, me, peer(j), peer(j)).wait_recv(), k)[1], 0)
        part = rsb[h, 0].astype(F32)
        for s in range(1, NLIB):
            part += rsb[h, s].astype(F32)
        dpb[h, dp] = part.astype(BF16)
        lax.fori_loop(1, ndp, lambda j, k: (dp_copy(h, j, dp, dpeer(j)).start(), k)[1], 0)

    def gg_begin(h):
        lax.fori_loop(1, ndp, lambda j, k: (dp_copy(h, j, dpeer(j), dpeer(j)).wait_recv(), k)[1], 0)
        part = dpb[h, 0].astype(F32)
        for s in range(1, ndp):
            part += dpb[h, s].astype(F32)
        ggb[h, me] = part.astype(BF16)
        lax.fori_loop(1, NLIB, lambda j, k: (gg_copy(h, j, me, peer(j)).start(), k)[1], 0)

    def gg_end(h):
        lax.fori_loop(1, NLIB, lambda j, k: (gg_copy(h, j, peer(j), peer(j)).wait_recv(), k)[1], 0)

    rs_begin(0)
    rs_begin(1)

    def out_copy(r):
        return pltpu.make_async_copy(
            acc.at[r, pl.ds(0, 256), pl.ds(0, D)],
            gm_out.at[pl.ds(pl.multiple_of(r * 256, 256), 256), :],
            out_sem.at[r],
        )

    def scatter(r, carry):
        row = (pkt[0:1, :].astype(I32) - 1) >> ROW_BITS
        pick = onehot(row == iota((256, NSLOTS), 0) + r * 256)
        acc[r, 0:256, 0:D] = dot_nt(pick, qs[...])
        out_copy(r).start()
        return carry

    lax.fori_loop(0, 2, scatter, 0)
    dp_begin(0)
    lax.fori_loop(2, 4, scatter, 0)
    dp_begin(1)
    lax.fori_loop(4, 6, scatter, 0)
    gg_begin(0)
    lax.fori_loop(6, 8, scatter, 0)
    gg_begin(1)

    lax.fori_loop(1, ndp, lambda j, k: (dl_copy(j, dpeer(j), dpeer(j)).wait_recv(), k)[1], 0)
    whole = jnp.zeros((8, 128), F32)
    for s in range(ndp):
        whole += dlb[s]
    loss_out[...] = whole[0:1, 0:1] * (1.0 / (Q * NLIB * ndp))

    gg_end(0)
    gg_end(1)
    gw_out[...] = ggb[...].reshape(D, D)

    lax.fori_loop(0, 8, lambda r, k: (out_copy(r).wait(), k)[1], 0)
    lax.fori_loop(1, NLIB, lambda j, k: (ids_copy(j).wait_send(), k)[1], 0)
    for k in range(9):
        ag_out[k].wait_send()
    for k in range(10):
        sb_out[k].wait_send()
    for h in (0, 1):
        lax.fori_loop(1, NLIB, lambda j, k: (rs_copy(h, j, peer(j), me, peer(j)).wait_send(), k)[1], 0)
        lax.fori_loop(1, NLIB, lambda j, k: (gg_copy(h, j, me, peer(j)).wait_send(), k)[1], 0)
        lax.fori_loop(1, ndp, lambda j, k: (dp_copy(h, j, dp, dpeer(j)).wait_send(), k)[1], 0)
    lax.fori_loop(1, ndp, lambda j, k: (dl_copy(j, dp, dpeer(j)).wait_send(), k)[1], 0)


def per_device(ndp, spectra, w_proj, fixed_library_matrix, mol_rows, cand_ids, iso_count):
    owner = cand_ids // MOL % NLIB
    row = cand_ids % MOL
    slot = lax.broadcasted_iota(I32, (Q, COLS), 0) * COLS + lax.broadcasted_iota(I32, (Q, COLS), 1)
    live = lax.broadcasted_iota(I32, (Q, COLS), 1) <= iso_count[:, None]
    code = jnp.where(live, (owner << OWNER_SHIFT) | (row << ROW_BITS) | slot, -1)
    code = code.reshape(Q * COLS // 128, 128)
    vmem = pl.BlockSpec(memory_space=pltpu.VMEM)
    hbm = pl.BlockSpec(memory_space=pl.ANY)
    dma = pltpu.SemaphoreType.DMA
    gw, gm, loss = pl.pallas_call(
        functools.partial(kernel, ndp),
        out_shape=(
            jax.ShapeDtypeStruct((D, D), BF16),
            jax.ShapeDtypeStruct((MOL, D), F32),
            jax.ShapeDtypeStruct((1, 1), F32),
        ),
        in_specs=[hbm, hbm, hbm, hbm, vmem],
        out_specs=(vmem, hbm, vmem),
        scratch_shapes=[
            pltpu.VMEM((Q, D), BF16),
            pltpu.VMEM((NCHIP, D, 2 * Q), BF16),
            pltpu.VMEM((D, D), BF16),
            pltpu.VMEM((D, D), BF16),
            pltpu.VMEM((BANK, D), BF16),
            pltpu.VMEM((D, BANK), BF16),
            pltpu.VMEM((MOL, D), BF16),
            pltpu.VMEM((D, MOL), BF16),
            pltpu.VMEM((NLIB, CODE_ROWS, 128), I32),
            pltpu.VMEM((NLIB, CODE_ROWS, 128), F32),
            pltpu.VMEM((NLIB, CODE_ROWS, 128), F32),
            pltpu.VMEM((8, NSLOTS), F32),
            pltpu.VMEM((D, NSLOTS), BF16),
            pltpu.VMEM((D, NSLOTS), BF16),
            pltpu.VMEM((NCHIP, D, 2 * Q), F32),
            pltpu.VMEM((NCHIP, D, 2 * Q), F32),
            pltpu.VMEM((NCHIP, 8, 2 * Q), F32),
            pltpu.VMEM((NCHIP, PAIR, 128), F32),
            pltpu.VMEM((NLIB, NCHIP, 8, 128), F32),
            pltpu.VMEM((NCHIP, 8, 128), F32),
            pltpu.VMEM((NCHIP, D, 2 * Q), BF16),
            pltpu.VMEM((2, NLIB, PIECE, D), BF16),
            pltpu.VMEM((2, NLIB, PIECE, D), BF16),
            pltpu.VMEM((2, ndp, PIECE, D), BF16),
            pltpu.VMEM((ndp, 8, 128), F32),
            pltpu.VMEM((2, NLIB, PIECE, D), BF16),
            dma((4,)),
            dma((NLIB,)),
            dma((NLIB,)),
            dma((9,)),
            dma((9,)),
            dma((10,)),
            dma((10,)),
            dma((NLIB,)),
            dma((NLIB,)),
            dma((2, NLIB)),
            dma((2, NLIB)),
            dma((2, ndp)),
            dma((2, ndp)),
            dma((ndp,)),
            dma((ndp,)),
            dma((2, NLIB)),
            dma((2, NLIB)),
            dma((8,)),
        ],
        compiler_params=pltpu.CompilerParams(
            collective_id=0, has_side_effects=True, vmem_limit_bytes=62 * 1024 * 1024
        ),
    )(spectra, w_proj, fixed_library_matrix, mol_rows, code)
    return gw.astype(F32), gm, loss.reshape(())


def solution(mesh):
    placed = (
        P(("dp", "lib"), None),
        P(),
        P("lib", None),
        P(("dp", "lib"), None),
        P(("dp", "lib"), None),
        P(("dp", "lib")),
    )
    return jax.shard_map(
        functools.partial(per_device, mesh.shape["dp"]),
        mesh=mesh,
        in_specs=placed,
        out_specs=(P(), P(("dp", "lib"), None), P()),
        check_vma=False,
    )
```

```python
import functools

import jax
import jax.numpy as jnp
from jax import lax
from jax.experimental import pallas as pl
from jax.experimental.pallas import tpu as pltpu
from jax.sharding import PartitionSpec as P

F32 = jnp.float32
BF16 = jnp.bfloat16
I32 = jnp.int32
MESH = pl.DeviceIdType.MESH

D = 512
Q = 384
COLS = 4
NLIB = 16
NCHIP = 8
CAP = 192
BANK = 1024
MOL = 2048
CODE_ROWS = 16
ROW_BITS = 11
SLOT_MASK = 2047
OWNER_SHIFT = 22
INV_T = 1.0 / 0.07
PIECE = D // 2 // NLIB
LOG2E = 1.4426950408889634
NSLOTS = NLIB * CAP
PAIR = 2 * CAP


def iota(shape, dim):
    return lax.broadcasted_iota(I32, shape, dim)


def to_row(v):
    eye = iota((128, 128), 0) == iota((128, 128), 1)
    return jnp.concatenate(
        [
            jnp.sum(jnp.where(eye, v[lo : lo + 128], 0.0), axis=0, keepdims=True)
            for lo in range(0, v.shape[0], 128)
        ],
        axis=1,
    )


def to_col(v):
    eye = iota((128, 128), 0) == iota((128, 128), 1)
    return jnp.concatenate(
        [
            jnp.sum(jnp.where(eye, v[:, lo : lo + 128], 0.0), axis=1, keepdims=True)
            for lo in range(0, v.shape[1], 128)
        ],
        axis=0,
    )


def onehot(mask):
    return jnp.where(mask, 1.0, 0.0).astype(BF16)


def dot(a, b):
    return jnp.dot(a, b, preferred_element_type=F32)


def dot_nt(a, b):
    return lax.dot_general(a, b, (((1,), (1,)), ((), ())), preferred_element_type=F32)


def kernel(
    ndp,
    spec_hbm,
    w_hbm,
    bank_hbm,
    mol_hbm,
    code_ref,
    gw_out,
    gm_out,
    loss_out,
    spv,
    gat,
    wv,
    wt,
    bankv,
    bankt,
    molv,
    molt,
    codes,
    posr,
    valr,
    pkt,
    mrow,
    qs,
    unit,
    acc,
    qrow,
    scol,
    stats,
    lse,
    dub,
    gwb,
    rsb,
    dpb,
    dlb,
    ggb,
    loc_sem,
    ids_send,
    ids_recv,
    ag_send,
    ag_recv,
    sb_send,
    sb_recv,
    st_send,
    st_recv,
    rs_send,
    rs_recv,
    dp_send,
    dp_recv,
    dl_send,
    dl_recv,
    gg_send,
    gg_recv,
    out_sem,
):
    dp = lax.axis_index("dp")
    me = lax.axis_index("lib")
    core = lax.rem(me, 2)
    chip = me // 2
    y = chip // 4
    x = lax.rem(chip, 4)

    def chip_at(dy, dx):
        return lax.rem(y + dy, 2) * 4 + lax.rem(x + dx, 4)

    def peer(j):
        return lax.rem(me + j, NLIB)

    def dpeer(j):
        return lax.rem(dp + j, ndp)

    loads = [
        pltpu.make_async_copy(spec_hbm, spv, loc_sem.at[0]),
        pltpu.make_async_copy(w_hbm, wv, loc_sem.at[1]),
        pltpu.make_async_copy(bank_hbm, bankv, loc_sem.at[2]),
        pltpu.make_async_copy(mol_hbm, molv, loc_sem.at[3]),
    ]
    for load in loads:
        load.start()

    barrier = pltpu.get_barrier_semaphore()

    def greet(j, carry):
        pl.semaphore_signal(barrier, inc=1, device_id={"lib": peer(j)}, device_id_type=MESH)
        return carry

    lax.fori_loop(1, NLIB, greet, 0)

    def greet_dp(j, carry):
        pl.semaphore_signal(barrier, inc=1, device_id={"dp": dpeer(j)}, device_id_type=MESH)
        return carry

    lax.fori_loop(1, ndp, greet_dp, 0)
    codes[me] = jnp.concatenate(
        [code_ref[...], jnp.full((CODE_ROWS - Q * COLS // 128, 128), -1, I32)], axis=0
    )
    loads[0].wait()
    gat[chip, :, pl.ds(pl.multiple_of(core * Q, 128), Q)] = spv[...].T
    pl.semaphore_wait(barrier, NLIB - 1 + ndp - 1)

    def ids_copy(j):
        return pltpu.make_async_remote_copy(
            src_ref=codes.at[me],
            dst_ref=codes.at[me],
            send_sem=ids_send.at[j],
            recv_sem=ids_recv.at[me],
            device_id={"lib": peer(j)},
            device_id_type=MESH,
        )

    def ids_from(j):
        s = peer(j)
        return pltpu.make_async_remote_copy(
            src_ref=codes.at[s],
            dst_ref=codes.at[s],
            send_sem=ids_send.at[j],
            recv_sem=ids_recv.at[s],
            device_id={"lib": s},
            device_id_type=MESH,
        )

    lax.fori_loop(1, NLIB, lambda j, c: (ids_copy(j).start(), c)[1], 0)

    def piece(ch, cr, lo, n):
        return gat.at[ch, pl.ds(lo, n), pl.ds(pl.multiple_of(cr * Q, 128), Q)]

    HALF = D // 2
    right = {"lib": chip_at(0, 1) * 2 + core}
    left = {"lib": chip_at(0, 3) * 2 + core}
    across = {"lib": chip_at(1, 0) * 2 + core}
    sibling = {"lib": chip * 2 + 1 - core}

    def ag(idx, dy, dx, lo, n, to):
        ref = piece(chip_at(dy, dx), core, lo, n)
        return pltpu.make_async_remote_copy(
            src_ref=ref, dst_ref=ref, send_sem=ag_send.at[idx], recv_sem=ag_recv.at[idx],
            device_id=to, device_id_type=MESH,
        )

    ag_out = [
        ag(0, 0, 0, 0, D, right),
        ag(1, 0, 0, 0, D, left),
        ag(2, 0, 0, 0, D, across),
        ag(3, 0, 3, 0, HALF, right),
        ag(4, 0, 1, HALF, HALF, left),
        ag(5, 1, 0, 0, D, right),
        ag(6, 1, 0, 0, D, left),
        ag(7, 0, 2, 0, HALF, across),
        ag(8, 0, 2, HALF, HALF, across),
    ]
    arriving = [
        (0, 3, 0, D),
        (0, 1, 0, D),
        (1, 0, 0, D),
        (0, 2, 0, HALF),
        (0, 2, HALF, HALF),
        (1, 3, 0, D),
        (1, 1, 0, D),
        (1, 2, 0, HALF),
        (1, 2, HALF, HALF),
    ]
    ag_in = [ag(k, dy, dx, lo, n, right) for k, (dy, dx, lo, n) in enumerate(arriving)]

    def sb(idx, dy, dx, lo, n, cr):
        ref = piece(chip_at(dy, dx), cr, lo, n)
        return pltpu.make_async_remote_copy(
            src_ref=ref, dst_ref=ref, send_sem=sb_send.at[idx], recv_sem=sb_recv.at[idx],
            device_id=sibling, device_id_type=MESH,
        )

    sb_list = arriving + [(0, 0, 0, D)]
    sb_out = [sb(k, dy, dx, lo, n, core) for k, (dy, dx, lo, n) in enumerate(sb_list)]
    sb_in = [sb(k, dy, dx, lo, n, 1 - core) for k, (dy, dx, lo, n) in enumerate(sb_list)]

    for k in (0, 1, 2):
        ag_out[k].start()
    sb_out[9].start()
    for load in loads[1:]:
        load.wait()
    wt[...] = wv[...].T
    bankt[...] = bankv[...].T
    sb_in[9].wait_recv()

    def compaction():
        lax.fori_loop(1, NLIB, lambda j, c: (ids_from(j).wait_recv(), c)[1], 0)
        n = NLIB * CODE_ROWS
        code = codes[...].reshape(n, 128)
        mine = (code >> OWNER_SHIFT) == me
        ones = onehot(mine)
        before = onehot(iota((128, 128), 0) < iota((128, 128), 1))
        inside = dot(ones, before)
        totals = dot(ones, jnp.ones((128, 128), BF16)).astype(BF16)
        ri, ci = iota((n, n), 0), iota((n, n), 1)
        ahead = onehot((ri // CODE_ROWS == ci // CODE_ROWS) & (ci < ri))
        pos = inside + dot(ahead, totals)
        low = (code & (2**OWNER_SHIFT - 1)) + 1
        posr[...] = jnp.where(mine, pos, -1.0).reshape(NLIB, CODE_ROWS, 128)
        valr[...] = jnp.where(mine, low.astype(F32), 0.0).reshape(NLIB, CODE_ROWS, 128)

        def one(i, carry):
            place = iota((CAP, 128), 0).astype(F32)
            both = []
            for c in (0, 1):
                s = 2 * i + c
                p_all, v_all = posr[s], valr[s]
                total = jnp.zeros((CAP, 128), F32)
                for j in range(Q * COLS // 128):
                    total += jnp.where(p_all[j : j + 1] == place, v_all[j : j + 1], 0.0)
                both.append(jnp.sum(total, axis=1, keepdims=True))
            packed = jnp.concatenate(both, axis=0)
            scol[i, :, 0:1] = packed
            pkt[0:1, pl.ds(pl.multiple_of(i * PAIR, 128), PAIR)] = to_row(packed)
            return carry

        lax.fori_loop(0, NCHIP, one, 0)
        molt[...] = molv[...].T

        def fetch(b, carry):
            lanes = pl.ds(pl.multiple_of(b * 768, 128), 768)
            row = (pkt[0:1, lanes].astype(I32) - 1) >> ROW_BITS
            pick = onehot(row == iota((MOL, 768), 0))
            mrow[:, lanes] = dot(molt[...], pick).astype(BF16)
            return carry

        lax.fori_loop(0, 2, fetch, 0)
        for k in (0, 1, 2):
            ag_in[k].wait_recv()
        for k in (3, 4, 5, 6):
            ag_out[k].start()
        for k in (0, 1, 2):
            sb_out[k].start()
        lax.fori_loop(2, NSLOTS // 768, fetch, 0)

    def bank_unit(ch):
        u = dot(wt[...], gat[ch])
        rn = lax.rsqrt(jnp.sum(u * u, axis=0, keepdims=True) + 1e-6)
        u = u * rn
        unit[ch] = u
        qrow[ch, 0:1, :] = rn
        s = dot(bankv[...], u.astype(BF16))
        m = jnp.max(s, axis=0, keepdims=True)
        e = jnp.exp2((s - m) * (INV_T * LOG2E))
        qrow[ch, 1:2, :] = m * INV_T
        qrow[ch, 2:3, :] = jnp.sum(e, axis=0, keepdims=True)
        acc[ch] = dot(bankt[...], e.astype(BF16))

    def st_copy(lo, n, j):
        ref = stats.at[me, pl.ds(lo, n)]
        return pltpu.make_async_remote_copy(
            src_ref=ref, dst_ref=ref,
            send_sem=st_send.at[j], recv_sem=st_recv.at[me],
            device_id={"lib": peer(j)}, device_id_type=MESH,
        )

    def st_all(j, s):
        return pltpu.make_async_remote_copy(
            src_ref=stats.at[s], dst_ref=stats.at[s],
            send_sem=st_send.at[j], recv_sem=st_recv.at[s],
            device_id={"lib": peer(j)}, device_id_type=MESH,
        )

    def pair_lanes(i):
        return pl.ds(pl.multiple_of(i * PAIR, 128), PAIR)

    def slot_rows(i):
        t = pkt[0:1, pair_lanes(i)].astype(I32) - 1
        second = jnp.where(iota((1, PAIR), 1) >= CAP, Q, 0)
        q = jnp.where(t < 0, -1, ((t & SLOT_MASK) >> 2) + second)
        return t >= 0, (t >= 0) & ((t & 3) == 0), onehot(q == iota((2 * Q, PAIR), 0))

    def cand_unit(t_order, i):
        lanes = pair_lanes(i)
        _, first, pick = slot_rows(i)
        q_slot = dot(unit[i].astype(BF16), pick)
        qs[:, lanes] = q_slot.astype(BF16)
        cs = jnp.sum(q_slot * mrow[:, lanes].astype(F32), axis=0, keepdims=True) * INV_T
        pkt[1:2, lanes] = cs
        part = jnp.sum(jnp.where(first, cs, 0.0), axis=1, keepdims=True)
        cs_col = to_col(cs)
        for c in (0, 1):
            t = scol[i, c * CAP : (c + 1) * CAP, 0:1].astype(I32) - 1
            q = (t & SLOT_MASK) >> 2
            chosen = jnp.where(q == iota((CAP, Q), 1), cs_col[c * CAP : (c + 1) * CAP], -1e30)
            mb = qrow[i, 1:2, c * Q : (c + 1) * Q]
            lb = qrow[i, 2:3, c * Q : (c + 1) * Q]
            top = jnp.maximum(mb, jnp.max(chosen, axis=0, keepdims=True))
            total = lb * jnp.exp(mb - top) + jnp.sum(jnp.exp(chosen - top), axis=0, keepdims=True)
            out = top + jnp.log(total)
            for k in range(3):
                stats[me, t_order, 3 * c + k : 3 * c + k + 1, :] = out[:, 128 * k : 128 * (k + 1)]
        stats[me, t_order, 6:8, :] = jnp.broadcast_to(part, (2, 128))

    def send_stats(lo, n):
        lax.fori_loop(1, NLIB, lambda j, k: (st_copy(lo, n, j).start(), k)[1], 0)

    def order(t):
        dy = jnp.where((t == 3) | (t >= 5), 1, 0)
        dx = jnp.where(
            (t == 1) | (t == 5), 1, jnp.where((t == 2) | (t == 6), 3, jnp.where((t == 4) | (t == 7), 2, 0))
        )
        return chip_at(dy, dx)

    bank_unit(chip)
    compaction()

    def step(t, carry):
        @pl.when(t == 1)
        def _():
            for k in (1, 0, 2):
                sb_in[k].wait_recv()

        @pl.when(t == 3)
        def _():
            for k in (3, 4):
                ag_in[k].wait_recv()
            for k in (7, 8):
                ag_out[k].start()
            for k in (3, 4):
                sb_out[k].start()

        @pl.when(t == 4)
        def _():
            for k in (3, 4):
                sb_in[k].wait_recv()
            for k in (5, 6):
                ag_in[k].wait_recv()
            for k in (5, 6):
                sb_out[k].start()

        @pl.when(t == 5)
        def _():
            for k in (5, 6):
                sb_in[k].wait_recv()

        @pl.when(t == 6)
        def _():
            for k in (7, 8):
                ag_in[k].wait_recv()
            for k in (7, 8):
                sb_out[k].start()

        @pl.when(t == 7)
        def _():
            for k in (7, 8):
                sb_in[k].wait_recv()

        last = order(t - 1)
        cand_unit(t - 1, last)
        bank_unit(order(t))
        pl.when(t == 4)(lambda: send_stats(0, 4))
        pl.when(t == 7)(lambda: send_stats(4, 3))
        return carry

    lax.fori_loop(1, NCHIP, step, 0)
    cand_unit(NCHIP - 1, chip_at(1, 2))
    send_stats(NCHIP - 1, 1)

    lax.fori_loop(1, NLIB, lambda j, k: (st_all(j, peer(j)).wait_recv(), k)[1], 0)

    place = {(0, 0): 0, (0, 1): 1, (0, 3): 2, (1, 0): 3, (0, 2): 4, (1, 1): 5, (1, 3): 6, (1, 2): 7}
    values, firsts = [], []
    for i in range(NCHIP):
        parts = []
        for s in range(NLIB):
            dy, dx = (i // 4 + s // 8) % 2, (i % 4 - s // 2 % 4) % 4
            parts.append(stats[s, place[dy, dx]])
        top = parts[0]
        for part in parts[1:]:
            top = jnp.maximum(top, part)
        total = jnp.exp(parts[0] - top)
        first_score = parts[0]
        for part in parts[1:]:
            total += jnp.exp(part - top)
            first_score += part
        one_value = top + jnp.log(total)
        lse[i] = one_value
        values.append(one_value)
        firsts.append(first_score)
    value = jnp.stack(values)
    first_scores = jnp.stack(firsts)
    in_row = iota((NCHIP, 8, 128), 1)
    lane0 = iota((NCHIP, 8, 128), 2) == 0
    terms = jnp.where(in_row < 6, value, jnp.where((in_row == 6) & lane0, -first_scores, 0.0))
    terms = jnp.sum(terms, axis=0)
    group_loss = jnp.sum(jnp.sum(terms, axis=1, keepdims=True), axis=0, keepdims=True)
    dlb[dp] = jnp.broadcast_to(group_loss, (8, 128))

    def dl_copy(j, s, to):
        return pltpu.make_async_remote_copy(
            src_ref=dlb.at[s], dst_ref=dlb.at[s], send_sem=dl_send.at[j], recv_sem=dl_recv.at[s],
            device_id={"dp": to}, device_id_type=MESH,
        )


    def grad_unit(i, carry):
        lanes = pair_lanes(i)
        lse_row = jnp.concatenate([lse[i, k : k + 1, :] for k in range(6)], axis=1)
        valid, first, pick = slot_rows(i)
        high = lse_row.astype(BF16).astype(F32)
        middle = (lse_row - high).astype(BF16).astype(F32)
        low = lse_row - high - middle
        thirds = jnp.concatenate([high, middle, low, jnp.zeros((5, 2 * Q), F32)], axis=0)
        thirds = dot(thirds.astype(BF16), pick)
        lse_slot = thirds[0:1] + thirds[1:2] + thirds[2:3]
        coef = jnp.where(
            valid, jnp.exp(pkt[1:2, lanes] - lse_slot) - jnp.where(first, 1.0, 0.0), 0.0
        )
        pkt[2:3, lanes] = coef * INV_T
        weighted = (mrow[:, lanes].astype(F32) * coef).astype(BF16)
        scale = jnp.exp(qrow[i, 1:2, :] - lse_row)
        dq = acc[i] * scale + dot_nt(weighted, pick)
        u = unit[i]
        along = jnp.sum(u * dq, axis=0, keepdims=True)
        du = (dq - u * along) * (qrow[i, 0:1, :] * INV_T)
        dub[i] = du.astype(BF16)
        return carry

    lax.fori_loop(0, NCHIP, grad_unit, 0)

    def rs_copy(h, j, src, dst, to):
        return pltpu.make_async_remote_copy(
            src_ref=gwb.at[h, src], dst_ref=rsb.at[h, dst],
            send_sem=rs_send.at[h, j], recv_sem=rs_recv.at[h, dst],
            device_id={"lib": to}, device_id_type=MESH,
        )

    def dp_copy(h, j, s, to):
        return pltpu.make_async_remote_copy(
            src_ref=dpb.at[h, s], dst_ref=dpb.at[h, s],
            send_sem=dp_send.at[h, j], recv_sem=dp_recv.at[h, s],
            device_id={"dp": to}, device_id_type=MESH,
        )

    def gg_copy(h, j, s, to):
        return pltpu.make_async_remote_copy(
            src_ref=ggb.at[h, s], dst_ref=ggb.at[h, s],
            send_sem=gg_send.at[h, j], recv_sem=gg_recv.at[h, s],
            device_id={"lib": to}, device_id_type=MESH,
        )

    def rs_begin(h):
        rows = slice(h * (D // 2), (h + 1) * (D // 2))
        half = dot_nt(gat[0, rows, :], dub[0])
        for i in range(1, NCHIP):
            half += dot_nt(gat[i, rows, :], dub[i])
        gwb[h] = half.astype(BF16).reshape(NLIB, PIECE, D)
        lax.fori_loop(1, NLIB, lambda j, k: (rs_copy(h, j, peer(j), me, peer(j)).start(), k)[1], 0)
        rsb[h, me] = gwb[h, me]

    def dp_begin(h):
        lax.fori_loop(1, NLIB, lambda j, k: (rs_copy(h, j, me, peer(j), peer(j)).wait_recv(), k)[1], 0)
        part = rsb[h, 0].astype(F32)
        for s in range(1, NLIB):
            part += rsb[h, s].astype(F32)
        dpb[h, dp] = part.astype(BF16)
        lax.fori_loop(1, ndp, lambda j, k: (dp_copy(h, j, dp, dpeer(j)).start(), k)[1], 0)

    def gg_begin(h):
        lax.fori_loop(1, ndp, lambda j, k: (dp_copy(h, j, dpeer(j), dpeer(j)).wait_recv(), k)[1], 0)
        part = dpb[h, 0].astype(F32)
        for s in range(1, ndp):
            part += dpb[h, s].astype(F32)
        ggb[h, me] = part.astype(BF16)
        lax.fori_loop(1, NLIB, lambda j, k: (gg_copy(h, j, me, peer(j)).start(), k)[1], 0)

    def gg_end(h):
        lax.fori_loop(1, NLIB, lambda j, k: (gg_copy(h, j, peer(j), peer(j)).wait_recv(), k)[1], 0)

    rs_begin(0)
    rs_begin(1)
    lax.fori_loop(1, ndp, lambda j, k: (dl_copy(j, dp, dpeer(j)).start(), k)[1], 0)

    def out_copy(r):
        return pltpu.make_async_copy(
            acc.at[r, pl.ds(0, 256), pl.ds(0, D)],
            gm_out.at[pl.ds(pl.multiple_of(r * 256, 256), 256), :],
            out_sem.at[r],
        )

    def scatter(r, carry):
        row = (pkt[0:1, :].astype(I32) - 1) >> ROW_BITS
        pick = onehot(row == iota((256, NSLOTS), 0) + r * 256)
        acc[r, 0:256, 0:D] = dot_nt(pick, qs[...])
        out_copy(r).start()
        return carry

    def slot_gradients(i, carry):
        lanes = pair_lanes(i)
        qs[:, lanes] = (qs[:, lanes].astype(F32) * pkt[2:3, lanes]).astype(BF16)
        return carry

    lax.fori_loop(0, NCHIP, slot_gradients, 0)
    lax.fori_loop(0, 2, scatter, 0)
    dp_begin(0)
    lax.fori_loop(2, 4, scatter, 0)
    dp_begin(1)
    lax.fori_loop(4, 6, scatter, 0)
    gg_begin(0)
    lax.fori_loop(6, 8, scatter, 0)
    gg_begin(1)

    lax.fori_loop(1, ndp, lambda j, k: (dl_copy(j, dpeer(j), dpeer(j)).wait_recv(), k)[1], 0)
    whole = jnp.zeros((8, 128), F32)
    for s in range(ndp):
        whole += dlb[s]
    loss_out[...] = whole[0:1, 0:1] * (1.0 / (Q * NLIB * ndp))

    gg_end(0)
    gg_end(1)
    gw_out[...] = ggb[...].reshape(D, D)

    lax.fori_loop(1, NLIB, lambda j, k: (st_all(j, me).wait_send(), k)[1], 0)
    lax.fori_loop(0, 8, lambda r, k: (out_copy(r).wait(), k)[1], 0)
    lax.fori_loop(1, NLIB, lambda j, k: (ids_copy(j).wait_send(), k)[1], 0)
    for k in range(9):
        ag_out[k].wait_send()
    for k in range(10):
        sb_out[k].wait_send()
    for h in (0, 1):
        lax.fori_loop(1, NLIB, lambda j, k: (rs_copy(h, j, peer(j), me, peer(j)).wait_send(), k)[1], 0)
        lax.fori_loop(1, NLIB, lambda j, k: (gg_copy(h, j, me, peer(j)).wait_send(), k)[1], 0)
        lax.fori_loop(1, ndp, lambda j, k: (dp_copy(h, j, dp, dpeer(j)).wait_send(), k)[1], 0)
    lax.fori_loop(1, ndp, lambda j, k: (dl_copy(j, dp, dpeer(j)).wait_send(), k)[1], 0)


def per_device(ndp, spectra, w_proj, fixed_library_matrix, mol_rows, cand_ids, iso_count):
    owner = cand_ids // MOL % NLIB
    row = cand_ids % MOL
    slot = lax.broadcasted_iota(I32, (Q, COLS), 0) * COLS + lax.broadcasted_iota(I32, (Q, COLS), 1)
    live = lax.broadcasted_iota(I32, (Q, COLS), 1) <= iso_count[:, None]
    code = jnp.where(live, (owner << OWNER_SHIFT) | (row << ROW_BITS) | slot, -1)
    code = code.reshape(Q * COLS // 128, 128)
    vmem = pl.BlockSpec(memory_space=pltpu.VMEM)
    hbm = pl.BlockSpec(memory_space=pl.ANY)
    dma = pltpu.SemaphoreType.DMA
    gw, gm, loss = pl.pallas_call(
        functools.partial(kernel, ndp),
        out_shape=(
            jax.ShapeDtypeStruct((D, D), BF16),
            jax.ShapeDtypeStruct((MOL, D), F32),
            jax.ShapeDtypeStruct((1, 1), F32),
        ),
        in_specs=[hbm, hbm, hbm, hbm, vmem],
        out_specs=(vmem, hbm, vmem),
        scratch_shapes=[
            pltpu.VMEM((Q, D), BF16),
            pltpu.VMEM((NCHIP, D, 2 * Q), BF16),
            pltpu.VMEM((D, D), BF16),
            pltpu.VMEM((D, D), BF16),
            pltpu.VMEM((BANK, D), BF16),
            pltpu.VMEM((D, BANK), BF16),
            pltpu.VMEM((MOL, D), BF16),
            pltpu.VMEM((D, MOL), BF16),
            pltpu.VMEM((NLIB, CODE_ROWS, 128), I32),
            pltpu.VMEM((NLIB, CODE_ROWS, 128), F32),
            pltpu.VMEM((NLIB, CODE_ROWS, 128), F32),
            pltpu.VMEM((8, NSLOTS), F32),
            pltpu.VMEM((D, NSLOTS), BF16),
            pltpu.VMEM((D, NSLOTS), BF16),
            pltpu.VMEM((NCHIP, D, 2 * Q), F32),
            pltpu.VMEM((NCHIP, D, 2 * Q), F32),
            pltpu.VMEM((NCHIP, 8, 2 * Q), F32),
            pltpu.VMEM((NCHIP, PAIR, 128), F32),
            pltpu.VMEM((NLIB, NCHIP, 8, 128), F32),
            pltpu.VMEM((NCHIP, 8, 128), F32),
            pltpu.VMEM((NCHIP, D, 2 * Q), BF16),
            pltpu.VMEM((2, NLIB, PIECE, D), BF16),
            pltpu.VMEM((2, NLIB, PIECE, D), BF16),
            pltpu.VMEM((2, ndp, PIECE, D), BF16),
            pltpu.VMEM((ndp, 8, 128), F32),
            pltpu.VMEM((2, NLIB, PIECE, D), BF16),
            dma((4,)),
            dma((NLIB,)),
            dma((NLIB,)),
            dma((9,)),
            dma((9,)),
            dma((10,)),
            dma((10,)),
            dma((NLIB,)),
            dma((NLIB,)),
            dma((2, NLIB)),
            dma((2, NLIB)),
            dma((2, ndp)),
            dma((2, ndp)),
            dma((ndp,)),
            dma((ndp,)),
            dma((2, NLIB)),
            dma((2, NLIB)),
            dma((8,)),
        ],
        compiler_params=pltpu.CompilerParams(
            collective_id=0, has_side_effects=True, vmem_limit_bytes=62 * 1024 * 1024
        ),
    )(spectra, w_proj, fixed_library_matrix, mol_rows, code)
    return gw.astype(F32), gm, loss.reshape(())


def solution(mesh):
    placed = (
        P(("dp", "lib"), None),
        P(),
        P("lib", None),
        P(("dp", "lib"), None),
        P(("dp", "lib"), None),
        P(("dp", "lib")),
    )
    return jax.shard_map(
        functools.partial(per_device, mesh.shape["dp"]),
        mesh=mesh,
        in_specs=placed,
        out_specs=(P(), P(("dp", "lib"), None), P()),
        check_vma=False,
    )
```

```python
import functools

import jax
import jax.numpy as jnp
from jax import lax
from jax.experimental import pallas as pl
from jax.experimental.pallas import tpu as pltpu
from jax.sharding import PartitionSpec as P

F32 = jnp.float32
BF16 = jnp.bfloat16
I32 = jnp.int32
MESH = pl.DeviceIdType.MESH

D = 512
Q = 384
COLS = 4
NLIB = 16
NCHIP = 8
CAP = 192
BANK = 1024
MOL = 2048
CODE_ROWS = 16
ROW_BITS = 11
SLOT_MASK = 2047
OWNER_SHIFT = 22
INV_T = 1.0 / 0.07
PIECE = D // 2 // NLIB
LOG2E = 1.4426950408889634
NSLOTS = NLIB * CAP
PAIR = 2 * CAP


def iota(shape, dim):
    return lax.broadcasted_iota(I32, shape, dim)


def to_row(v):
    eye = iota((128, 128), 0) == iota((128, 128), 1)
    return jnp.concatenate(
        [
            jnp.sum(jnp.where(eye, v[lo : lo + 128], 0.0), axis=0, keepdims=True)
            for lo in range(0, v.shape[0], 128)
        ],
        axis=1,
    )


def to_col(v):
    eye = iota((128, 128), 0) == iota((128, 128), 1)
    return jnp.concatenate(
        [
            jnp.sum(jnp.where(eye, v[:, lo : lo + 128], 0.0), axis=1, keepdims=True)
            for lo in range(0, v.shape[1], 128)
        ],
        axis=0,
    )


def onehot(mask):
    return jnp.where(mask, 1.0, 0.0).astype(BF16)


def dot(a, b):
    return jnp.dot(a, b, preferred_element_type=F32)


def dot_nt(a, b):
    return lax.dot_general(a, b, (((1,), (1,)), ((), ())), preferred_element_type=F32)


def kernel(
    ndp,
    spec_hbm,
    w_hbm,
    bank_hbm,
    mol_hbm,
    ids_ref,
    iso_ref,
    gw_out,
    gm_out,
    loss_out,
    spv,
    gat,
    wv,
    wt,
    bankv,
    bankt,
    molv,
    molt,
    codes,
    posr,
    valr,
    pkt,
    mrow,
    qs,
    unit,
    acc,
    qrow,
    scol,
    stats,
    lse,
    dub,
    gwb,
    rsb,
    dpb,
    dlb,
    ggb,
    loc_sem,
    ids_send,
    ids_recv,
    ag_send,
    ag_recv,
    sb_send,
    sb_recv,
    st_send,
    st_recv,
    rs_send,
    rs_recv,
    dp_send,
    dp_recv,
    dl_send,
    dl_recv,
    gg_send,
    gg_recv,
    out_sem,
):
    dp = lax.axis_index("dp")
    me = lax.axis_index("lib")
    core = lax.rem(me, 2)
    chip = me // 2
    y = chip // 4
    x = lax.rem(chip, 4)

    def chip_at(dy, dx):
        return lax.rem(y + dy, 2) * 4 + lax.rem(x + dx, 4)

    def peer(j):
        return lax.rem(me + j, NLIB)

    def dpeer(j):
        return lax.rem(dp + j, ndp)

    loads = [
        pltpu.make_async_copy(spec_hbm, spv, loc_sem.at[0]),
        pltpu.make_async_copy(w_hbm, wv, loc_sem.at[1]),
        pltpu.make_async_copy(bank_hbm, bankv, loc_sem.at[2]),
        pltpu.make_async_copy(mol_hbm, molv, loc_sem.at[3]),
    ]
    for load in loads:
        load.start()

    barrier = pltpu.get_barrier_semaphore()

    def greet(j, carry):
        pl.semaphore_signal(barrier, inc=1, device_id={"lib": peer(j)}, device_id_type=MESH)
        return carry

    lax.fori_loop(1, NLIB, greet, 0)

    def greet_dp(j, carry):
        pl.semaphore_signal(barrier, inc=1, device_id={"dp": dpeer(j)}, device_id_type=MESH)
        return carry

    lax.fori_loop(1, ndp, greet_dp, 0)
    ids = ids_ref[...]
    column = iota((COLS, Q), 0)
    slot = iota((COLS, Q), 1) * COLS + column
    owner = (ids >> ROW_BITS) & (NLIB - 1)
    code = (owner << OWNER_SHIFT) | ((ids & (MOL - 1)) << ROW_BITS) | slot
    code = jnp.where(column <= iso_ref[...], code, -1)
    for k in range(Q // 128):
        codes[me, COLS * k : COLS * (k + 1), :] = code[:, 128 * k : 128 * (k + 1)]
    codes[me, Q * COLS // 128 : CODE_ROWS, :] = jnp.full((CODE_ROWS - Q * COLS // 128, 128), -1, I32)
    loads[0].wait()
    gat[chip, :, pl.ds(pl.multiple_of(core * Q, 128), Q)] = spv[...].T
    pl.semaphore_wait(barrier, NLIB - 1 + ndp - 1)

    def ids_copy(j):
        return pltpu.make_async_remote_copy(
            src_ref=codes.at[me],
            dst_ref=codes.at[me],
            send_sem=ids_send.at[j],
            recv_sem=ids_recv.at[me],
            device_id={"lib": peer(j)},
            device_id_type=MESH,
        )

    def ids_from(j):
        s = peer(j)
        return pltpu.make_async_remote_copy(
            src_ref=codes.at[s],
            dst_ref=codes.at[s],
            send_sem=ids_send.at[j],
            recv_sem=ids_recv.at[s],
            device_id={"lib": s},
            device_id_type=MESH,
        )

    lax.fori_loop(1, NLIB, lambda j, c: (ids_copy(j).start(), c)[1], 0)

    def piece(ch, cr, lo, n):
        return gat.at[ch, pl.ds(lo, n), pl.ds(pl.multiple_of(cr * Q, 128), Q)]

    HALF = D // 2
    right = {"lib": chip_at(0, 1) * 2 + core}
    left = {"lib": chip_at(0, 3) * 2 + core}
    across = {"lib": chip_at(1, 0) * 2 + core}
    sibling = {"lib": chip * 2 + 1 - core}

    def ag(idx, dy, dx, lo, n, to):
        ref = piece(chip_at(dy, dx), core, lo, n)
        return pltpu.make_async_remote_copy(
            src_ref=ref, dst_ref=ref, send_sem=ag_send.at[idx], recv_sem=ag_recv.at[idx],
            device_id=to, device_id_type=MESH,
        )

    ag_out = [
        ag(0, 0, 0, 0, D, right),
        ag(1, 0, 0, 0, D, left),
        ag(2, 0, 0, 0, D, across),
        ag(3, 0, 3, 0, HALF, right),
        ag(4, 0, 1, HALF, HALF, left),
        ag(5, 1, 0, 0, D, right),
        ag(6, 1, 0, 0, D, left),
        ag(7, 0, 2, 0, HALF, across),
        ag(8, 0, 2, HALF, HALF, across),
    ]
    arriving = [
        (0, 3, 0, D),
        (0, 1, 0, D),
        (1, 0, 0, D),
        (0, 2, 0, HALF),
        (0, 2, HALF, HALF),
        (1, 3, 0, D),
        (1, 1, 0, D),
        (1, 2, 0, HALF),
        (1, 2, HALF, HALF),
    ]
    ag_in = [ag(k, dy, dx, lo, n, right) for k, (dy, dx, lo, n) in enumerate(arriving)]

    def sb(idx, dy, dx, lo, n, cr):
        ref = piece(chip_at(dy, dx), cr, lo, n)
        return pltpu.make_async_remote_copy(
            src_ref=ref, dst_ref=ref, send_sem=sb_send.at[idx], recv_sem=sb_recv.at[idx],
            device_id=sibling, device_id_type=MESH,
        )

    sb_list = arriving + [(0, 0, 0, D)]
    sb_out = [sb(k, dy, dx, lo, n, core) for k, (dy, dx, lo, n) in enumerate(sb_list)]
    sb_in = [sb(k, dy, dx, lo, n, 1 - core) for k, (dy, dx, lo, n) in enumerate(sb_list)]

    for k in (0, 1, 2):
        ag_out[k].start()
    sb_out[9].start()
    for load in loads[1:]:
        load.wait()
    wt[...] = wv[...].T
    bankt[...] = bankv[...].T
    sb_in[9].wait_recv()

    def compaction():
        lax.fori_loop(1, NLIB, lambda j, c: (ids_from(j).wait_recv(), c)[1], 0)
        n = NLIB * CODE_ROWS
        code = codes[...].reshape(n, 128)
        mine = (code >> OWNER_SHIFT) == me
        ones = onehot(mine)
        before = onehot(iota((128, 128), 0) < iota((128, 128), 1))
        inside = dot(ones, before)
        totals = dot(ones, jnp.ones((128, 128), BF16)).astype(BF16)
        ri, ci = iota((n, n), 0), iota((n, n), 1)
        ahead = onehot((ri // CODE_ROWS == ci // CODE_ROWS) & (ci < ri))
        pos = inside + dot(ahead, totals)
        low = (code & (2**OWNER_SHIFT - 1)) + 1
        posr[...] = jnp.where(mine, pos, -1.0).reshape(NLIB, CODE_ROWS, 128)
        valr[...] = jnp.where(mine, low.astype(F32), 0.0).reshape(NLIB, CODE_ROWS, 128)

        def one(i, carry):
            place = iota((CAP, 128), 0).astype(F32)
            both = []
            for c in (0, 1):
                s = 2 * i + c
                p_all, v_all = posr[s], valr[s]
                total = jnp.zeros((CAP, 128), F32)
                for j in range(Q * COLS // 128):
                    total += jnp.where(p_all[j : j + 1] == place, v_all[j : j + 1], 0.0)
                both.append(jnp.sum(total, axis=1, keepdims=True))
            packed = jnp.concatenate(both, axis=0)
            scol[i, :, 0:1] = packed
            pkt[0:1, pl.ds(pl.multiple_of(i * PAIR, 128), PAIR)] = to_row(packed)
            return carry

        lax.fori_loop(0, NCHIP, one, 0)
        molt[...] = molv[...].T

        def fetch(b, carry):
            lanes = pl.ds(pl.multiple_of(b * 768, 128), 768)
            row = (pkt[0:1, lanes].astype(I32) - 1) >> ROW_BITS
            pick = onehot(row == iota((MOL, 768), 0))
            mrow[:, lanes] = dot(molt[...], pick).astype(BF16)
            return carry

        lax.fori_loop(0, 2, fetch, 0)
        for k in (0, 1, 2):
            ag_in[k].wait_recv()
        for k in (3, 4, 5, 6):
            ag_out[k].start()
        for k in (0, 1, 2):
            sb_out[k].start()
        lax.fori_loop(2, NSLOTS // 768, fetch, 0)

    def bank_unit(ch, kept=None):
        u = dot(wt[...], gat[ch])
        rn = lax.rsqrt(jnp.sum(u * u, axis=0, keepdims=True) + 1e-6)
        u = u * rn
        unit[ch] = u
        qrow[ch, 0:1, :] = rn
        s = dot(bankv[...], u.astype(BF16))
        m = jnp.max(s, axis=0, keepdims=True)
        e = jnp.exp2((s - m) * (INV_T * LOG2E))
        qrow[ch, 1:2, :] = m * INV_T
        qrow[ch, 2:3, :] = jnp.sum(e, axis=0, keepdims=True)
        if kept is None:
            acc[ch] = dot(bankt[...], e.astype(BF16))
        else:
            dub[kept, :] = e.astype(BF16)

    def st_copy(lo, n, j):
        ref = stats.at[me, pl.ds(lo, n)]
        return pltpu.make_async_remote_copy(
            src_ref=ref, dst_ref=ref,
            send_sem=st_send.at[j], recv_sem=st_recv.at[me],
            device_id={"lib": peer(j)}, device_id_type=MESH,
        )

    def st_all(j, s):
        return pltpu.make_async_remote_copy(
            src_ref=stats.at[s], dst_ref=stats.at[s],
            send_sem=st_send.at[j], recv_sem=st_recv.at[s],
            device_id={"lib": peer(j)}, device_id_type=MESH,
        )

    def pair_lanes(i):
        return pl.ds(pl.multiple_of(i * PAIR, 128), PAIR)

    def slot_rows(i):
        t = pkt[0:1, pair_lanes(i)].astype(I32) - 1
        second = jnp.where(iota((1, PAIR), 1) >= CAP, Q, 0)
        q = jnp.where(t < 0, -1, ((t & SLOT_MASK) >> 2) + second)
        return t >= 0, (t >= 0) & ((t & 3) == 0), onehot(q == iota((2 * Q, PAIR), 0))

    def cand_unit(t_order, i):
        lanes = pair_lanes(i)
        _, first, pick = slot_rows(i)
        q_slot = dot(unit[i].astype(BF16), pick)
        qs[:, lanes] = q_slot.astype(BF16)
        cs = jnp.sum(q_slot * mrow[:, lanes].astype(F32), axis=0, keepdims=True) * INV_T
        pkt[1:2, lanes] = cs
        part = jnp.sum(jnp.where(first, cs, 0.0), axis=1, keepdims=True)
        cs_col = to_col(cs)
        for c in (0, 1):
            t = scol[i, c * CAP : (c + 1) * CAP, 0:1].astype(I32) - 1
            q = (t & SLOT_MASK) >> 2
            chosen = jnp.where(q == iota((CAP, Q), 1), cs_col[c * CAP : (c + 1) * CAP], -1e30)
            mb = qrow[i, 1:2, c * Q : (c + 1) * Q]
            lb = qrow[i, 2:3, c * Q : (c + 1) * Q]
            top = jnp.maximum(mb, jnp.max(chosen, axis=0, keepdims=True))
            total = lb * jnp.exp(mb - top) + jnp.sum(jnp.exp(chosen - top), axis=0, keepdims=True)
            out = top + jnp.log(total)
            for k in range(3):
                stats[me, t_order, 3 * c + k : 3 * c + k + 1, :] = out[:, 128 * k : 128 * (k + 1)]
        stats[me, t_order, 6:8, :] = jnp.broadcast_to(part, (2, 128))

    def send_stats(lo, n):
        lax.fori_loop(1, NLIB, lambda j, k: (st_copy(lo, n, j).start(), k)[1], 0)

    def order(t):
        dy = jnp.where((t == 3) | (t >= 5), 1, 0)
        dx = jnp.where(
            (t == 1) | (t == 5), 1, jnp.where((t == 2) | (t == 6), 3, jnp.where((t == 4) | (t == 7), 2, 0))
        )
        return chip_at(dy, dx)

    bank_unit(chip)
    compaction()

    def step(keep, t, carry):
        @pl.when(t == 1)
        def _():
            for k in (1, 0, 2):
                sb_in[k].wait_recv()

        @pl.when(t == 3)
        def _():
            for k in (3, 4):
                ag_in[k].wait_recv()
            for k in (7, 8):
                ag_out[k].start()
            for k in (3, 4):
                sb_out[k].start()

        @pl.when(t == 4)
        def _():
            for k in (3, 4):
                sb_in[k].wait_recv()
            for k in (5, 6):
                ag_in[k].wait_recv()
            for k in (5, 6):
                sb_out[k].start()

        @pl.when(t == 5)
        def _():
            for k in (5, 6):
                sb_in[k].wait_recv()

        @pl.when(t == 6)
        def _():
            for k in (7, 8):
                ag_in[k].wait_recv()
            for k in (7, 8):
                sb_out[k].start()

        @pl.when(t == 7)
        def _():
            for k in (7, 8):
                sb_in[k].wait_recv()

        cand_unit(t - 1, order(t - 1))
        bank_unit(order(t), kept_rows(t) if keep else None)
        return carry

    def kept_rows(t):
        return pl.ds(pl.multiple_of((t - 4) * BANK, BANK), BANK)

    lax.fori_loop(1, 4, functools.partial(step, False), 0)
    lax.fori_loop(4, 5, functools.partial(step, True), 0)
    send_stats(0, 4)
    lax.fori_loop(5, NCHIP, functools.partial(step, True), 0)
    send_stats(4, 3)
    cand_unit(NCHIP - 1, chip_at(1, 2))
    send_stats(NCHIP - 1, 1)

    def kept_sum(t, carry):
        acc[order(t)] = dot(bankt[...], dub[kept_rows(t), :])
        return carry

    lax.fori_loop(4, NCHIP, kept_sum, 0)

    lax.fori_loop(1, NLIB, lambda j, k: (st_all(j, peer(j)).wait_recv(), k)[1], 0)

    place = {(0, 0): 0, (0, 1): 1, (0, 3): 2, (1, 0): 3, (0, 2): 4, (1, 1): 5, (1, 3): 6, (1, 2): 7}
    values, firsts = [], []
    for i in range(NCHIP):
        parts = []
        for s in range(NLIB):
            dy, dx = (i // 4 + s // 8) % 2, (i % 4 - s // 2 % 4) % 4
            parts.append(stats[s, place[dy, dx]])
        top = parts[0]
        for part in parts[1:]:
            top = jnp.maximum(top, part)
        total = jnp.exp(parts[0] - top)
        first_score = parts[0]
        for part in parts[1:]:
            total += jnp.exp(part - top)
            first_score += part
        one_value = top + jnp.log(total)
        lse[i] = one_value
        values.append(one_value)
        firsts.append(first_score)
    value = jnp.stack(values)
    first_scores = jnp.stack(firsts)
    in_row = iota((NCHIP, 8, 128), 1)
    lane0 = iota((NCHIP, 8, 128), 2) == 0
    terms = jnp.where(in_row < 6, value, jnp.where((in_row == 6) & lane0, -first_scores, 0.0))
    terms = jnp.sum(terms, axis=0)
    group_loss = jnp.sum(jnp.sum(terms, axis=1, keepdims=True), axis=0, keepdims=True)
    dlb[dp] = jnp.broadcast_to(group_loss, (8, 128))

    def dl_copy(j, s, to):
        return pltpu.make_async_remote_copy(
            src_ref=dlb.at[s], dst_ref=dlb.at[s], send_sem=dl_send.at[j], recv_sem=dl_recv.at[s],
            device_id={"dp": to}, device_id_type=MESH,
        )


    def grad_unit(i, carry):
        lanes = pair_lanes(i)
        lse_row = jnp.concatenate([lse[i, k : k + 1, :] for k in range(6)], axis=1)
        valid, first, pick = slot_rows(i)
        high = lse_row.astype(BF16).astype(F32)
        middle = (lse_row - high).astype(BF16).astype(F32)
        low = lse_row - high - middle
        thirds = jnp.concatenate([high, middle, low, jnp.zeros((5, 2 * Q), F32)], axis=0)
        thirds = dot(thirds.astype(BF16), pick)
        lse_slot = thirds[0:1] + thirds[1:2] + thirds[2:3]
        coef = jnp.where(
            valid, jnp.exp(pkt[1:2, lanes] - lse_slot) - jnp.where(first, 1.0, 0.0), 0.0
        )
        pkt[2:3, lanes] = coef * INV_T
        weighted = (mrow[:, lanes].astype(F32) * coef).astype(BF16)
        scale = jnp.exp(qrow[i, 1:2, :] - lse_row)
        dq = acc[i] * scale + dot_nt(weighted, pick)
        u = unit[i]
        along = jnp.sum(u * dq, axis=0, keepdims=True)
        du = (dq - u * along) * (qrow[i, 0:1, :] * INV_T)
        dub[pl.ds(pl.multiple_of(i * D, D), D), :] = du.astype(BF16)
        return carry

    lax.fori_loop(0, NCHIP, grad_unit, 0)

    def rs_copy(h, j, src, dst, to):
        return pltpu.make_async_remote_copy(
            src_ref=gwb.at[h, src], dst_ref=rsb.at[h, dst],
            send_sem=rs_send.at[h, j], recv_sem=rs_recv.at[h, dst],
            device_id={"lib": to}, device_id_type=MESH,
        )

    def dp_copy(h, j, s, to):
        return pltpu.make_async_remote_copy(
            src_ref=dpb.at[h, s], dst_ref=dpb.at[h, s],
            send_sem=dp_send.at[h, j], recv_sem=dp_recv.at[h, s],
            device_id={"dp": to}, device_id_type=MESH,
        )

    def gg_copy(h, j, s, to):
        return pltpu.make_async_remote_copy(
            src_ref=ggb.at[h, s], dst_ref=ggb.at[h, s],
            send_sem=gg_send.at[h, j], recv_sem=gg_recv.at[h, s],
            device_id={"lib": to}, device_id_type=MESH,
        )

    def rs_begin(h):
        rows = slice(h * (D // 2), (h + 1) * (D // 2))
        half = dot_nt(gat[0, rows, :], dub[0:D, :])
        for i in range(1, NCHIP):
            half += dot_nt(gat[i, rows, :], dub[i * D : (i + 1) * D, :])
        gwb[h] = half.astype(BF16).reshape(NLIB, PIECE, D)
        lax.fori_loop(1, NLIB, lambda j, k: (rs_copy(h, j, peer(j), me, peer(j)).start(), k)[1], 0)
        rsb[h, me] = gwb[h, me]

    def dp_begin(h):
        lax.fori_loop(1, NLIB, lambda j, k: (rs_copy(h, j, me, peer(j), peer(j)).wait_recv(), k)[1], 0)
        part = rsb[h, 0].astype(F32)
        for s in range(1, NLIB):
            part += rsb[h, s].astype(F32)
        dpb[h, dp] = part.astype(BF16)
        lax.fori_loop(1, ndp, lambda j, k: (dp_copy(h, j, dp, dpeer(j)).start(), k)[1], 0)

    def gg_begin(h):
        lax.fori_loop(1, ndp, lambda j, k: (dp_copy(h, j, dpeer(j), dpeer(j)).wait_recv(), k)[1], 0)
        part = dpb[h, 0].astype(F32)
        for s in range(1, ndp):
            part += dpb[h, s].astype(F32)
        ggb[h, me] = part.astype(BF16)
        lax.fori_loop(1, NLIB, lambda j, k: (gg_copy(h, j, me, peer(j)).start(), k)[1], 0)

    def gg_end(h):
        lax.fori_loop(1, NLIB, lambda j, k: (gg_copy(h, j, peer(j), peer(j)).wait_recv(), k)[1], 0)

    rs_begin(0)
    rs_begin(1)
    lax.fori_loop(1, ndp, lambda j, k: (dl_copy(j, dp, dpeer(j)).start(), k)[1], 0)

    def out_copy(r):
        return pltpu.make_async_copy(
            acc.at[r, pl.ds(0, 256), pl.ds(0, D)],
            gm_out.at[pl.ds(pl.multiple_of(r * 256, 256), 256), :],
            out_sem.at[r],
        )

    def scatter(r, carry):
        row = (pkt[0:1, :].astype(I32) - 1) >> ROW_BITS
        pick = onehot(row == iota((256, NSLOTS), 0) + r * 256)
        acc[r, 0:256, 0:D] = dot_nt(pick, qs[...])
        out_copy(r).start()
        return carry

    def slot_gradients(i, carry):
        lanes = pair_lanes(i)
        qs[:, lanes] = (qs[:, lanes].astype(F32) * pkt[2:3, lanes]).astype(BF16)
        return carry

    lax.fori_loop(0, NCHIP, slot_gradients, 0)
    lax.fori_loop(0, 2, scatter, 0)
    dp_begin(0)
    lax.fori_loop(2, 4, scatter, 0)
    dp_begin(1)
    lax.fori_loop(4, 6, scatter, 0)
    gg_begin(0)
    lax.fori_loop(6, 8, scatter, 0)
    gg_begin(1)

    lax.fori_loop(1, ndp, lambda j, k: (dl_copy(j, dpeer(j), dpeer(j)).wait_recv(), k)[1], 0)
    whole = jnp.zeros((8, 128), F32)
    for s in range(ndp):
        whole += dlb[s]
    loss_out[...] = whole[0:1, 0:1] * (1.0 / (Q * NLIB * ndp))

    gg_end(0)
    gg_end(1)
    gw_out[...] = ggb[...].reshape(D, D)

    lax.fori_loop(1, NLIB, lambda j, k: (st_all(j, me).wait_send(), k)[1], 0)
    lax.fori_loop(0, 8, lambda r, k: (out_copy(r).wait(), k)[1], 0)
    lax.fori_loop(1, NLIB, lambda j, k: (ids_copy(j).wait_send(), k)[1], 0)
    for k in range(9):
        ag_out[k].wait_send()
    for k in range(10):
        sb_out[k].wait_send()
    for h in (0, 1):
        lax.fori_loop(1, NLIB, lambda j, k: (rs_copy(h, j, peer(j), me, peer(j)).wait_send(), k)[1], 0)
        lax.fori_loop(1, NLIB, lambda j, k: (gg_copy(h, j, me, peer(j)).wait_send(), k)[1], 0)
        lax.fori_loop(1, ndp, lambda j, k: (dp_copy(h, j, dp, dpeer(j)).wait_send(), k)[1], 0)
    lax.fori_loop(1, ndp, lambda j, k: (dl_copy(j, dp, dpeer(j)).wait_send(), k)[1], 0)


def per_device(ndp, spectra, w_proj, fixed_library_matrix, mol_rows, cand_ids, iso_count):
    vmem = pl.BlockSpec(memory_space=pltpu.VMEM)
    hbm = pl.BlockSpec(memory_space=pl.ANY)
    dma = pltpu.SemaphoreType.DMA
    gw, gm, loss = pl.pallas_call(
        functools.partial(kernel, ndp),
        out_shape=(
            jax.ShapeDtypeStruct((D, D), BF16),
            jax.ShapeDtypeStruct((MOL, D), F32),
            jax.ShapeDtypeStruct((1, 1), F32),
        ),
        in_specs=[hbm, hbm, hbm, hbm, vmem, vmem],
        out_specs=(vmem, hbm, vmem),
        scratch_shapes=[
            pltpu.VMEM((Q, D), BF16),
            pltpu.VMEM((NCHIP, D, 2 * Q), BF16),
            pltpu.VMEM((D, D), BF16),
            pltpu.VMEM((D, D), BF16),
            pltpu.VMEM((BANK, D), BF16),
            pltpu.VMEM((D, BANK), BF16),
            pltpu.VMEM((MOL, D), BF16),
            pltpu.VMEM((D, MOL), BF16),
            pltpu.VMEM((NLIB, CODE_ROWS, 128), I32),
            pltpu.VMEM((NLIB, CODE_ROWS, 128), F32),
            pltpu.VMEM((NLIB, CODE_ROWS, 128), F32),
            pltpu.VMEM((8, NSLOTS), F32),
            pltpu.VMEM((D, NSLOTS), BF16),
            pltpu.VMEM((D, NSLOTS), BF16),
            pltpu.VMEM((NCHIP, D, 2 * Q), F32),
            pltpu.VMEM((NCHIP, D, 2 * Q), F32),
            pltpu.VMEM((NCHIP, 8, 2 * Q), F32),
            pltpu.VMEM((NCHIP, PAIR, 128), F32),
            pltpu.VMEM((NLIB, NCHIP, 8, 128), F32),
            pltpu.VMEM((NCHIP, 8, 128), F32),
            pltpu.VMEM((NCHIP * D, 2 * Q), BF16),
            pltpu.VMEM((2, NLIB, PIECE, D), BF16),
            pltpu.VMEM((2, NLIB, PIECE, D), BF16),
            pltpu.VMEM((2, ndp, PIECE, D), BF16),
            pltpu.VMEM((ndp, 8, 128), F32),
            pltpu.VMEM((2, NLIB, PIECE, D), BF16),
            dma((4,)),
            dma((NLIB,)),
            dma((NLIB,)),
            dma((9,)),
            dma((9,)),
            dma((10,)),
            dma((10,)),
            dma((NLIB,)),
            dma((NLIB,)),
            dma((2, NLIB)),
            dma((2, NLIB)),
            dma((2, ndp)),
            dma((2, ndp)),
            dma((ndp,)),
            dma((ndp,)),
            dma((2, NLIB)),
            dma((2, NLIB)),
            dma((8,)),
        ],
        compiler_params=pltpu.CompilerParams(
            collective_id=0, has_side_effects=True, vmem_limit_bytes=62 * 1024 * 1024
        ),
    )(spectra, w_proj, fixed_library_matrix, mol_rows, cand_ids.T, iso_count.reshape(1, Q))
    return gw.astype(F32), gm, loss.reshape(())


def solution(mesh):
    placed = (
        P(("dp", "lib"), None),
        P(),
        P("lib", None),
        P(("dp", "lib"), None),
        P(("dp", "lib"), None),
        P(("dp", "lib")),
    )
    return jax.shard_map(
        functools.partial(per_device, mesh.shape["dp"]),
        mesh=mesh,
        in_specs=placed,
        out_specs=(P(), P(("dp", "lib"), None), P()),
        check_vma=False,
    )
```

```python
import functools

import jax
import jax.numpy as jnp
from jax import lax
from jax.experimental import pallas as pl
from jax.experimental.pallas import tpu as pltpu
from jax.sharding import PartitionSpec as P

F32 = jnp.float32
BF16 = jnp.bfloat16
I32 = jnp.int32
MESH = pl.DeviceIdType.MESH

D = 512
Q = 384
COLS = 4
NLIB = 16
NCHIP = 8
CAP = 192
BANK = 1024
MOL = 2048
CODE_ROWS = 16
ROW_BITS = 11
SLOT_MASK = 2047
OWNER_SHIFT = 22
INV_T = 1.0 / 0.07
PIECE = D // 2 // NLIB
LOG2E = 1.4426950408889634
NSLOTS = NLIB * CAP
PAIR = 2 * CAP


def iota(shape, dim):
    return lax.broadcasted_iota(I32, shape, dim)


def to_row(v):
    eye = iota((128, 128), 0) == iota((128, 128), 1)
    return jnp.concatenate(
        [
            jnp.sum(jnp.where(eye, v[lo : lo + 128], 0.0), axis=0, keepdims=True)
            for lo in range(0, v.shape[0], 128)
        ],
        axis=1,
    )


def to_col(v):
    eye = iota((128, 128), 0) == iota((128, 128), 1)
    return jnp.concatenate(
        [
            jnp.sum(jnp.where(eye, v[:, lo : lo + 128], 0.0), axis=1, keepdims=True)
            for lo in range(0, v.shape[1], 128)
        ],
        axis=0,
    )


def onehot(mask):
    return jnp.where(mask, 1.0, 0.0).astype(BF16)


def dot(a, b):
    return jnp.dot(a, b, preferred_element_type=F32)


def dot_nt(a, b):
    return lax.dot_general(a, b, (((1,), (1,)), ((), ())), preferred_element_type=F32)


def kernel(
    ndp,
    spec_hbm,
    w_hbm,
    bank_hbm,
    mol_hbm,
    ids_ref,
    iso_ref,
    gw_out,
    gm_out,
    loss_out,
    spv,
    gat,
    wv,
    wt,
    bankv,
    bankt,
    molv,
    molt,
    codes,
    posr,
    valr,
    pkt,
    mrow,
    qs,
    unit,
    acc,
    qrow,
    scol,
    stats,
    lse,
    dub,
    gwb,
    rsb,
    dpb,
    dlb,
    ggb,
    loc_sem,
    ids_send,
    ids_recv,
    ag_send,
    ag_recv,
    sb_send,
    sb_recv,
    st_send,
    st_recv,
    rs_send,
    rs_recv,
    dp_send,
    dp_recv,
    dl_send,
    dl_recv,
    gg_send,
    gg_recv,
    out_sem,
):
    dp = lax.axis_index("dp")
    me = lax.axis_index("lib")
    core = lax.rem(me, 2)
    chip = me // 2
    y = chip // 4
    x = lax.rem(chip, 4)

    def chip_at(dy, dx):
        return lax.rem(y + dy, 2) * 4 + lax.rem(x + dx, 4)

    def peer(j):
        return lax.rem(me + j, NLIB)

    def dpeer(j):
        return lax.rem(dp + j, ndp)

    loads = [
        pltpu.make_async_copy(spec_hbm, spv, loc_sem.at[0]),
        pltpu.make_async_copy(w_hbm, wv, loc_sem.at[1]),
        pltpu.make_async_copy(bank_hbm, bankv, loc_sem.at[2]),
        pltpu.make_async_copy(mol_hbm, molv, loc_sem.at[3]),
    ]
    for load in loads:
        load.start()

    barrier = pltpu.get_barrier_semaphore()

    def greet(j, carry):
        pl.semaphore_signal(barrier, inc=1, device_id={"lib": peer(j)}, device_id_type=MESH)
        return carry

    lax.fori_loop(1, NLIB, greet, 0)

    def greet_dp(j, carry):
        pl.semaphore_signal(barrier, inc=1, device_id={"dp": dpeer(j)}, device_id_type=MESH)
        return carry

    lax.fori_loop(1, ndp, greet_dp, 0)
    ids = ids_ref[...]
    column = iota((COLS, Q), 0)
    slot = iota((COLS, Q), 1) * COLS + column
    owner = (ids >> ROW_BITS) & (NLIB - 1)
    code = (owner << OWNER_SHIFT) | ((ids & (MOL - 1)) << ROW_BITS) | slot
    code = jnp.where(column <= iso_ref[...][None, :], code, -1)
    for k in range(Q // 128):
        codes[me, COLS * k : COLS * (k + 1), :] = code[:, 128 * k : 128 * (k + 1)]
    codes[me, Q * COLS // 128 : CODE_ROWS, :] = jnp.full((CODE_ROWS - Q * COLS // 128, 128), -1, I32)
    loads[0].wait()
    gat[chip, :, pl.ds(pl.multiple_of(core * Q, 128), Q)] = spv[...].T
    pl.semaphore_wait(barrier, NLIB - 1 + ndp - 1)

    def ids_copy(j):
        return pltpu.make_async_remote_copy(
            src_ref=codes.at[me],
            dst_ref=codes.at[me],
            send_sem=ids_send.at[j],
            recv_sem=ids_recv.at[me],
            device_id={"lib": peer(j)},
            device_id_type=MESH,
        )

    def ids_from(j):
        s = peer(j)
        return pltpu.make_async_remote_copy(
            src_ref=codes.at[s],
            dst_ref=codes.at[s],
            send_sem=ids_send.at[j],
            recv_sem=ids_recv.at[s],
            device_id={"lib": s},
            device_id_type=MESH,
        )

    lax.fori_loop(1, NLIB, lambda j, c: (ids_copy(j).start(), c)[1], 0)

    def piece(ch, cr, lo, n):
        return gat.at[ch, pl.ds(lo, n), pl.ds(pl.multiple_of(cr * Q, 128), Q)]

    HALF = D // 2
    right = {"lib": chip_at(0, 1) * 2 + core}
    left = {"lib": chip_at(0, 3) * 2 + core}
    across = {"lib": chip_at(1, 0) * 2 + core}
    sibling = {"lib": chip * 2 + 1 - core}

    def ag(idx, dy, dx, lo, n, to):
        ref = piece(chip_at(dy, dx), core, lo, n)
        return pltpu.make_async_remote_copy(
            src_ref=ref, dst_ref=ref, send_sem=ag_send.at[idx], recv_sem=ag_recv.at[idx],
            device_id=to, device_id_type=MESH,
        )

    ag_out = [
        ag(0, 0, 0, 0, D, right),
        ag(1, 0, 0, 0, D, left),
        ag(2, 0, 0, 0, D, across),
        ag(3, 0, 3, 0, HALF, right),
        ag(4, 0, 1, HALF, HALF, left),
        ag(5, 1, 0, 0, D, right),
        ag(6, 1, 0, 0, D, left),
        ag(7, 0, 2, 0, HALF, across),
        ag(8, 0, 2, HALF, HALF, across),
    ]
    arriving = [
        (0, 3, 0, D),
        (0, 1, 0, D),
        (1, 0, 0, D),
        (0, 2, 0, HALF),
        (0, 2, HALF, HALF),
        (1, 3, 0, D),
        (1, 1, 0, D),
        (1, 2, 0, HALF),
        (1, 2, HALF, HALF),
    ]
    ag_in = [ag(k, dy, dx, lo, n, right) for k, (dy, dx, lo, n) in enumerate(arriving)]

    def sb(idx, dy, dx, lo, n, cr):
        ref = piece(chip_at(dy, dx), cr, lo, n)
        return pltpu.make_async_remote_copy(
            src_ref=ref, dst_ref=ref, send_sem=sb_send.at[idx], recv_sem=sb_recv.at[idx],
            device_id=sibling, device_id_type=MESH,
        )

    sb_list = arriving + [(0, 0, 0, D)]
    sb_out = [sb(k, dy, dx, lo, n, core) for k, (dy, dx, lo, n) in enumerate(sb_list)]
    sb_in = [sb(k, dy, dx, lo, n, 1 - core) for k, (dy, dx, lo, n) in enumerate(sb_list)]

    for k in (0, 1, 2):
        ag_out[k].start()
    sb_out[9].start()
    for load in loads[1:]:
        load.wait()
    wt[...] = wv[...].T
    bankt[...] = bankv[...].T
    sb_in[9].wait_recv()

    def compaction():
        lax.fori_loop(1, NLIB, lambda j, c: (ids_from(j).wait_recv(), c)[1], 0)
        n = NLIB * CODE_ROWS
        code = codes[...].reshape(n, 128)
        mine = (code >> OWNER_SHIFT) == me
        ones = onehot(mine)
        before = onehot(iota((128, 128), 0) < iota((128, 128), 1))
        inside = dot(ones, before)
        totals = dot(ones, jnp.ones((128, 128), BF16)).astype(BF16)
        ri, ci = iota((n, n), 0), iota((n, n), 1)
        ahead = onehot((ri // CODE_ROWS == ci // CODE_ROWS) & (ci < ri))
        pos = inside + dot(ahead, totals)
        low = (code & (2**OWNER_SHIFT - 1)) + 1
        posr[...] = jnp.where(mine, pos, -1.0).reshape(NLIB, CODE_ROWS, 128)
        valr[...] = jnp.where(mine, low.astype(F32), 0.0).reshape(NLIB, CODE_ROWS, 128)

        def one(i, carry):
            place = iota((CAP, 128), 0).astype(F32)
            both = []
            for c in (0, 1):
                s = 2 * i + c
                p_all, v_all = posr[s], valr[s]
                total = jnp.zeros((CAP, 128), F32)
                for j in range(Q * COLS // 128):
                    total += jnp.where(p_all[j : j + 1] == place, v_all[j : j + 1], 0.0)
                both.append(jnp.sum(total, axis=1, keepdims=True))
            packed = jnp.concatenate(both, axis=0)
            scol[i, :, 0:1] = packed
            pkt[0:1, pl.ds(pl.multiple_of(i * PAIR, 128), PAIR)] = to_row(packed)
            return carry

        lax.fori_loop(0, NCHIP, one, 0, unroll=4)
        molt[...] = molv[...].T

        def fetch(b, carry):
            lanes = pl.ds(pl.multiple_of(b * 768, 128), 768)
            row = (pkt[0:1, lanes].astype(I32) - 1) >> ROW_BITS
            pick = onehot(row == iota((MOL, 768), 0))
            mrow[:, lanes] = dot(molt[...], pick).astype(BF16)
            return carry

        lax.fori_loop(0, 2, fetch, 0)
        for k in (0, 1, 2):
            ag_in[k].wait_recv()
        for k in (3, 4, 5, 6):
            ag_out[k].start()
        for k in (0, 1, 2):
            sb_out[k].start()
        lax.fori_loop(2, NSLOTS // 768, fetch, 0)

    def bank_unit(ch, kept=None):
        u = dot(wt[...], gat[ch])
        rn = lax.rsqrt(jnp.sum(u * u, axis=0, keepdims=True) + 1e-6)
        u = u * rn
        unit[ch] = u
        qrow[ch, 0:1, :] = rn
        s = dot(bankv[...], u.astype(BF16))
        m = jnp.max(s, axis=0, keepdims=True)
        e = jnp.exp2((s - m) * (INV_T * LOG2E))
        qrow[ch, 1:2, :] = m * INV_T
        qrow[ch, 2:3, :] = jnp.sum(e, axis=0, keepdims=True)
        if kept is None:
            acc[ch] = dot(bankt[...], e.astype(BF16))
        else:
            dub[kept, :] = e.astype(BF16)

    def st_copy(lo, n, j):
        ref = stats.at[me, pl.ds(lo, n)]
        return pltpu.make_async_remote_copy(
            src_ref=ref, dst_ref=ref,
            send_sem=st_send.at[j], recv_sem=st_recv.at[me],
            device_id={"lib": peer(j)}, device_id_type=MESH,
        )

    def st_all(j, s):
        return pltpu.make_async_remote_copy(
            src_ref=stats.at[s], dst_ref=stats.at[s],
            send_sem=st_send.at[j], recv_sem=st_recv.at[s],
            device_id={"lib": peer(j)}, device_id_type=MESH,
        )

    def pair_lanes(i):
        return pl.ds(pl.multiple_of(i * PAIR, 128), PAIR)

    def slot_rows(i):
        t = pkt[0:1, pair_lanes(i)].astype(I32) - 1
        second = jnp.where(iota((1, PAIR), 1) >= CAP, Q, 0)
        q = jnp.where(t < 0, -1, ((t & SLOT_MASK) >> 2) + second)
        return t >= 0, (t >= 0) & ((t & 3) == 0), onehot(q == iota((2 * Q, PAIR), 0))

    def cand_unit(t_order, i):
        lanes = pair_lanes(i)
        _, first, pick = slot_rows(i)
        q_slot = dot(unit[i].astype(BF16), pick)
        qs[:, lanes] = q_slot.astype(BF16)
        cs = jnp.sum(q_slot * mrow[:, lanes].astype(F32), axis=0, keepdims=True) * INV_T
        pkt[1:2, lanes] = cs
        part = jnp.sum(jnp.where(first, cs, 0.0), axis=1, keepdims=True)
        cs_col = to_col(cs)
        for c in (0, 1):
            t = scol[i, c * CAP : (c + 1) * CAP, 0:1].astype(I32) - 1
            q = (t & SLOT_MASK) >> 2
            chosen = jnp.where(q == iota((CAP, Q), 1), cs_col[c * CAP : (c + 1) * CAP], -1e30)
            mb = qrow[i, 1:2, c * Q : (c + 1) * Q]
            lb = qrow[i, 2:3, c * Q : (c + 1) * Q]
            top = jnp.maximum(mb, jnp.max(chosen, axis=0, keepdims=True))
            total = lb * jnp.exp(mb - top) + jnp.sum(jnp.exp(chosen - top), axis=0, keepdims=True)
            out = top + jnp.log(total)
            for k in range(3):
                stats[me, t_order, 3 * c + k : 3 * c + k + 1, :] = out[:, 128 * k : 128 * (k + 1)]
        stats[me, t_order, 6:8, :] = jnp.broadcast_to(part, (2, 128))

    def send_stats(lo, n):
        lax.fori_loop(1, NLIB, lambda j, k: (st_copy(lo, n, j).start(), k)[1], 0)

    def order(t):
        dy = jnp.where((t == 3) | (t >= 5), 1, 0)
        dx = jnp.where(
            (t == 1) | (t == 5), 1, jnp.where((t == 2) | (t == 6), 3, jnp.where((t == 4) | (t == 7), 2, 0))
        )
        return chip_at(dy, dx)

    bank_unit(chip)
    compaction()

    def step(keep, t, carry):
        @pl.when(t == 1)
        def _():
            for k in (1, 0, 2):
                sb_in[k].wait_recv()

        @pl.when(t == 3)
        def _():
            for k in (3, 4):
                ag_in[k].wait_recv()
            for k in (7, 8):
                ag_out[k].start()
            for k in (3, 4):
                sb_out[k].start()

        @pl.when(t == 4)
        def _():
            for k in (3, 4):
                sb_in[k].wait_recv()
            for k in (5, 6):
                ag_in[k].wait_recv()
            for k in (5, 6):
                sb_out[k].start()

        @pl.when(t == 5)
        def _():
            for k in (5, 6):
                sb_in[k].wait_recv()

        @pl.when(t == 6)
        def _():
            for k in (7, 8):
                ag_in[k].wait_recv()
            for k in (7, 8):
                sb_out[k].start()

        @pl.when(t == 7)
        def _():
            for k in (7, 8):
                sb_in[k].wait_recv()

        cand_unit(t - 1, order(t - 1))
        bank_unit(order(t), kept_rows(t) if keep else None)
        return carry

    def kept_rows(t):
        return pl.ds(pl.multiple_of((t - 4) * BANK, BANK), BANK)

    lax.fori_loop(1, 4, functools.partial(step, False), 0)
    lax.fori_loop(4, 5, functools.partial(step, True), 0)
    send_stats(0, 4)
    lax.fori_loop(5, NCHIP, functools.partial(step, True), 0)
    send_stats(4, 3)
    cand_unit(NCHIP - 1, chip_at(1, 2))
    send_stats(NCHIP - 1, 1)

    def kept_sum(t, carry):
        acc[order(t)] = dot(bankt[...], dub[kept_rows(t), :])
        return carry

    lax.fori_loop(4, NCHIP, kept_sum, 0)

    lax.fori_loop(1, NLIB, lambda j, k: (st_all(j, peer(j)).wait_recv(), k)[1], 0)

    place = {(0, 0): 0, (0, 1): 1, (0, 3): 2, (1, 0): 3, (0, 2): 4, (1, 1): 5, (1, 3): 6, (1, 2): 7}
    values, firsts = [], []
    for i in range(NCHIP):
        parts = []
        for s in range(NLIB):
            dy, dx = (i // 4 + s // 8) % 2, (i % 4 - s // 2 % 4) % 4
            parts.append(stats[s, place[dy, dx]])
        top = parts[0]
        for part in parts[1:]:
            top = jnp.maximum(top, part)
        total = jnp.exp(parts[0] - top)
        first_score = parts[0]
        for part in parts[1:]:
            total += jnp.exp(part - top)
            first_score += part
        one_value = top + jnp.log(total)
        lse[i] = one_value
        values.append(one_value)
        firsts.append(first_score)
    value = jnp.stack(values)
    first_scores = jnp.stack(firsts)
    in_row = iota((NCHIP, 8, 128), 1)
    lane0 = iota((NCHIP, 8, 128), 2) == 0
    terms = jnp.where(in_row < 6, value, jnp.where((in_row == 6) & lane0, -first_scores, 0.0))
    terms = jnp.sum(terms, axis=0)
    group_loss = jnp.sum(jnp.sum(terms, axis=1, keepdims=True), axis=0, keepdims=True)
    dlb[dp] = jnp.broadcast_to(group_loss, (8, 128))

    def dl_copy(j, s, to):
        return pltpu.make_async_remote_copy(
            src_ref=dlb.at[s], dst_ref=dlb.at[s], send_sem=dl_send.at[j], recv_sem=dl_recv.at[s],
            device_id={"dp": to}, device_id_type=MESH,
        )


    def grad_unit(i, carry):
        lanes = pair_lanes(i)
        lse_row = jnp.concatenate([lse[i, k : k + 1, :] for k in range(6)], axis=1)
        valid, first, pick = slot_rows(i)
        high = lse_row.astype(BF16).astype(F32)
        middle = (lse_row - high).astype(BF16).astype(F32)
        low = lse_row - high - middle
        thirds = jnp.concatenate([high, middle, low, jnp.zeros((5, 2 * Q), F32)], axis=0)
        thirds = dot(thirds.astype(BF16), pick)
        lse_slot = thirds[0:1] + thirds[1:2] + thirds[2:3]
        coef = jnp.where(
            valid, jnp.exp(pkt[1:2, lanes] - lse_slot) - jnp.where(first, 1.0, 0.0), 0.0
        )
        pkt[2:3, lanes] = coef * INV_T
        weighted = (mrow[:, lanes].astype(F32) * coef).astype(BF16)
        scale = jnp.exp(qrow[i, 1:2, :] - lse_row)
        dq = acc[i] * scale + dot_nt(weighted, pick)
        u = unit[i]
        along = jnp.sum(u * dq, axis=0, keepdims=True)
        du = (dq - u * along) * (qrow[i, 0:1, :] * INV_T)
        dub[pl.ds(pl.multiple_of(i * D, D), D), :] = du.astype(BF16)
        return carry

    lax.fori_loop(0, NCHIP, grad_unit, 0, unroll=2)

    def rs_copy(h, j, src, dst, to):
        return pltpu.make_async_remote_copy(
            src_ref=gwb.at[h, src], dst_ref=rsb.at[h, dst],
            send_sem=rs_send.at[h, j], recv_sem=rs_recv.at[h, dst],
            device_id={"lib": to}, device_id_type=MESH,
        )

    def dp_copy(h, j, s, to):
        return pltpu.make_async_remote_copy(
            src_ref=dpb.at[h, s], dst_ref=dpb.at[h, s],
            send_sem=dp_send.at[h, j], recv_sem=dp_recv.at[h, s],
            device_id={"dp": to}, device_id_type=MESH,
        )

    def gg_copy(h, j, s, to):
        return pltpu.make_async_remote_copy(
            src_ref=ggb.at[h, s], dst_ref=ggb.at[h, s],
            send_sem=gg_send.at[h, j], recv_sem=gg_recv.at[h, s],
            device_id={"lib": to}, device_id_type=MESH,
        )

    def rs_begin(h):
        rows = slice(h * (D // 2), (h + 1) * (D // 2))
        half = dot_nt(gat[0, rows, :], dub[0:D, :])
        for i in range(1, NCHIP):
            half += dot_nt(gat[i, rows, :], dub[i * D : (i + 1) * D, :])
        gwb[h] = half.astype(BF16).reshape(NLIB, PIECE, D)
        lax.fori_loop(1, NLIB, lambda j, k: (rs_copy(h, j, peer(j), me, peer(j)).start(), k)[1], 0)
        rsb[h, me] = gwb[h, me]

    def dp_begin(h):
        lax.fori_loop(1, NLIB, lambda j, k: (rs_copy(h, j, me, peer(j), peer(j)).wait_recv(), k)[1], 0)
        part = rsb[h, 0].astype(F32)
        for s in range(1, NLIB):
            part += rsb[h, s].astype(F32)
        dpb[h, dp] = part.astype(BF16)
        lax.fori_loop(1, ndp, lambda j, k: (dp_copy(h, j, dp, dpeer(j)).start(), k)[1], 0)

    def gg_begin(h):
        lax.fori_loop(1, ndp, lambda j, k: (dp_copy(h, j, dpeer(j), dpeer(j)).wait_recv(), k)[1], 0)
        part = dpb[h, 0].astype(F32)
        for s in range(1, ndp):
            part += dpb[h, s].astype(F32)
        ggb[h, me] = part.astype(BF16)
        lax.fori_loop(1, NLIB, lambda j, k: (gg_copy(h, j, me, peer(j)).start(), k)[1], 0)

    def gg_end(h):
        lax.fori_loop(1, NLIB, lambda j, k: (gg_copy(h, j, peer(j), peer(j)).wait_recv(), k)[1], 0)

    rs_begin(0)
    rs_begin(1)
    lax.fori_loop(1, ndp, lambda j, k: (dl_copy(j, dp, dpeer(j)).start(), k)[1], 0)

    def out_copy(r):
        return pltpu.make_async_copy(
            acc.at[r, pl.ds(0, 256), pl.ds(0, D)],
            gm_out.at[pl.ds(pl.multiple_of(r * 256, 256), 256), :],
            out_sem.at[r],
        )

    def scatter(r, carry):
        row = (pkt[0:1, :].astype(I32) - 1) >> ROW_BITS
        pick = onehot(row == iota((256, NSLOTS), 0) + r * 256)
        acc[r, 0:256, 0:D] = dot_nt(pick, qs[...])
        out_copy(r).start()
        return carry

    def slot_gradients(i, carry):
        lanes = pair_lanes(i)
        qs[:, lanes] = (qs[:, lanes].astype(F32) * pkt[2:3, lanes]).astype(BF16)
        return carry

    lax.fori_loop(0, NCHIP, slot_gradients, 0)
    lax.fori_loop(0, 2, scatter, 0)
    dp_begin(0)
    lax.fori_loop(2, 4, scatter, 0)
    dp_begin(1)
    lax.fori_loop(4, 6, scatter, 0)
    gg_begin(0)
    lax.fori_loop(6, 8, scatter, 0)
    gg_begin(1)

    lax.fori_loop(1, ndp, lambda j, k: (dl_copy(j, dpeer(j), dpeer(j)).wait_recv(), k)[1], 0)
    whole = jnp.zeros((8, 128), F32)
    for s in range(ndp):
        whole += dlb[s]
    loss_out[...] = whole[0:1, 0:1] * (1.0 / (Q * NLIB * ndp))

    gg_end(0)
    gg_end(1)
    gw_out[...] = ggb[...].reshape(D, D)

    lax.fori_loop(1, NLIB, lambda j, k: (st_all(j, me).wait_send(), k)[1], 0)
    lax.fori_loop(0, 8, lambda r, k: (out_copy(r).wait(), k)[1], 0)
    lax.fori_loop(1, NLIB, lambda j, k: (ids_copy(j).wait_send(), k)[1], 0)
    for k in range(9):
        ag_out[k].wait_send()
    for k in range(10):
        sb_out[k].wait_send()
    for h in (0, 1):
        lax.fori_loop(1, NLIB, lambda j, k: (rs_copy(h, j, peer(j), me, peer(j)).wait_send(), k)[1], 0)
        lax.fori_loop(1, NLIB, lambda j, k: (gg_copy(h, j, me, peer(j)).wait_send(), k)[1], 0)
        lax.fori_loop(1, ndp, lambda j, k: (dp_copy(h, j, dp, dpeer(j)).wait_send(), k)[1], 0)
    lax.fori_loop(1, ndp, lambda j, k: (dl_copy(j, dp, dpeer(j)).wait_send(), k)[1], 0)


def per_device(ndp, spectra, w_proj, fixed_library_matrix, mol_rows, cand_ids, iso_count):
    vmem = pl.BlockSpec(memory_space=pltpu.VMEM)
    hbm = pl.BlockSpec(memory_space=pl.ANY)
    dma = pltpu.SemaphoreType.DMA
    gw, gm, loss = pl.pallas_call(
        functools.partial(kernel, ndp),
        out_shape=(
            jax.ShapeDtypeStruct((D, D), BF16),
            jax.ShapeDtypeStruct((MOL, D), F32),
            jax.ShapeDtypeStruct((1, 1), F32),
        ),
        in_specs=[hbm, hbm, hbm, hbm, vmem, vmem],
        out_specs=(vmem, hbm, vmem),
        scratch_shapes=[
            pltpu.VMEM((Q, D), BF16),
            pltpu.VMEM((NCHIP, D, 2 * Q), BF16),
            pltpu.VMEM((D, D), BF16),
            pltpu.VMEM((D, D), BF16),
            pltpu.VMEM((BANK, D), BF16),
            pltpu.VMEM((D, BANK), BF16),
            pltpu.VMEM((MOL, D), BF16),
            pltpu.VMEM((D, MOL), BF16),
            pltpu.VMEM((NLIB, CODE_ROWS, 128), I32),
            pltpu.VMEM((NLIB, CODE_ROWS, 128), F32),
            pltpu.VMEM((NLIB, CODE_ROWS, 128), F32),
            pltpu.VMEM((8, NSLOTS), F32),
            pltpu.VMEM((D, NSLOTS), BF16),
            pltpu.VMEM((D, NSLOTS), BF16),
            pltpu.VMEM((NCHIP, D, 2 * Q), F32),
            pltpu.VMEM((NCHIP, D, 2 * Q), F32),
            pltpu.VMEM((NCHIP, 8, 2 * Q), F32),
            pltpu.VMEM((NCHIP, PAIR, 128), F32),
            pltpu.VMEM((NLIB, NCHIP, 8, 128), F32),
            pltpu.VMEM((NCHIP, 8, 128), F32),
            pltpu.VMEM((NCHIP * D, 2 * Q), BF16),
            pltpu.VMEM((2, NLIB, PIECE, D), BF16),
            pltpu.VMEM((2, NLIB, PIECE, D), BF16),
            pltpu.VMEM((2, ndp, PIECE, D), BF16),
            pltpu.VMEM((ndp, 8, 128), F32),
            pltpu.VMEM((2, NLIB, PIECE, D), BF16),
            dma((4,)),
            dma((NLIB,)),
            dma((NLIB,)),
            dma((9,)),
            dma((9,)),
            dma((10,)),
            dma((10,)),
            dma((NLIB,)),
            dma((NLIB,)),
            dma((2, NLIB)),
            dma((2, NLIB)),
            dma((2, ndp)),
            dma((2, ndp)),
            dma((ndp,)),
            dma((ndp,)),
            dma((2, NLIB)),
            dma((2, NLIB)),
            dma((8,)),
        ],
        compiler_params=pltpu.CompilerParams(
            collective_id=0, has_side_effects=True, vmem_limit_bytes=62 * 1024 * 1024
        ),
    )(spectra, w_proj, fixed_library_matrix, mol_rows, cand_ids.T, iso_count)
    return gw.astype(F32), gm, loss.reshape(())


def solution(mesh):
    placed = (
        P(("dp", "lib"), None),
        P(),
        P("lib", None),
        P(("dp", "lib"), None),
        P(("dp", "lib"), None),
        P(("dp", "lib")),
    )
    return jax.shard_map(
        functools.partial(per_device, mesh.shape["dp"]),
        mesh=mesh,
        in_specs=placed,
        out_specs=(P(), P(("dp", "lib"), None), P()),
        check_vma=False,
    )
```

```python
import functools

import jax
import jax.numpy as jnp
from jax import lax
from jax.experimental import pallas as pl
from jax.experimental.pallas import tpu as pltpu
from jax.sharding import PartitionSpec as P

F32 = jnp.float32
BF16 = jnp.bfloat16
I32 = jnp.int32
MESH = pl.DeviceIdType.MESH

D = 512
Q = 384
COLS = 4
NLIB = 16
NCHIP = 8
CAP = 192
BANK = 1024
MOL = 2048
CODE_ROWS = 16
ROW_BITS = 11
SLOT_MASK = 2047
OWNER_SHIFT = 22
INV_T = 1.0 / 0.07
PIECE = D // 2 // NLIB
LOG2E = 1.4426950408889634
NSLOTS = NLIB * CAP
PAIR = 2 * CAP


def iota(shape, dim):
    return lax.broadcasted_iota(I32, shape, dim)


def to_row(v):
    eye = iota((128, 128), 0) == iota((128, 128), 1)
    return jnp.concatenate(
        [
            jnp.sum(jnp.where(eye, v[lo : lo + 128], 0.0), axis=0, keepdims=True)
            for lo in range(0, v.shape[0], 128)
        ],
        axis=1,
    )


def to_col(v):
    eye = iota((128, 128), 0) == iota((128, 128), 1)
    return jnp.concatenate(
        [
            jnp.sum(jnp.where(eye, v[:, lo : lo + 128], 0.0), axis=1, keepdims=True)
            for lo in range(0, v.shape[1], 128)
        ],
        axis=0,
    )


def onehot(mask):
    return jnp.where(mask, 1.0, 0.0).astype(BF16)


def dot(a, b):
    return jnp.dot(a, b, preferred_element_type=F32)


def dot_nt(a, b):
    return lax.dot_general(a, b, (((1,), (1,)), ((), ())), preferred_element_type=F32)


def kernel(
    ndp,
    spec_hbm,
    w_hbm,
    bank_hbm,
    mol_hbm,
    ids_ref,
    iso_ref,
    gw_out,
    gm_out,
    loss_out,
    spv,
    gat,
    wv,
    wt,
    bankv,
    bankt,
    molv,
    molt,
    codes,
    posr,
    valr,
    pkt,
    mrow,
    qs,
    unit,
    acc,
    qrow,
    scol,
    stats,
    lse,
    dub,
    gwb,
    rsb,
    dpb,
    dlb,
    ggb,
    loc_sem,
    ids_send,
    ids_recv,
    ag_send,
    ag_recv,
    sb_send,
    sb_recv,
    st_send,
    st_recv,
    rs_send,
    rs_recv,
    dp_send,
    dp_recv,
    dl_send,
    dl_recv,
    gg_send,
    gg_recv,
    out_sem,
):
    dp = lax.axis_index("dp")
    me = lax.axis_index("lib")
    core = lax.rem(me, 2)
    chip = me // 2
    y = chip // 4
    x = lax.rem(chip, 4)

    def chip_at(dy, dx):
        return lax.rem(y + dy, 2) * 4 + lax.rem(x + dx, 4)

    def peer(j):
        return lax.rem(me + j, NLIB)

    def dpeer(j):
        return lax.rem(dp + j, ndp)

    loads = [
        pltpu.make_async_copy(spec_hbm, spv, loc_sem.at[0]),
        pltpu.make_async_copy(w_hbm, wv, loc_sem.at[1]),
        pltpu.make_async_copy(bank_hbm, bankv, loc_sem.at[2]),
        pltpu.make_async_copy(mol_hbm, molv, loc_sem.at[3]),
    ]
    for load in loads:
        load.start()

    barrier = pltpu.get_barrier_semaphore()

    def greet(j, carry):
        pl.semaphore_signal(barrier, inc=1, device_id={"lib": peer(j)}, device_id_type=MESH)
        return carry

    lax.fori_loop(1, NLIB, greet, 0)

    def greet_dp(j, carry):
        pl.semaphore_signal(barrier, inc=1, device_id={"dp": dpeer(j)}, device_id_type=MESH)
        return carry

    lax.fori_loop(1, ndp, greet_dp, 0)
    ids = ids_ref[...]
    column = iota((COLS, Q), 0)
    slot = iota((COLS, Q), 1) * COLS + column
    owner = (ids >> ROW_BITS) & (NLIB - 1)
    code = (owner << OWNER_SHIFT) | ((ids & (MOL - 1)) << ROW_BITS) | slot
    code = jnp.where(column <= iso_ref[...][None, :], code, -1)
    for k in range(Q // 128):
        codes[me, COLS * k : COLS * (k + 1), :] = code[:, 128 * k : 128 * (k + 1)]
    codes[me, Q * COLS // 128 : CODE_ROWS, :] = jnp.full((CODE_ROWS - Q * COLS // 128, 128), -1, I32)
    loads[0].wait()
    gat[chip, :, pl.ds(pl.multiple_of(core * Q, 128), Q)] = spv[...].T
    pl.semaphore_wait(barrier, NLIB - 1 + ndp - 1)

    def ids_copy(j):
        return pltpu.make_async_remote_copy(
            src_ref=codes.at[me],
            dst_ref=codes.at[me],
            send_sem=ids_send.at[j],
            recv_sem=ids_recv.at[me],
            device_id={"lib": peer(j)},
            device_id_type=MESH,
        )

    def ids_from(j):
        s = peer(j)
        return pltpu.make_async_remote_copy(
            src_ref=codes.at[s],
            dst_ref=codes.at[s],
            send_sem=ids_send.at[j],
            recv_sem=ids_recv.at[s],
            device_id={"lib": s},
            device_id_type=MESH,
        )

    lax.fori_loop(1, NLIB, lambda j, c: (ids_copy(j).start(), c)[1], 0)

    def piece(ch, cr, lo, n):
        return gat.at[ch, pl.ds(lo, n), pl.ds(pl.multiple_of(cr * Q, 128), Q)]

    HALF = D // 2
    right = {"lib": chip_at(0, 1) * 2 + core}
    left = {"lib": chip_at(0, 3) * 2 + core}
    across = {"lib": chip_at(1, 0) * 2 + core}
    sibling = {"lib": chip * 2 + 1 - core}

    def ag(idx, dy, dx, lo, n, to):
        ref = piece(chip_at(dy, dx), core, lo, n)
        return pltpu.make_async_remote_copy(
            src_ref=ref, dst_ref=ref, send_sem=ag_send.at[idx], recv_sem=ag_recv.at[idx],
            device_id=to, device_id_type=MESH,
        )

    ag_out = [
        ag(0, 0, 0, 0, D, right),
        ag(1, 0, 0, 0, D, left),
        ag(2, 0, 0, 0, D, across),
        ag(3, 0, 3, 0, HALF, right),
        ag(4, 0, 1, HALF, HALF, left),
        ag(5, 1, 0, 0, D, right),
        ag(6, 1, 0, 0, D, left),
        ag(7, 0, 2, 0, HALF, across),
        ag(8, 0, 2, HALF, HALF, across),
    ]
    arriving = [
        (0, 3, 0, D),
        (0, 1, 0, D),
        (1, 0, 0, D),
        (0, 2, 0, HALF),
        (0, 2, HALF, HALF),
        (1, 3, 0, D),
        (1, 1, 0, D),
        (1, 2, 0, HALF),
        (1, 2, HALF, HALF),
    ]
    ag_in = [ag(k, dy, dx, lo, n, right) for k, (dy, dx, lo, n) in enumerate(arriving)]

    def sb(idx, dy, dx, lo, n, cr):
        ref = piece(chip_at(dy, dx), cr, lo, n)
        return pltpu.make_async_remote_copy(
            src_ref=ref, dst_ref=ref, send_sem=sb_send.at[idx], recv_sem=sb_recv.at[idx],
            device_id=sibling, device_id_type=MESH,
        )

    sb_list = arriving + [(0, 0, 0, D)]
    sb_out = [sb(k, dy, dx, lo, n, core) for k, (dy, dx, lo, n) in enumerate(sb_list)]
    sb_in = [sb(k, dy, dx, lo, n, 1 - core) for k, (dy, dx, lo, n) in enumerate(sb_list)]

    for k in (0, 1, 2):
        ag_out[k].start()
    sb_out[9].start()
    for load in loads[1:]:
        load.wait()
    wt[...] = wv[...].T
    bankt[...] = bankv[...].T
    sb_in[9].wait_recv()

    def compaction():
        lax.fori_loop(1, NLIB, lambda j, c: (ids_from(j).wait_recv(), c)[1], 0)
        n = NLIB * CODE_ROWS
        code = codes[...].reshape(n, 128)
        mine = (code >> OWNER_SHIFT) == me
        ones = onehot(mine)
        before = onehot(iota((128, 128), 0) < iota((128, 128), 1))
        inside = dot(ones, before)
        totals = dot(ones, jnp.ones((128, 128), BF16)).astype(BF16)
        ri, ci = iota((n, n), 0), iota((n, n), 1)
        ahead = onehot((ri // CODE_ROWS == ci // CODE_ROWS) & (ci < ri))
        pos = inside + dot(ahead, totals)
        low = (code & (2**OWNER_SHIFT - 1)) + 1
        posr[...] = jnp.where(mine, pos, -1.0).reshape(NLIB, CODE_ROWS, 128)
        valr[...] = jnp.where(mine, low.astype(F32), 0.0).reshape(NLIB, CODE_ROWS, 128)

        def one(i, carry):
            place = iota((CAP, 128), 0).astype(F32)
            both = []
            for c in (0, 1):
                s = 2 * i + c
                p_all, v_all = posr[s], valr[s]
                total = jnp.zeros((CAP, 128), F32)
                for j in range(Q * COLS // 128):
                    total += jnp.where(p_all[j : j + 1] == place, v_all[j : j + 1], 0.0)
                both.append(jnp.sum(total, axis=1, keepdims=True))
            packed = jnp.concatenate(both, axis=0)
            scol[i, :, 0:1] = packed
            pkt[0:1, pl.ds(pl.multiple_of(i * PAIR, 128), PAIR)] = to_row(packed)
            return carry

        lax.fori_loop(0, NCHIP, one, 0, unroll=4)
        molt[...] = molv[...].T

        def fetch(b, carry):
            lanes = pl.ds(pl.multiple_of(b * 768, 128), 768)
            row = (pkt[0:1, lanes].astype(I32) - 1) >> ROW_BITS
            pick = onehot(row == iota((MOL, 768), 0))
            mrow[:, lanes] = dot(molt[...], pick).astype(BF16)
            return carry

        lax.fori_loop(0, 2, fetch, 0, unroll=2)
        for k in (0, 1, 2):
            ag_in[k].wait_recv()
        for k in (3, 4, 5, 6):
            ag_out[k].start()
        for k in (0, 1, 2):
            sb_out[k].start()
        lax.fori_loop(2, NSLOTS // 768, fetch, 0, unroll=2)

    def bank_unit(ch, kept=None):
        u = dot(wt[...], gat[ch])
        rn = lax.rsqrt(jnp.sum(u * u, axis=0, keepdims=True) + 1e-6)
        u = u * rn
        unit[ch] = u
        qrow[ch, 0:1, :] = rn
        s = dot(bankv[...], u.astype(BF16))
        m = jnp.max(s, axis=0, keepdims=True)
        e = jnp.exp2((s - m) * (INV_T * LOG2E))
        qrow[ch, 1:2, :] = m * INV_T
        qrow[ch, 2:3, :] = jnp.sum(e, axis=0, keepdims=True)
        if kept is None:
            acc[ch] = dot(bankt[...], e.astype(BF16))
        else:
            dub[kept, :] = e.astype(BF16)

    def st_copy(lo, n, j):
        ref = stats.at[me, pl.ds(lo, n)]
        return pltpu.make_async_remote_copy(
            src_ref=ref, dst_ref=ref,
            send_sem=st_send.at[j], recv_sem=st_recv.at[me],
            device_id={"lib": peer(j)}, device_id_type=MESH,
        )

    def st_all(j, s):
        return pltpu.make_async_remote_copy(
            src_ref=stats.at[s], dst_ref=stats.at[s],
            send_sem=st_send.at[j], recv_sem=st_recv.at[s],
            device_id={"lib": peer(j)}, device_id_type=MESH,
        )

    def pair_lanes(i):
        return pl.ds(pl.multiple_of(i * PAIR, 128), PAIR)

    def slot_rows(i):
        t = pkt[0:1, pair_lanes(i)].astype(I32) - 1
        second = jnp.where(iota((1, PAIR), 1) >= CAP, Q, 0)
        q = jnp.where(t < 0, -1, ((t & SLOT_MASK) >> 2) + second)
        return t >= 0, (t >= 0) & ((t & 3) == 0), onehot(q == iota((2 * Q, PAIR), 0))

    def cand_unit(t_order, i):
        lanes = pair_lanes(i)
        _, first, pick = slot_rows(i)
        q_slot = dot(unit[i].astype(BF16), pick)
        qs[:, lanes] = q_slot.astype(BF16)
        cs = jnp.sum(q_slot * mrow[:, lanes].astype(F32), axis=0, keepdims=True) * INV_T
        pkt[1:2, lanes] = cs
        part = jnp.sum(jnp.where(first, cs, 0.0), axis=1, keepdims=True)
        cs_col = to_col(cs)
        for c in (0, 1):
            t = scol[i, c * CAP : (c + 1) * CAP, 0:1].astype(I32) - 1
            q = (t & SLOT_MASK) >> 2
            chosen = jnp.where(q == iota((CAP, Q), 1), cs_col[c * CAP : (c + 1) * CAP], -1e30)
            mb = qrow[i, 1:2, c * Q : (c + 1) * Q]
            lb = qrow[i, 2:3, c * Q : (c + 1) * Q]
            top = jnp.maximum(mb, jnp.max(chosen, axis=0, keepdims=True))
            total = lb * jnp.exp(mb - top) + jnp.sum(jnp.exp(chosen - top), axis=0, keepdims=True)
            out = top + jnp.log(total)
            for k in range(3):
                stats[me, t_order, 3 * c + k : 3 * c + k + 1, :] = out[:, 128 * k : 128 * (k + 1)]
        stats[me, t_order, 6:8, :] = jnp.broadcast_to(part, (2, 128))

    def send_stats(lo, n):
        lax.fori_loop(1, NLIB, lambda j, k: (st_copy(lo, n, j).start(), k)[1], 0)

    def order(t):
        dy = jnp.where((t == 3) | (t >= 5), 1, 0)
        dx = jnp.where(
            (t == 1) | (t == 5), 1, jnp.where((t == 2) | (t == 6), 3, jnp.where((t == 4) | (t == 7), 2, 0))
        )
        return chip_at(dy, dx)

    bank_unit(chip)
    compaction()

    def step(keep, t, carry):
        @pl.when(t == 1)
        def _():
            for k in (1, 0, 2):
                sb_in[k].wait_recv()

        @pl.when(t == 3)
        def _():
            for k in (3, 4):
                ag_in[k].wait_recv()
            for k in (7, 8):
                ag_out[k].start()
            for k in (3, 4):
                sb_out[k].start()

        @pl.when(t == 4)
        def _():
            for k in (3, 4):
                sb_in[k].wait_recv()
            for k in (5, 6):
                ag_in[k].wait_recv()
            for k in (5, 6):
                sb_out[k].start()

        @pl.when(t == 5)
        def _():
            for k in (5, 6):
                sb_in[k].wait_recv()

        @pl.when(t == 6)
        def _():
            for k in (7, 8):
                ag_in[k].wait_recv()
            for k in (7, 8):
                sb_out[k].start()

        @pl.when(t == 7)
        def _():
            for k in (7, 8):
                sb_in[k].wait_recv()

        cand_unit(t - 1, order(t - 1))
        bank_unit(order(t), kept_rows(t) if keep else None)
        return carry

    def kept_rows(t):
        return pl.ds(pl.multiple_of((t - 4) * BANK, BANK), BANK)

    lax.fori_loop(1, 4, functools.partial(step, False), 0)
    lax.fori_loop(4, 5, functools.partial(step, True), 0)
    send_stats(0, 4)
    lax.fori_loop(5, NCHIP, functools.partial(step, True), 0)
    send_stats(4, 3)
    cand_unit(NCHIP - 1, chip_at(1, 2))
    send_stats(NCHIP - 1, 1)

    def kept_sum(t, carry):
        acc[order(t)] = dot(bankt[...], dub[kept_rows(t), :])
        return carry

    lax.fori_loop(4, NCHIP, kept_sum, 0, unroll=2)

    lax.fori_loop(1, NLIB, lambda j, k: (st_all(j, peer(j)).wait_recv(), k)[1], 0)

    place = {(0, 0): 0, (0, 1): 1, (0, 3): 2, (1, 0): 3, (0, 2): 4, (1, 1): 5, (1, 3): 6, (1, 2): 7}
    values, firsts = [], []
    for i in range(NCHIP):
        parts = []
        for s in range(NLIB):
            dy, dx = (i // 4 + s // 8) % 2, (i % 4 - s // 2 % 4) % 4
            parts.append(stats[s, place[dy, dx]])
        top = parts[0]
        for part in parts[1:]:
            top = jnp.maximum(top, part)
        total = jnp.exp(parts[0] - top)
        first_score = parts[0]
        for part in parts[1:]:
            total += jnp.exp(part - top)
            first_score += part
        one_value = top + jnp.log(total)
        lse[i] = one_value
        values.append(one_value)
        firsts.append(first_score)
    value = jnp.stack(values)
    first_scores = jnp.stack(firsts)
    in_row = iota((NCHIP, 8, 128), 1)
    lane0 = iota((NCHIP, 8, 128), 2) == 0
    terms = jnp.where(in_row < 6, value, jnp.where((in_row == 6) & lane0, -first_scores, 0.0))
    terms = jnp.sum(terms, axis=0)
    group_loss = jnp.sum(jnp.sum(terms, axis=1, keepdims=True), axis=0, keepdims=True)
    dlb[dp] = jnp.broadcast_to(group_loss, (8, 128))

    def dl_copy(j, s, to):
        return pltpu.make_async_remote_copy(
            src_ref=dlb.at[s], dst_ref=dlb.at[s], send_sem=dl_send.at[j], recv_sem=dl_recv.at[s],
            device_id={"dp": to}, device_id_type=MESH,
        )


    def grad_unit(i, carry):
        lanes = pair_lanes(i)
        lse_row = jnp.concatenate([lse[i, k : k + 1, :] for k in range(6)], axis=1)
        valid, first, pick = slot_rows(i)
        high = lse_row.astype(BF16).astype(F32)
        middle = (lse_row - high).astype(BF16).astype(F32)
        low = lse_row - high - middle
        thirds = jnp.concatenate([high, middle, low, jnp.zeros((5, 2 * Q), F32)], axis=0)
        thirds = dot(thirds.astype(BF16), pick)
        lse_slot = thirds[0:1] + thirds[1:2] + thirds[2:3]
        coef = jnp.where(
            valid, jnp.exp(pkt[1:2, lanes] - lse_slot) - jnp.where(first, 1.0, 0.0), 0.0
        )
        pkt[2:3, lanes] = coef * INV_T
        weighted = (mrow[:, lanes].astype(F32) * coef).astype(BF16)
        scale = jnp.exp(qrow[i, 1:2, :] - lse_row)
        dq = acc[i] * scale + dot_nt(weighted, pick)
        u = unit[i]
        along = jnp.sum(u * dq, axis=0, keepdims=True)
        du = (dq - u * along) * (qrow[i, 0:1, :] * INV_T)
        dub[pl.ds(pl.multiple_of(i * D, D), D), :] = du.astype(BF16)
        return carry

    lax.fori_loop(0, NCHIP, grad_unit, 0, unroll=2)

    def rs_copy(h, j, src, dst, to):
        return pltpu.make_async_remote_copy(
            src_ref=gwb.at[h, src], dst_ref=rsb.at[h, dst],
            send_sem=rs_send.at[h, j], recv_sem=rs_recv.at[h, dst],
            device_id={"lib": to}, device_id_type=MESH,
        )

    def dp_copy(h, j, s, to):
        return pltpu.make_async_remote_copy(
            src_ref=dpb.at[h, s], dst_ref=dpb.at[h, s],
            send_sem=dp_send.at[h, j], recv_sem=dp_recv.at[h, s],
            device_id={"dp": to}, device_id_type=MESH,
        )

    def gg_copy(h, j, s, to):
        return pltpu.make_async_remote_copy(
            src_ref=ggb.at[h, s], dst_ref=ggb.at[h, s],
            send_sem=gg_send.at[h, j], recv_sem=gg_recv.at[h, s],
            device_id={"lib": to}, device_id_type=MESH,
        )

    def rs_begin(h):
        rows = slice(h * (D // 2), (h + 1) * (D // 2))
        half = dot_nt(gat[0, rows, :], dub[0:D, :])
        for i in range(1, NCHIP):
            half += dot_nt(gat[i, rows, :], dub[i * D : (i + 1) * D, :])
        gwb[h] = half.astype(BF16).reshape(NLIB, PIECE, D)
        lax.fori_loop(1, NLIB, lambda j, k: (rs_copy(h, j, peer(j), me, peer(j)).start(), k)[1], 0)
        rsb[h, me] = gwb[h, me]

    def dp_begin(h):
        lax.fori_loop(1, NLIB, lambda j, k: (rs_copy(h, j, me, peer(j), peer(j)).wait_recv(), k)[1], 0)
        part = rsb[h, 0].astype(F32)
        for s in range(1, NLIB):
            part += rsb[h, s].astype(F32)
        dpb[h, dp] = part.astype(BF16)
        lax.fori_loop(1, ndp, lambda j, k: (dp_copy(h, j, dp, dpeer(j)).start(), k)[1], 0)

    def gg_begin(h):
        lax.fori_loop(1, ndp, lambda j, k: (dp_copy(h, j, dpeer(j), dpeer(j)).wait_recv(), k)[1], 0)
        part = dpb[h, 0].astype(F32)
        for s in range(1, ndp):
            part += dpb[h, s].astype(F32)
        ggb[h, me] = part.astype(BF16)
        lax.fori_loop(1, NLIB, lambda j, k: (gg_copy(h, j, me, peer(j)).start(), k)[1], 0)

    def gg_end(h):
        lax.fori_loop(1, NLIB, lambda j, k: (gg_copy(h, j, peer(j), peer(j)).wait_recv(), k)[1], 0)

    rs_begin(0)
    rs_begin(1)
    lax.fori_loop(1, ndp, lambda j, k: (dl_copy(j, dp, dpeer(j)).start(), k)[1], 0)

    def out_copy(r):
        return pltpu.make_async_copy(
            acc.at[r, pl.ds(0, 256), pl.ds(0, D)],
            gm_out.at[pl.ds(pl.multiple_of(r * 256, 256), 256), :],
            out_sem.at[r],
        )

    def scatter(r, carry):
        row = (pkt[0:1, :].astype(I32) - 1) >> ROW_BITS
        pick = onehot(row == iota((256, NSLOTS), 0) + r * 256)
        acc[r, 0:256, 0:D] = dot_nt(pick, qs[...])
        out_copy(r).start()
        return carry

    def slot_gradients(i, carry):
        lanes = pair_lanes(i)
        qs[:, lanes] = (qs[:, lanes].astype(F32) * pkt[2:3, lanes]).astype(BF16)
        return carry

    lax.fori_loop(0, NCHIP, slot_gradients, 0)
    lax.fori_loop(0, 2, scatter, 0, unroll=2)
    dp_begin(0)
    lax.fori_loop(2, 4, scatter, 0, unroll=2)
    dp_begin(1)
    lax.fori_loop(4, 6, scatter, 0, unroll=2)
    gg_begin(0)
    lax.fori_loop(6, 8, scatter, 0, unroll=2)
    gg_begin(1)

    lax.fori_loop(1, ndp, lambda j, k: (dl_copy(j, dpeer(j), dpeer(j)).wait_recv(), k)[1], 0)
    whole = jnp.zeros((8, 128), F32)
    for s in range(ndp):
        whole += dlb[s]
    loss_out[...] = whole[0:1, 0:1] * (1.0 / (Q * NLIB * ndp))

    gg_end(0)
    gg_end(1)
    gw_out[...] = ggb[...].reshape(D, D)

    lax.fori_loop(1, NLIB, lambda j, k: (st_all(j, me).wait_send(), k)[1], 0)
    lax.fori_loop(0, 8, lambda r, k: (out_copy(r).wait(), k)[1], 0)
    lax.fori_loop(1, NLIB, lambda j, k: (ids_copy(j).wait_send(), k)[1], 0)
    for k in range(9):
        ag_out[k].wait_send()
    for k in range(10):
        sb_out[k].wait_send()
    for h in (0, 1):
        lax.fori_loop(1, NLIB, lambda j, k: (rs_copy(h, j, peer(j), me, peer(j)).wait_send(), k)[1], 0)
        lax.fori_loop(1, NLIB, lambda j, k: (gg_copy(h, j, me, peer(j)).wait_send(), k)[1], 0)
        lax.fori_loop(1, ndp, lambda j, k: (dp_copy(h, j, dp, dpeer(j)).wait_send(), k)[1], 0)
    lax.fori_loop(1, ndp, lambda j, k: (dl_copy(j, dp, dpeer(j)).wait_send(), k)[1], 0)


def per_device(ndp, spectra, w_proj, fixed_library_matrix, mol_rows, cand_ids, iso_count):
    vmem = pl.BlockSpec(memory_space=pltpu.VMEM)
    hbm = pl.BlockSpec(memory_space=pl.ANY)
    dma = pltpu.SemaphoreType.DMA
    gw, gm, loss = pl.pallas_call(
        functools.partial(kernel, ndp),
        out_shape=(
            jax.ShapeDtypeStruct((D, D), BF16),
            jax.ShapeDtypeStruct((MOL, D), F32),
            jax.ShapeDtypeStruct((1, 1), F32),
        ),
        in_specs=[hbm, hbm, hbm, hbm, vmem, vmem],
        out_specs=(vmem, hbm, vmem),
        scratch_shapes=[
            pltpu.VMEM((Q, D), BF16),
            pltpu.VMEM((NCHIP, D, 2 * Q), BF16),
            pltpu.VMEM((D, D), BF16),
            pltpu.VMEM((D, D), BF16),
            pltpu.VMEM((BANK, D), BF16),
            pltpu.VMEM((D, BANK), BF16),
            pltpu.VMEM((MOL, D), BF16),
            pltpu.VMEM((D, MOL), BF16),
            pltpu.VMEM((NLIB, CODE_ROWS, 128), I32),
            pltpu.VMEM((NLIB, CODE_ROWS, 128), F32),
            pltpu.VMEM((NLIB, CODE_ROWS, 128), F32),
            pltpu.VMEM((8, NSLOTS), F32),
            pltpu.VMEM((D, NSLOTS), BF16),
            pltpu.VMEM((D, NSLOTS), BF16),
            pltpu.VMEM((NCHIP, D, 2 * Q), F32),
            pltpu.VMEM((NCHIP, D, 2 * Q), F32),
            pltpu.VMEM((NCHIP, 8, 2 * Q), F32),
            pltpu.VMEM((NCHIP, PAIR, 128), F32),
            pltpu.VMEM((NLIB, NCHIP, 8, 128), F32),
            pltpu.VMEM((NCHIP, 8, 128), F32),
            pltpu.VMEM((NCHIP * D, 2 * Q), BF16),
            pltpu.VMEM((2, NLIB, PIECE, D), BF16),
            pltpu.VMEM((2, NLIB, PIECE, D), BF16),
            pltpu.VMEM((2, ndp, PIECE, D), BF16),
            pltpu.VMEM((ndp, 8, 128), F32),
            pltpu.VMEM((2, NLIB, PIECE, D), BF16),
            dma((4,)),
            dma((NLIB,)),
            dma((NLIB,)),
            dma((9,)),
            dma((9,)),
            dma((10,)),
            dma((10,)),
            dma((NLIB,)),
            dma((NLIB,)),
            dma((2, NLIB)),
            dma((2, NLIB)),
            dma((2, ndp)),
            dma((2, ndp)),
            dma((ndp,)),
            dma((ndp,)),
            dma((2, NLIB)),
            dma((2, NLIB)),
            dma((8,)),
        ],
        compiler_params=pltpu.CompilerParams(
            collective_id=0, has_side_effects=True, vmem_limit_bytes=62 * 1024 * 1024
        ),
    )(spectra, w_proj, fixed_library_matrix, mol_rows, cand_ids.T, iso_count)
    return gw.astype(F32), gm, loss.reshape(())


def solution(mesh):
    placed = (
        P(("dp", "lib"), None),
        P(),
        P("lib", None),
        P(("dp", "lib"), None),
        P(("dp", "lib"), None),
        P(("dp", "lib")),
    )
    return jax.shard_map(
        functools.partial(per_device, mesh.shape["dp"]),
        mesh=mesh,
        in_specs=placed,
        out_specs=(P(), P(("dp", "lib"), None), P()),
        check_vma=False,
    )
```
